128 devices in a mesh: seq: 32 (over x, y, core), sub: 4 (over z).
Axes of the slice: x: 4, y: 4, z: 4, core: 2. Of those that a mesh axis runs over, the one named last changes fastest.
Arguments:
- queries: bfloat16 [32768, 512], P(('seq', 'sub')), may hold values from -128 to 128
- keys: bfloat16 [32768, 128], P(('seq', 'sub')), may hold values from -8 to 8
- values: bfloat16 [32768, 128], P(('seq', 'sub')), may hold values from -6 to 6
- dout: bfloat16 [32768, 512], P(('seq', 'sub')), may hold values from -6 to 6
- doc_lengths: int32 [32], replicated, may hold values from 1 to 8192, 32768 in all
Outputs:
- attended: bfloat16 [32768, 512], P(('seq', 'sub'))
- query_grad: bfloat16 [32768, 512], P(('seq', 'sub'))
- key_grad: bfloat16 [32768, 128], P(('seq', 'sub'))
- value_grad: bfloat16 [32768, 128], P(('seq', 'sub'))
The draws below stay inside these ranges and needn't reach their ends.
Inputs may be any that keep to these rules, and one draw needn't show every extreme that they name: `doc_lengths`: each document has 1 to 8192 tokens, one exactly 8192, and together they fill the batch.
All inputs are finite; a program needn't handle non-finite values.
Results may differ from the reference program's by a relative error of at most 0.04.
Values may be sent and summed in bfloat16 or wider, within the bound.
No kernel may reach another device: no remote copies, remote signals or barrier semaphores. Data moves between devices by JAX's collectives and lax.ppermute only.
A program may use at most 64 MiB of HBM per device.

```python
import math
import jax
import jax.numpy as jnp
import numpy as np
from jax import lax

HD = 128
HEADS = 4
TOK_DEV = 256
KEY_BLOCK = 512
SPAN = 8
TOKENS = 32768
DOC_MOST = 8192
NDOCS = 32
N_SEQ = 32
N_SUB = 4


def shared_keys(key):
    base = jax.random.truncated_normal(jax.random.fold_in(key, 101), -6.0, 6.0, (TOKENS, HD), jnp.float32)
    positions = lax.broadcasted_iota(jnp.int32, (TOKENS, 1), 0)
    chosen = positions % 97 == 49
    return jnp.where(chosen, base, base)


def draw_keys(key, part):
    result = shared_keys(key)
    return result.astype(jnp.bfloat16)


def draw_queries(key, part):
    key = jax.random.fold_in(key, 5)
    return jax.random.truncated_normal(key, -6.0, 6.0, (TOKENS, HEADS * HD), jnp.float32).astype(jnp.bfloat16)


def steps_of(own_key, extent, split, least, largest):
    def one(dim, blocks):
        steps = jax.random.uniform(jax.random.fold_in(jax.random.fold_in(own_key, 6), dim), (blocks,), jnp.float32, least / len(split), largest / len(split))
        return jnp.repeat(jnp.exp(steps), extent[dim] // blocks).reshape((-1,) + (1,) * (len(extent) - dim - 1))

    factor_of = one(*split[0])
    for cut in split[1:]:
        factor_of = factor_of * one(*cut)
    return factor_of


def profile(number_of, total, bound, lean):
    portions = [(1 << 20) // math.isqrt(standing ** lean) + 1 for standing in range(2, number_of + 1)]
    rest, holding = total - bound - (number_of - 1), [1] * (number_of - 1)
    while rest > 0:
        candidates = [i for i in range(number_of - 1) if holding[i] < bound]
        whole, left = sum([portions[i] for i in candidates]), rest
        for i in candidates:
            extra = min(bound - holding[i], max(1, left * portions[i] // whole), rest)
            holding[i] = holding[i] + extra
            rest = rest - extra
    return np.array([bound] + holding)


def uneven_parts(stream_key, number_of, total, bound, skew):
    if number_of == 2:
        one = jax.random.randint(stream_key, (), max(1, total - bound), min(bound, total - 1) + 1)
        return jnp.stack([one, total - one])
    sizes = jnp.asarray(profile(number_of, total, bound, skew), jnp.int32)
    pairs = (number_of - 1) // 2
    giver, sink = sizes[1:1 + 2 * pairs:2], sizes[2:2 + 2 * pairs:2]
    room = jnp.minimum(giver - 1, bound - sink)
    passed = jax.random.randint(jax.random.fold_in(stream_key, 1), (pairs,), 0, 1 << 20) % (room + 1)
    sizes = sizes.at[1:1 + 2 * pairs:2].set(giver - passed).at[2:2 + 2 * pairs:2].set(sink + passed)
    return sizes[jax.random.permutation(jax.random.fold_in(stream_key, 2), number_of)]


def bell_draw(rng, shape, spread, limit, pieces=(), held_as=jnp.bfloat16):
    array = spread * jax.random.normal(rng, shape, jnp.float32)
    if pieces:
        array = array * steps_of(rng, shape, pieces, -0.22, 0.18)
    return jnp.clip(array, -limit, limit).astype(held_as)


def setup_inputs(seed: int = 0) -> dict:
    key_of = jax.random.split(jax.random.key(seed), 6)
    return {
        "queries": draw_queries(jax.random.fold_in(key_of[5], 71), 0),
        "keys": draw_keys(jax.random.fold_in(key_of[5], 71), 0),
        "values": bell_draw(key_of[2], (TOKENS, HD), 1.0, 6.0, ((0, 128),)),
        "dout": bell_draw(key_of[3], (TOKENS, HEADS * HD), 1.0, 6.0, ((0, 128),)),
        "doc_lengths": uneven_parts(key_of[4], NDOCS, TOKENS, DOC_MOST, 2).astype(jnp.int32),
    }


big_negative = -1e+30

def document_of(positions, ends):
    return lax.optimization_barrier(jnp.sum((positions[:, None] >= ends[None, :]).astype(jnp.int32), axis=1))

def reference(queries, keys, values, dout, doc_lengths):
    group_rows = TOK_DEV * N_SUB
    width = (SPAN + 1) * group_rows
    margin = SPAN * group_rows
    nblocks = width // KEY_BLOCK
    scale = 1.0 / math.sqrt(HD)
    ends = jnp.cumsum(doc_lengths).astype(jnp.int32)
    padded_keys = jnp.concatenate([jnp.zeros((margin, HD), jnp.bfloat16), keys], axis=0)
    padded_values = jnp.concatenate([jnp.zeros((margin, HD), jnp.bfloat16), values], axis=0)

    def one_group(carry, group):
        key_acc, value_acc = carry
        start = (group * group_rows).astype(jnp.int32)
        query_heads = lax.dynamic_slice_in_dim(queries, start, group_rows, 0).reshape(group_rows, HEADS, HD).astype(jnp.float32)
        dout_heads = lax.dynamic_slice_in_dim(dout, start, group_rows, 0).reshape(group_rows, HEADS, HD).astype(jnp.float32)
        key_block = lax.dynamic_slice_in_dim(padded_keys, start, width, 0).astype(jnp.float32)
        value_block = lax.dynamic_slice_in_dim(padded_values, start, width, 0).astype(jnp.float32)
        query_pos = start + jnp.arange(group_rows, dtype=jnp.int32)
        key_pos = start - margin + jnp.arange(width, dtype=jnp.int32)
        query_doc = document_of(query_pos, ends)
        key_doc = document_of(key_pos, ends)
        mask = (query_doc[:, None] == key_doc[None, :]) & (key_pos[None, :] <= query_pos[:, None]) & (key_pos[None, :] >= 0)
        raw = jnp.einsum('qhd,kd->hqk', query_heads, key_block) * scale
        found = jnp.where(mask[None], raw, big_negative)
        found_blocks = jnp.moveaxis(found.reshape(HEADS, group_rows, nblocks, KEY_BLOCK), 2, 0)
        value_parts = value_block.reshape(nblocks, KEY_BLOCK, HD)

        def forward_block(state, block):
            top, total, accum = state
            scores_block, value_piece = block
            new_top = jnp.maximum(top, lax.optimization_barrier(jnp.max(scores_block, axis=2)))
            factor = jnp.exp(top - new_top)
            part = jnp.exp(scores_block - new_top[:, :, None])
            new_total = total * factor + lax.optimization_barrier(jnp.sum(part, axis=2))
            part_weights = lax.optimization_barrier(part.astype(jnp.bfloat16)).astype(jnp.float32)
            new_accum = accum * factor[:, :, None] + jnp.einsum('hqk,kd->hqd', part_weights, value_piece)
            return ((new_top, new_total, new_accum), None)
        start_state = (jnp.full((HEADS, group_rows), big_negative, jnp.float32), jnp.zeros((HEADS, group_rows), jnp.float32), jnp.zeros((HEADS, group_rows, HD), jnp.float32))
        (top, total, accum), _ = lax.scan(forward_block, start_state, (found_blocks, value_parts))
        attended = lax.optimization_barrier(jnp.transpose(accum / total[:, :, None], (1, 0, 2)).astype(jnp.bfloat16))
        chance = jnp.exp(found - top[:, :, None]) / total[:, :, None]
        weights = lax.optimization_barrier(chance.astype(jnp.bfloat16)).astype(jnp.float32)
        delta = lax.optimization_barrier(jnp.sum(dout_heads * attended.astype(jnp.float32), axis=2)).T
        pushed = jnp.einsum('qhd,kd->hqk', dout_heads, value_block)
        slope = lax.optimization_barrier((chance * (pushed - delta[:, :, None])).astype(jnp.bfloat16)).astype(jnp.float32)
        query_grad = (jnp.einsum('hqk,kd->qhd', slope, key_block) * scale).astype(jnp.bfloat16)
        key_part = jnp.einsum('hqk,qhd->kd', slope, query_heads) * scale
        value_part = jnp.einsum('hqk,qhd->kd', weights, dout_heads)
        key_acc = lax.dynamic_update_slice_in_dim(key_acc, lax.dynamic_slice_in_dim(key_acc, start, width, 0) + key_part, start, 0)
        value_acc = lax.dynamic_update_slice_in_dim(value_acc, lax.dynamic_slice_in_dim(value_acc, start, width, 0) + value_part, start, 0)
        return ((key_acc, value_acc), (attended.reshape(group_rows, HEADS * HD), query_grad.reshape(group_rows, HEADS * HD)))
    empty = jnp.zeros((margin + TOKENS, HD), jnp.float32)
    (key_acc, value_acc), (outputs, query_grads) = lax.scan(one_group, (empty, empty), jnp.arange(N_SEQ, dtype=jnp.int32))
    return (outputs.reshape(TOKENS, HEADS * HD), query_grads.reshape(TOKENS, HEADS * HD), key_acc[margin:].astype(jnp.bfloat16), value_acc[margin:].astype(jnp.bfloat16))
```

```python
import functools
import math

import jax
import jax.numpy as jnp
from jax import lax
from jax.experimental import pallas as pl
from jax.experimental.pallas import tpu as pltpu
from jax.sharding import PartitionSpec as P

BIG_NEG = -1e30
LOG2E = 1.4426950408889634
PART = 5


def nt(a, b):
    return lax.dot_general(a, b, (((1,), (1,)), ((), ())), preferred_element_type=jnp.float32)


def nn(a, b):
    return lax.dot_general(a, b, (((1,), (0,)), ((), ())), preferred_element_type=jnp.float32)


def doc_start(len_ref, pos):
    def step(d, carry):
        begin, found = carry
        return (begin + len_ref[d], jnp.where(begin <= pos, begin, found))

    return lax.fori_loop(0, len_ref.shape[0], step, (jnp.int32(0), jnp.zeros_like(pos)))[1]


def chunk_start(info_ref, share, j, blk, subs):
    chip, core = info_ref[0], info_ref[1]
    sub = info_ref[2 + share]
    other = jnp.where(j >= PART, 1, 0)
    owner = jnp.where(other == 1, 1 - core, core)
    jj = j - other * PART
    back = jnp.where(jj < 2, 2 + 2 * owner, jnp.where(jj < 4, 1 + 2 * owner, 0))
    parity = jnp.where(lax.rem(jj, 2) == 0, owner, 1 - owner)
    group = 2 * (chip - back) + parity
    return (group * subs + sub) * blk


def query_start(info_ref, r, blk, subs):
    chip, core = info_ref[0], info_ref[1]
    sub = jnp.where(r == 0, info_ref[2], info_ref[4])
    return ((2 * chip + core) * subs + sub) * blk


def prepare(info_ref, len_ref, start_ref, bound_ref, blk, subs):
    for r in range(2):
        q0 = query_start(info_ref, r, blk, subs)
        start_ref[r] = doc_start(len_ref, q0 + lax.broadcasted_iota(jnp.int32, (1, blk), 1))
        bound_ref[2 * r] = doc_start(len_ref, q0)
        bound_ref[2 * r + 1] = doc_start(len_ref, q0 + blk - 1)


def on_tile(info_ref, bound_ref, start_ref, r, kstart, blk, subs, body):
    q0 = query_start(info_ref, r, blk, subs)
    first, last = bound_ref[2 * r], bound_ref[2 * r + 1]
    active = (kstart + blk - 1 >= first) & (kstart <= q0 + blk - 1)
    whole = (kstart >= last) & (kstart + blk - 1 <= q0)

    @pl.when(active & whole)
    def _():
        body(None)

    @pl.when(active & jnp.logical_not(whole))
    def _():
        kpos = kstart + lax.broadcasted_iota(jnp.int32, (blk, blk), 0)
        qpos = q0 + lax.broadcasted_iota(jnp.int32, (blk, blk), 1)
        body((kpos <= qpos) & (kpos >= start_ref[r]))


def fill(window_ref, part_refs, blk):
    for a, part in enumerate(part_refs):
        for kind in range(2):
            for j in range(PART):
                window_ref[kind, a * PART + j] = part[kind, j * blk:(j + 1) * blk, :]


def forward_kernel(heads, hd, subs, share, info_ref, len_ref, q0_ref, q1_ref, ka_ref, kb_ref, *rest):
    blk = q0_ref.shape[0]
    scale = LOG2E / math.sqrt(hd)
    if share == 0:
        m_ref, l_ref, a_ref, q_ref, window_ref, start_ref, bound_ref = rest
        m_ref[...] = jnp.full(m_ref.shape, BIG_NEG, jnp.float32)
        l_ref[...] = jnp.zeros(l_ref.shape, jnp.float32)
        a_ref[...] = jnp.zeros(a_ref.shape, jnp.float32)
    else:
        m_in, l_in, a_in, d0_ref, d1_ref, stat_ref, mine_ref, theirs_ref = rest[:8]
        q_ref, window_ref, start_ref, bound_ref, m_ref, l_ref, a_ref = rest[8:]
        m_ref[...] = m_in[...]
        l_ref[...] = l_in[...]
        a_ref[...] = a_in[...]
    prepare(info_ref, len_ref, start_ref, bound_ref, blk, subs)
    fill(window_ref, (ka_ref, kb_ref), blk)
    q_ref[0] = q0_ref[...]
    q_ref[1] = q1_ref[...]

    def tile(t, _):
        j, r = t // 2, lax.rem(t, 2)

        def body(mask):
            kb = window_ref[0, j]
            vt = window_ref[1, j].T
            for h in range(heads):
                s = nt(kb, q_ref[r, :, h * hd:(h + 1) * hd]) * scale
                if mask is not None:
                    s = jnp.where(mask, s, BIG_NEG)
                x = r * heads + h
                m_old = m_ref[x]
                m_new = jnp.maximum(m_old, jnp.max(s, axis=0, keepdims=True))
                p = jnp.exp2(s - m_new)
                f = jnp.exp2(m_old - m_new)
                l_ref[x] = l_ref[x] * f + jnp.sum(p, axis=0, keepdims=True)
                a_ref[x] = a_ref[x] * f + nn(vt, p.astype(jnp.bfloat16))
                m_ref[x] = m_new

        on_tile(info_ref, bound_ref, start_ref, r, chunk_start(info_ref, share, j, blk, subs), blk, subs, body)
        return 0

    lax.fori_loop(0, 2 * PART * 2, tile, 0)
    if share == 1:
        for r, d_ref in enumerate((d0_ref, d1_ref)):
            for h in range(heads):
                x = r * heads + h
                dt = d_ref[:, h * hd:(h + 1) * hd].astype(jnp.float32).T
                stat_ref[x, 0:1] = m_ref[x]
                stat_ref[x, 1:2] = l_ref[x]
                stat_ref[x, 2:3] = jnp.sum(dt * a_ref[x], axis=0, keepdims=True)
        mine_ref[...] = a_ref[:heads]
        theirs_ref[...] = a_ref[heads:].astype(jnp.bfloat16)


def vm():
    return pl.BlockSpec(memory_space=pltpu.VMEM)


def sm():
    return pl.BlockSpec(memory_space=pltpu.SMEM)


def params():
    return pltpu.CompilerParams(vmem_limit_bytes=40 << 20)


def forward(info, lens, q0, q1, part_a, part_b, subs, share, state=(), douts=()):
    blk, width = q0.shape
    hd = part_a.shape[2]
    heads = width // hd
    n = 2 * heads
    f32 = jnp.float32
    row = jax.ShapeDtypeStruct((n, 1, blk), f32)
    work = [pltpu.VMEM((2, blk, width), q0.dtype), pltpu.VMEM((2, 2 * PART, blk, hd), part_a.dtype),
            pltpu.VMEM((2, 1, blk), jnp.int32), pltpu.SMEM((4,), jnp.int32)]
    if share == 0:
        shapes = (row, row, jax.ShapeDtypeStruct((n, hd, blk), f32))
    else:
        shapes = (jax.ShapeDtypeStruct((n, 3, blk), f32), jax.ShapeDtypeStruct((heads, hd, blk), f32),
                  jax.ShapeDtypeStruct((heads, hd, blk), jnp.bfloat16))
        work += [pltpu.VMEM((n, 1, blk), f32), pltpu.VMEM((n, 1, blk), f32), pltpu.VMEM((n, hd, blk), f32)]
    args = (info, lens, q0, q1, part_a, part_b) + tuple(state) + tuple(douts)
    return pl.pallas_call(
        functools.partial(forward_kernel, heads, hd, subs, share),
        out_shape=shapes,
        in_specs=[sm(), sm()] + [vm()] * (len(args) - 2),
        out_specs=(vm(),) * 3,
        scratch_shapes=work,
        compiler_params=params(),
        cost_estimate=pl.CostEstimate(flops=8 * PART * n * blk * blk * hd, bytes_accessed=4 << 20, transcendentals=0),
        name="forward_part",
    )(*args)


def merge_stats(s_mine, s_theirs):
    m = jnp.maximum(s_mine[0:1], s_theirs[0:1])
    fa = jnp.exp2(s_mine[0:1] - m)
    fb = jnp.exp2(s_theirs[0:1] - m)
    total = s_mine[1:2] * fa + s_theirs[1:2] * fb
    delta = (s_mine[2:3] * fa + s_theirs[2:3] * fb) / total
    return m + jnp.log2(total), fa / total, fb / total, delta


def backward_kernel(heads, hd, subs, share, info_ref, len_ref, q0_ref, q1_ref, d0_ref, d1_ref, ka_ref, kb_ref,
                    sa_ref, sb_ref, *rest):
    blk = q0_ref.shape[0]
    scale = LOG2E / math.sqrt(hd)
    back = 1.0 / math.sqrt(hd)
    if share == 1:
        ga_ref, gb_ref, dq_ref = rest[:3]
        work = rest[3:]
        dq_ref[...] = jnp.zeros(dq_ref.shape, jnp.float32)
    else:
        mine_ref, theirs_ref, dq_in, ga_ref, gb_ref, att_ref, dq0_ref, dq1_ref = rest[:8]
        work = rest[8:-1]
        dq_ref = rest[-1]
        dq_ref[...] = dq_in[...]
    q_ref, d_ref, window_ref, grad_ref, start_ref, bound_ref, log_ref, delta_ref, dk_ref, dv_ref = work
    prepare(info_ref, len_ref, start_ref, bound_ref, blk, subs)
    fill(window_ref, (ka_ref, kb_ref), blk)
    q_ref[0] = q0_ref[...]
    q_ref[1] = q1_ref[...]
    d_ref[0] = d0_ref[...]
    d_ref[1] = d1_ref[...]
    for r in range(2):
        for h in range(heads):
            x = r * heads + h
            log_total, wa, wb, delta = merge_stats(sa_ref[x], sb_ref[(1 - r) * heads + h])
            log_ref[x] = log_total
            delta_ref[x] = delta
            if share == 0 and r == 0:
                att = mine_ref[h] * wa + theirs_ref[h].astype(jnp.float32) * wb
                att_ref[:, h * hd:(h + 1) * hd] = att.T.astype(jnp.bfloat16)

    def chunk(j, _):
        kstart = chunk_start(info_ref, share, j, blk, subs)
        dk_ref[...] = jnp.zeros(dk_ref.shape, jnp.float32)
        dv_ref[...] = jnp.zeros(dv_ref.shape, jnp.float32)

        def row(r, _):
            def body(mask):
                kb = window_ref[0, j]
                vb = window_ref[1, j]
                kt = kb.T
                dk = dk_ref[...]
                dv = dv_ref[...]
                for h in range(heads):
                    q = q_ref[r, :, h * hd:(h + 1) * hd]
                    d = d_ref[r, :, h * hd:(h + 1) * hd]
                    x = r * heads + h
                    s = nt(kb, q) * scale
                    if mask is not None:
                        s = jnp.where(mask, s, BIG_NEG)
                    p = jnp.exp2(s - log_ref[x])
                    slope = (p * (nt(vb, d) - delta_ref[x])).astype(jnp.bfloat16)
                    dv = dv + nn(p.astype(jnp.bfloat16), d)
                    dk = dk + nn(slope, q)
                    dq_ref[x] = dq_ref[x] + nn(kt, slope)
                dk_ref[...] = dk
                dv_ref[...] = dv

            on_tile(info_ref, bound_ref, start_ref, r, kstart, blk, subs, body)
            return 0

        lax.fori_loop(0, 2, row, 0)
        grad_ref[0, j] = (dk_ref[...] * back).astype(jnp.bfloat16)
        grad_ref[1, j] = dv_ref[...].astype(jnp.bfloat16)
        return 0

    lax.fori_loop(0, 2 * PART, chunk, 0)
    for a, g_ref in enumerate((ga_ref, gb_ref)):
        for kind in range(2):
            for j in range(PART):
                g_ref[kind, j * blk:(j + 1) * blk, :] = grad_ref[kind, a * PART + j]
    if share == 0:
        for h in range(heads):
            columns = slice(h * hd, (h + 1) * hd)
            dq0_ref[:, columns] = (dq_ref[h] * back).T
            dq1_ref[:, columns] = (dq_ref[heads + h] * back).T.astype(jnp.bfloat16)


def backward(info, lens, q0, q1, d0, d1, part_a, part_b, s_mine, s_theirs, subs, share, sums=()):
    blk, width = q0.shape
    hd = part_a.shape[2]
    heads = width // hd
    n = 2 * heads
    f32 = jnp.float32
    grad = jax.ShapeDtypeStruct(part_a.shape, jnp.bfloat16)
    two = pltpu.VMEM((2, blk, width), q0.dtype)
    window = pltpu.VMEM((2, 2 * PART, blk, hd), part_a.dtype)
    row = pltpu.VMEM((n, 1, blk), f32)
    work = [two, two, window, window, pltpu.VMEM((2, 1, blk), jnp.int32), pltpu.SMEM((4,), jnp.int32),
            row, row, pltpu.VMEM((blk, hd), f32), pltpu.VMEM((blk, hd), f32)]
    if share == 1:
        shapes = (grad, grad, jax.ShapeDtypeStruct((n, hd, blk), f32))
    else:
        out = jax.ShapeDtypeStruct((blk, width), jnp.bfloat16)
        shapes = (grad, grad, out, jax.ShapeDtypeStruct((blk, width), f32), out)
        work += [pltpu.VMEM((n, hd, blk), f32)]
    args = (info, lens, q0, q1, d0, d1, part_a, part_b, s_mine, s_theirs) + tuple(sums)
    return pl.pallas_call(
        functools.partial(backward_kernel, heads, hd, subs, share),
        out_shape=shapes,
        in_specs=[sm(), sm()] + [vm()] * (len(args) - 2),
        out_specs=(vm(),) * len(shapes),
        scratch_shapes=work,
        compiler_params=params(),
        cost_estimate=pl.CostEstimate(flops=20 * PART * n * blk * blk * hd, bytes_accessed=4 << 20, transcendentals=0),
        name="backward_part",
    )(*args)


def per_device(queries, keys, values, dout, doc_lengths):
    blk = queries.shape[0]
    seqs, subs = lax.axis_size("seq"), lax.axis_size("sub")
    seq, sub = lax.axis_index("seq"), lax.axis_index("sub")
    f32, bf16 = jnp.float32, jnp.bfloat16
    chip, core = seq // 2, seq % 2
    mate = sub + 1 - 2 * (sub % 2)
    far = (sub + 2 * (sub % 2) - 1 + subs) % subs
    info = jnp.stack([chip, core, sub, far, mate]).astype(jnp.int32)

    def swap_core(value):
        return lax.ppermute(value, "seq", [(s, s ^ 1) for s in range(seqs)])

    def swap_mate(value):
        return lax.ppermute(value, "sub", [(s, s ^ 1) for s in range(subs)])

    def swap_far(value):
        return lax.ppermute(value, "sub", [(s, (s + 2 * (s % 2) - 1) % subs) for s in range(subs)])

    def route(step, sign):
        pairs = [(s, s + 2 * (1 + step + 2 * (s % 2))) for s in range(seqs)]
        return [(a, b)[::sign] for a, b in pairs if b < seqs]

    own = jnp.stack([keys, values])
    pair = jnp.concatenate([own, swap_core(own)], axis=1)
    q_mate = swap_mate(queries)
    near = lax.ppermute(pair, "seq", route(0, 1))
    away = lax.ppermute(pair, "seq", route(1, 1))
    d_mate = swap_mate(dout)
    part_a = jnp.concatenate([away, near, own], axis=1)
    part_c = swap_far(part_a)
    part_b = swap_core(part_a)
    state = forward(info, doc_lengths, queries, q_mate, part_a, part_b, subs, 0)
    part_d = swap_core(part_c)
    stats, mine, theirs = forward(
        info, doc_lengths, queries, q_mate, part_c, part_d, subs, 1, state, (dout, d_mate)
    )
    stats_mate = swap_mate(stats)
    theirs = swap_mate(theirs)
    common = (info, doc_lengths, queries, q_mate, dout, d_mate)
    grad_c, grad_d, dq = backward(*common, part_c, part_d, stats, stats_mate, subs, 1)
    grad_c = (grad_c.astype(f32) + swap_core(grad_d).astype(f32)).astype(bf16)
    grad_far = swap_far(grad_c)
    grad_a, grad_b, attended, dq_mine, dq_mate = backward(
        *common, part_a, part_b, stats, stats_mate, subs, 0, (mine, theirs, dq)
    )
    dq_back = swap_mate(dq_mate)
    query_grad = (dq_mine + dq_back.astype(f32)).astype(bf16)
    grad = grad_a.astype(f32) + swap_core(grad_b).astype(f32) + grad_far.astype(f32)
    home = grad[:, : 4 * blk].astype(bf16)
    near = lax.ppermute(home[:, 2 * blk :], "seq", route(0, -1)).astype(f32)
    away = lax.ppermute(home[:, : 2 * blk], "seq", route(1, -1)).astype(f32)
    back = near + away
    other = swap_core(back[:, blk:].astype(bf16)).astype(f32)
    total = (grad[:, 4 * blk :] + back[:, :blk] + other).astype(bf16)
    return attended, query_grad, total[0], total[1]


def solution(mesh):
    rows = P(("seq", "sub"), None)
    return jax.shard_map(
        per_device,
        mesh=mesh,
        in_specs=(rows, rows, rows, rows, P()),
        out_specs=(rows, rows, rows, rows),
        check_vma=False,
    )
```

```python
import functools
import math

import jax
import jax.numpy as jnp
from jax import lax
from jax.experimental import pallas as pl
from jax.experimental.pallas import tpu as pltpu
from jax.sharding import PartitionSpec as P

BIG_NEG = -1e30
LOG2E = 1.4426950408889634
PART = 5


def nt(a, b):
    return lax.dot_general(a, b, (((1,), (1,)), ((), ())), preferred_element_type=jnp.float32)


def nn(a, b):
    return lax.dot_general(a, b, (((1,), (0,)), ((), ())), preferred_element_type=jnp.float32)


def doc_start(begins, pos):
    return jnp.max(jnp.where(begins <= pos[..., None], begins, 0), axis=-1)


def tables(doc_lengths, chip, core, sub, mate, far, blk, subs):
    begins = jnp.cumsum(doc_lengths) - doc_lengths
    q0 = ((2 * chip + core) * subs + jnp.stack([sub, mate])) * blk
    starts = doc_start(begins, q0[:, None] + jnp.arange(blk, dtype=jnp.int32))
    j = jnp.arange(2 * PART, dtype=jnp.int32)
    jj = j % PART
    owner = jnp.where(j >= PART, 1 - core, core)
    back = jnp.where(jj < 2, 2 + 2 * owner, jnp.where(jj < 4, 1 + 2 * owner, 0))
    parity = jnp.where(jj % 2 == 0, owner, 1 - owner)
    group = 2 * (chip - back) + parity

    def listed(chosen):
        place = jnp.cumsum(chosen.astype(jnp.int32)) - 1
        n = chosen.shape[0]
        slot = jnp.arange(n, dtype=jnp.int32)[:, None]
        entry = jnp.sum(jnp.where(chosen & (place == slot), jnp.arange(n, dtype=jnp.int32), 0), axis=1)
        return jnp.sum(chosen.astype(jnp.int32))[None], entry

    infos = []
    for share in (sub, far):
        kstart = (group * subs + share) * blk
        kend = kstart + blk - 1
        first, last = starts[:, 0], starts[:, -1]
        active = (kend[:, None] >= first) & (kstart[:, None] <= q0 + blk - 1)
        whole = (kstart[:, None] >= last) & (kend[:, None] <= q0)
        double = jnp.all(whole & active, axis=1)
        single = active & jnp.logical_not(double)[:, None]
        n2, list2 = listed(double)
        n1, list1 = listed(single.reshape(-1))
        infos.append(jnp.concatenate([n2, n1, q0, kstart, list2, list1]).astype(jnp.int32))
    return infos, starts[:, None, :]


def fill(window_ref, part_refs, blk):
    for a, part in enumerate(part_refs):
        for kind in range(2):
            for j in range(PART):
                window_ref[kind, a * PART + j] = part[kind, j * blk:(j + 1) * blk, :]


def fill_heads(dest_ref, sources, heads, hd):
    for r, source in enumerate(sources):
        for h in range(heads):
            dest_ref[r * heads + h] = source[:, h * hd:(h + 1) * hd]


def over_tiles(info_ref, start_ref, blk, heads, body):
    count2, count1 = info_ref[0], info_ref[1]
    list2 = 4 + 2 * PART
    list1 = list2 + 2 * PART

    def double(i, _):
        body(info_ref[list2 + i], list(range(2 * heads)), None)
        return 0

    def single(i, _):
        entry = info_ref[list1 + i]
        j, r = lax.shift_right_logical(entry, 1), lax.bitwise_and(entry, 1)
        kpos = info_ref[4 + j] + lax.broadcasted_iota(jnp.int32, (blk, blk), 0)
        qpos = info_ref[2 + r] + lax.broadcasted_iota(jnp.int32, (blk, blk), 1)
        body(j, [r * heads + h for h in range(heads)], (kpos <= qpos) & (kpos >= start_ref[r]))
        return 0

    lax.fori_loop(0, count2, double, 0)
    lax.fori_loop(0, count1, single, 0)


def forward_kernel(heads, hd, share, info_ref, start_ref, q0_ref, q1_ref, ka_ref, kb_ref, *rest):
    blk = q0_ref.shape[0]
    scale = LOG2E / math.sqrt(hd)
    if share == 0:
        m_ref, l_ref, a_ref, q_ref, window_ref = rest
        m_ref[...] = jnp.full(m_ref.shape, BIG_NEG, jnp.float32)
        l_ref[...] = jnp.zeros(l_ref.shape, jnp.float32)
        a_ref[...] = jnp.zeros(a_ref.shape, jnp.float32)
    else:
        m_in, l_in, a_in, d0_ref, d1_ref, stat_ref, mine_ref, theirs_ref = rest[:8]
        q_ref, window_ref, m_ref, l_ref, a_ref = rest[8:]
        m_ref[...] = m_in[...]
        l_ref[...] = l_in[...]
        a_ref[...] = a_in[...]
    fill(window_ref, (ka_ref, kb_ref), blk)
    fill_heads(q_ref, (q0_ref, q1_ref), heads, hd)

    def tile(j, xs, mask):
        kb = window_ref[0, j]
        vt = window_ref[1, j].T
        old = [(m_ref[x], l_ref[x], a_ref[x]) for x in xs]
        found = [nt(kb, q_ref[x]) * scale for x in xs]
        if mask is not None:
            found = [jnp.where(mask, s, BIG_NEG) for s in found]
        new = []
        for s, (m_old, l_old, a_old) in zip(found, old):
            m_new = jnp.maximum(m_old, jnp.max(s, axis=0, keepdims=True))
            p = jnp.exp2(s - m_new)
            f = jnp.exp2(m_old - m_new)
            total = l_old * f + jnp.sum(p, axis=0, keepdims=True)
            new.append((m_new, total, a_old * f + nn(vt, p.astype(jnp.bfloat16))))
        for x, (m_new, total, acc) in zip(xs, new):
            m_ref[x] = m_new
            l_ref[x] = total
            a_ref[x] = acc

    over_tiles(info_ref, start_ref, blk, heads, tile)
    if share == 1:
        for r, d_ref in enumerate((d0_ref, d1_ref)):
            for h in range(heads):
                x = r * heads + h
                dt = d_ref[:, h * hd:(h + 1) * hd].astype(jnp.float32).T
                stat_ref[x, 0:1] = m_ref[x]
                stat_ref[x, 1:2] = l_ref[x]
                stat_ref[x, 2:3] = jnp.sum(dt * a_ref[x], axis=0, keepdims=True)
        mine_ref[...] = a_ref[:heads]
        theirs_ref[...] = a_ref[heads:].astype(jnp.bfloat16)


def vm():
    return pl.BlockSpec(memory_space=pltpu.VMEM)


def sm():
    return pl.BlockSpec(memory_space=pltpu.SMEM)


def params():
    return pltpu.CompilerParams(vmem_limit_bytes=40 << 20)


def forward(info, starts, q0, q1, part_a, part_b, share, state=(), douts=()):
    blk, width = q0.shape
    hd = part_a.shape[2]
    heads = width // hd
    n = 2 * heads
    f32 = jnp.float32
    row = jax.ShapeDtypeStruct((n, 1, blk), f32)
    work = [pltpu.VMEM((n, blk, hd), q0.dtype), pltpu.VMEM((2, 2 * PART, blk, hd), part_a.dtype)]
    if share == 0:
        shapes = (row, row, jax.ShapeDtypeStruct((n, hd, blk), f32))
    else:
        shapes = (jax.ShapeDtypeStruct((n, 3, blk), f32), jax.ShapeDtypeStruct((heads, hd, blk), f32),
                  jax.ShapeDtypeStruct((heads, hd, blk), jnp.bfloat16))
        work += [pltpu.VMEM((n, 1, blk), f32), pltpu.VMEM((n, 1, blk), f32), pltpu.VMEM((n, hd, blk), f32)]
    args = (info, starts, q0, q1, part_a, part_b) + tuple(state) + tuple(douts)
    return pl.pallas_call(
        functools.partial(forward_kernel, heads, hd, share),
        out_shape=shapes,
        in_specs=[sm()] + [vm()] * (len(args) - 1),
        out_specs=(vm(),) * 3,
        scratch_shapes=work,
        compiler_params=params(),
        cost_estimate=pl.CostEstimate(flops=8 * PART * n * blk * blk * hd, bytes_accessed=4 << 20, transcendentals=0),
        name="forward_part",
    )(*args)


def merge_stats(s_mine, s_theirs):
    m = jnp.maximum(s_mine[0:1], s_theirs[0:1])
    fa = jnp.exp2(s_mine[0:1] - m)
    fb = jnp.exp2(s_theirs[0:1] - m)
    total = s_mine[1:2] * fa + s_theirs[1:2] * fb
    delta = (s_mine[2:3] * fa + s_theirs[2:3] * fb) / total
    return m + jnp.log2(total), fa / total, fb / total, delta


def backward_kernel(heads, hd, share, info_ref, start_ref, q0_ref, q1_ref, d0_ref, d1_ref, ka_ref, kb_ref,
                    sa_ref, sb_ref, *rest):
    blk = q0_ref.shape[0]
    scale = LOG2E / math.sqrt(hd)
    back = 1.0 / math.sqrt(hd)
    if share == 1:
        ga_ref, gb_ref, dq_ref = rest[:3]
        work = rest[3:]
        dq_ref[...] = jnp.zeros(dq_ref.shape, jnp.float32)
    else:
        mine_ref, theirs_ref, dq_in, ga_ref, gb_ref, att_ref, dq0_ref, dq1_ref = rest[:8]
        work = rest[8:-1]
        dq_ref = rest[-1]
        dq_ref[...] = dq_in[...]
    q_ref, d_ref, window_ref, grad_ref, log_ref, delta_ref = work
    grad_ref[...] = jnp.zeros(grad_ref.shape, jnp.float32)
    fill(window_ref, (ka_ref, kb_ref), blk)
    fill_heads(q_ref, (q0_ref, q1_ref), heads, hd)
    fill_heads(d_ref, (d0_ref, d1_ref), heads, hd)
    for r in range(2):
        for h in range(heads):
            x = r * heads + h
            log_total, wa, wb, delta = merge_stats(sa_ref[x], sb_ref[(1 - r) * heads + h])
            log_ref[x] = log_total
            delta_ref[x] = delta
            if share == 0 and r == 0:
                att = mine_ref[h] * wa + theirs_ref[h].astype(jnp.float32) * wb
                att_ref[:, h * hd:(h + 1) * hd] = att.T.astype(jnp.bfloat16)

    def tile(j, xs, mask):
        kb = window_ref[0, j]
        vb = window_ref[1, j]
        kt = kb.T
        qs = [q_ref[x] for x in xs]
        ds = [d_ref[x] for x in xs]
        rows = [(log_ref[x], delta_ref[x]) for x in xs]
        sums = [dq_ref[x] for x in xs]
        dk, dv = grad_ref[0, j], grad_ref[1, j]
        found = [nt(kb, q) for q in qs]
        pushed = [nt(vb, d) for d in ds]
        weights, slopes = [], []
        for s, dp, (log_total, delta) in zip(found, pushed, rows):
            s = s * scale
            if mask is not None:
                s = jnp.where(mask, s, BIG_NEG)
            p = jnp.exp2(s - log_total)
            weights.append(p.astype(jnp.bfloat16))
            slopes.append((p * (dp - delta)).astype(jnp.bfloat16))
        dv = dv + nn(jnp.concatenate(weights, axis=1), jnp.concatenate(ds, axis=0))
        dk = dk + nn(jnp.concatenate(slopes, axis=1), jnp.concatenate(qs, axis=0))
        sums = [dq + nn(kt, slope) for dq, slope in zip(sums, slopes)]
        for x, dq in zip(xs, sums):
            dq_ref[x] = dq
        grad_ref[0, j] = dk
        grad_ref[1, j] = dv

    over_tiles(info_ref, start_ref, blk, heads, tile)
    for a, g_ref in enumerate((ga_ref, gb_ref)):
        for j in range(PART):
            rows = slice(j * blk, (j + 1) * blk)
            g_ref[0, rows, :] = (grad_ref[0, a * PART + j] * back).astype(jnp.bfloat16)
            g_ref[1, rows, :] = grad_ref[1, a * PART + j].astype(jnp.bfloat16)
    if share == 0:
        for h in range(heads):
            columns = slice(h * hd, (h + 1) * hd)
            dq0_ref[:, columns] = (dq_ref[h] * back).T
            dq1_ref[:, columns] = (dq_ref[heads + h] * back).T.astype(jnp.bfloat16)


def backward(info, starts, q0, q1, d0, d1, part_a, part_b, s_mine, s_theirs, share, sums=()):
    blk, width = q0.shape
    hd = part_a.shape[2]
    heads = width // hd
    n = 2 * heads
    f32 = jnp.float32
    grad = jax.ShapeDtypeStruct(part_a.shape, jnp.bfloat16)
    two = pltpu.VMEM((n, blk, hd), q0.dtype)
    row = pltpu.VMEM((n, 1, blk), f32)
    work = [two, two, pltpu.VMEM((2, 2 * PART, blk, hd), part_a.dtype), pltpu.VMEM((2, 2 * PART, blk, hd), f32), row, row]
    if share == 1:
        shapes = (grad, grad, jax.ShapeDtypeStruct((n, hd, blk), f32))
    else:
        out = jax.ShapeDtypeStruct((blk, width), jnp.bfloat16)
        shapes = (grad, grad, out, jax.ShapeDtypeStruct((blk, width), f32), out)
        work += [pltpu.VMEM((n, hd, blk), f32)]
    args = (info, starts, q0, q1, d0, d1, part_a, part_b, s_mine, s_theirs) + tuple(sums)
    return pl.pallas_call(
        functools.partial(backward_kernel, heads, hd, share),
        out_shape=shapes,
        in_specs=[sm()] + [vm()] * (len(args) - 1),
        out_specs=(vm(),) * len(shapes),
        scratch_shapes=work,
        compiler_params=params(),
        cost_estimate=pl.CostEstimate(flops=20 * PART * n * blk * blk * hd, bytes_accessed=4 << 20, transcendentals=0),
        name="backward_part",
    )(*args)


def per_device(queries, keys, values, dout, doc_lengths):
    blk = queries.shape[0]
    seqs, subs = lax.axis_size("seq"), lax.axis_size("sub")
    seq, sub = lax.axis_index("seq"), lax.axis_index("sub")
    f32, bf16 = jnp.float32, jnp.bfloat16
    chip, core = seq // 2, seq % 2
    mate = sub + 1 - 2 * (sub % 2)
    far = (sub + 2 * (sub % 2) - 1 + subs) % subs
    infos, starts = tables(doc_lengths, chip, core, sub, mate, far, blk, subs)

    def swap_core(value):
        return lax.ppermute(value, "seq", [(s, s ^ 1) for s in range(seqs)])

    def swap_mate(value):
        return lax.ppermute(value, "sub", [(s, s ^ 1) for s in range(subs)])

    def swap_far(value):
        return lax.ppermute(value, "sub", [(s, (s + 2 * (s % 2) - 1) % subs) for s in range(subs)])

    def route(step, sign):
        pairs = [(s, s + 2 * (1 + step + 2 * (s % 2))) for s in range(seqs)]
        return [(a, b)[::sign] for a, b in pairs if b < seqs]

    own = jnp.stack([keys, values])
    q_mate = swap_mate(queries)
    pair = jnp.concatenate([own, swap_core(own)], axis=1)
    near = lax.ppermute(pair, "seq", route(0, 1))
    away = lax.ppermute(pair, "seq", route(1, 1))
    part_a = jnp.concatenate([away, near, own], axis=1)
    part_c = swap_far(part_a)
    part_b = swap_core(part_a)
    d_mate = swap_mate(dout)
    state = forward(infos[0], starts, queries, q_mate, part_a, part_b, 0)
    part_c, state = lax.optimization_barrier((part_c, state))
    part_d = swap_core(part_c)
    stats, mine, theirs = forward(infos[1], starts, queries, q_mate, part_c, part_d, 1, state, (dout, d_mate))
    stats_mate = swap_mate(stats)
    theirs = swap_mate(theirs)
    common = (queries, q_mate, dout, d_mate)
    grad_c, grad_d, dq = backward(infos[1], starts, *common, part_c, part_d, stats, stats_mate, 1)
    grad_c = (grad_c.astype(f32) + swap_core(grad_d).astype(f32)).astype(bf16)
    grad_c, dq = lax.optimization_barrier((grad_c, dq))
    grad_far = swap_far(grad_c)
    grad_a, grad_b, attended, dq_mine, dq_mate = backward(
        infos[0], starts, *common, part_a, part_b, stats, stats_mate, 0, (mine, theirs, dq)
    )
    dq_back = swap_mate(dq_mate)
    query_grad = (dq_mine + dq_back.astype(f32)).astype(bf16)
    grad = grad_a.astype(f32) + swap_core(grad_b).astype(f32) + grad_far.astype(f32)
    home = grad[:, : 4 * blk].astype(bf16)
    near = lax.ppermute(home[:, 2 * blk :], "seq", route(0, -1)).astype(f32)
    away = lax.ppermute(home[:, : 2 * blk], "seq", route(1, -1)).astype(f32)
    back = near + away
    other = swap_core(back[:, blk:].astype(bf16)).astype(f32)
    total = (grad[:, 4 * blk :] + back[:, :blk] + other).astype(bf16)
    return attended, query_grad, total[0], total[1]


def solution(mesh):
    rows = P(("seq", "sub"), None)
    return jax.shard_map(
        per_device,
        mesh=mesh,
        in_specs=(rows, rows, rows, rows, P()),
        out_specs=(rows, rows, rows, rows),
        check_vma=False,
    )
```

```python
import functools
import math

import jax
import jax.numpy as jnp
from jax import lax
from jax.experimental import pallas as pl
from jax.experimental.pallas import tpu as pltpu
from jax.sharding import PartitionSpec as P

BIG_NEG = -1e30
LOG2E = 1.4426950408889634
PART = 5


def nt(a, b):
    return lax.dot_general(a, b, (((1,), (1,)), ((), ())), preferred_element_type=jnp.float32)


def nn(a, b):
    return lax.dot_general(a, b, (((1,), (0,)), ((), ())), preferred_element_type=jnp.float32)


def table_kernel(blk, subs, ids_ref, len_ref, near_ref, far_ref, start_ref):
    chip, core, sub, mate, far = (ids_ref[i] for i in range(5))
    q0 = [((2 * chip + core) * subs + side) * blk for side in (sub, mate)]
    qpos = [q + lax.broadcasted_iota(jnp.int32, (1, blk), 1) for q in q0]
    zero = jnp.int32(0)
    begin, first, last = zero, [zero] * 2, [zero] * 2
    found = [jnp.zeros((1, blk), jnp.int32)] * 2
    for d in range(len_ref.shape[0]):
        for r in range(2):
            first[r] = jnp.where(begin <= q0[r], begin, first[r])
            last[r] = jnp.where(begin <= q0[r] + blk - 1, begin, last[r])
            found[r] = jnp.where(begin <= qpos[r], begin, found[r])
        begin = begin + len_ref[d]
    for r in range(2):
        start_ref[r] = found[r]
    list2 = 4 + 2 * PART
    list1 = list2 + 2 * PART
    for info_ref, share in ((near_ref, sub), (far_ref, far)):
        count2, count1 = zero, zero
        for j in range(2 * PART):
            owner = core if j < PART else 1 - core
            jj = j % PART
            back = 2 + 2 * owner if jj < 2 else 1 + 2 * owner if jj < 4 else 0
            parity = owner if jj % 2 == 0 else 1 - owner
            kstart = ((2 * (chip - back) + parity) * subs + share) * blk
            kend = kstart + blk - 1
            active = [(kend >= first[r]) & (kstart <= q0[r] + blk - 1) for r in range(2)]
            whole = [(kstart >= last[r]) & (kend <= q0[r]) for r in range(2)]
            double = active[0] & whole[0] & active[1] & whole[1]
            info_ref[4 + j] = kstart
            info_ref[list2 + count2] = j
            count2 = count2 + double.astype(jnp.int32)
            for r in range(2):
                info_ref[list1 + count1] = 2 * j + r
                count1 = count1 + (active[r] & jnp.logical_not(double)).astype(jnp.int32)
        info_ref[0] = count2
        info_ref[1] = count1
        info_ref[2] = q0[0]
        info_ref[3] = q0[1]


def tables(ids, doc_lengths, blk, subs):
    info = jax.ShapeDtypeStruct((4 + 2 * PART + 2 * PART + 4 * PART + 1,), jnp.int32)
    return pl.pallas_call(
        functools.partial(table_kernel, blk, subs),
        out_shape=(info, info, jax.ShapeDtypeStruct((2, 1, blk), jnp.int32)),
        in_specs=[sm(), sm()],
        out_specs=(sm(), sm(), vm()),
        name="tile_tables",
    )(ids, doc_lengths)


def fill(window_ref, part_refs, blk):
    for a, part in enumerate(part_refs):
        for kind in range(2):
            for j in range(PART):
                window_ref[kind, a * PART + j] = part[kind, j * blk:(j + 1) * blk, :]


def fill_heads(dest_ref, sources, heads, hd):
    for r, source in enumerate(sources):
        for h in range(heads):
            dest_ref[r * heads + h] = source[:, h * hd:(h + 1) * hd]


def over_tiles(info_ref, start_ref, blk, heads, body):
    count2, count1 = info_ref[0], info_ref[1]
    list2 = 4 + 2 * PART
    list1 = list2 + 2 * PART

    def double(i, _):
        body(info_ref[list2 + i], list(range(2 * heads)), None)
        return 0

    def single(i, _):
        entry = info_ref[list1 + i]
        j, r = lax.shift_right_logical(entry, 1), lax.bitwise_and(entry, 1)
        kpos = info_ref[4 + j] + lax.broadcasted_iota(jnp.int32, (blk, blk), 0)
        qpos = info_ref[2 + r] + lax.broadcasted_iota(jnp.int32, (blk, blk), 1)
        body(j, [r * heads + h for h in range(heads)], (kpos <= qpos) & (kpos >= start_ref[r]))
        return 0

    lax.fori_loop(0, count2, double, 0)
    lax.fori_loop(0, count1, single, 0)


def forward_kernel(heads, hd, share, info_ref, start_ref, q0_ref, q1_ref, ka_ref, kb_ref, *rest):
    blk = q0_ref.shape[0]
    scale = LOG2E / math.sqrt(hd)
    if share == 0:
        m_ref, l_ref, a_ref, q_ref, window_ref = rest
        m_ref[...] = jnp.full(m_ref.shape, BIG_NEG, jnp.float32)
        l_ref[...] = jnp.zeros(l_ref.shape, jnp.float32)
        a_ref[...] = jnp.zeros(a_ref.shape, jnp.float32)
    else:
        m_in, l_in, a_in, d0_ref, d1_ref, stat_ref, mine_ref, theirs_ref = rest[:8]
        q_ref, window_ref, m_ref, l_ref, a_ref = rest[8:]
        m_ref[...] = m_in[...]
        l_ref[...] = l_in[...]
        a_ref[...] = a_in[...]
    fill(window_ref, (ka_ref, kb_ref), blk)
    fill_heads(q_ref, (q0_ref, q1_ref), heads, hd)

    def tile(j, xs, mask):
        kb = window_ref[0, j]
        vt = window_ref[1, j].T
        old = [(m_ref[x], l_ref[x], a_ref[x]) for x in xs]
        found = [nt(kb, q_ref[x]) * scale for x in xs]
        if mask is not None:
            found = [jnp.where(mask, s, BIG_NEG) for s in found]
        new = []
        for s, (m_old, l_old, a_old) in zip(found, old):
            m_new = jnp.maximum(m_old, jnp.max(s, axis=0, keepdims=True))
            p = jnp.exp2(s - m_new)
            f = jnp.exp2(m_old - m_new)
            total = l_old * f + jnp.sum(p, axis=0, keepdims=True)
            new.append((m_new, total, a_old * f + nn(vt, p.astype(jnp.bfloat16))))
        for x, (m_new, total, acc) in zip(xs, new):
            m_ref[x] = m_new
            l_ref[x] = total
            a_ref[x] = acc

    over_tiles(info_ref, start_ref, blk, heads, tile)
    if share == 1:
        for r, d_ref in enumerate((d0_ref, d1_ref)):
            for h in range(heads):
                x = r * heads + h
                dt = d_ref[:, h * hd:(h + 1) * hd].astype(jnp.float32).T
                stat_ref[x, 0:1] = m_ref[x]
                stat_ref[x, 1:2] = l_ref[x]
                stat_ref[x, 2:3] = jnp.sum(dt * a_ref[x], axis=0, keepdims=True)
        mine_ref[...] = a_ref[:heads]
        theirs_ref[...] = a_ref[heads:].astype(jnp.bfloat16)


def vm():
    return pl.BlockSpec(memory_space=pltpu.VMEM)


def sm():
    return pl.BlockSpec(memory_space=pltpu.SMEM)


def params():
    return pltpu.CompilerParams(vmem_limit_bytes=24 << 20)


def forward(info, starts, q0, q1, part_a, part_b, share, state=(), douts=()):
    blk, width = q0.shape
    hd = part_a.shape[2]
    heads = width // hd
    n = 2 * heads
    f32 = jnp.float32
    row = jax.ShapeDtypeStruct((n, 1, blk), f32)
    work = [pltpu.VMEM((n, blk, hd), q0.dtype), pltpu.VMEM((2, 2 * PART, blk, hd), part_a.dtype)]
    if share == 0:
        shapes = (row, row, jax.ShapeDtypeStruct((n, hd, blk), f32))
    else:
        shapes = (jax.ShapeDtypeStruct((n, 3, blk), f32), jax.ShapeDtypeStruct((heads, hd, blk), f32),
                  jax.ShapeDtypeStruct((heads, hd, blk), jnp.bfloat16))
        work += [pltpu.VMEM((n, 1, blk), f32), pltpu.VMEM((n, 1, blk), f32), pltpu.VMEM((n, hd, blk), f32)]
    args = (info, starts, q0, q1, part_a, part_b) + tuple(state) + tuple(douts)
    return pl.pallas_call(
        functools.partial(forward_kernel, heads, hd, share),
        out_shape=shapes,
        in_specs=[sm()] + [vm()] * (len(args) - 1),
        out_specs=(vm(),) * 3,
        scratch_shapes=work,
        compiler_params=params(),
        cost_estimate=pl.CostEstimate(flops=8 * PART * n * blk * blk * hd, bytes_accessed=4 << 20, transcendentals=0),
        name="forward_part",
    )(*args)


def merge_stats(s_mine, s_theirs):
    m = jnp.maximum(s_mine[0:1], s_theirs[0:1])
    fa = jnp.exp2(s_mine[0:1] - m)
    fb = jnp.exp2(s_theirs[0:1] - m)
    total = s_mine[1:2] * fa + s_theirs[1:2] * fb
    delta = (s_mine[2:3] * fa + s_theirs[2:3] * fb) / total
    return m + jnp.log2(total), fa / total, fb / total, delta


def backward_kernel(heads, hd, share, info_ref, start_ref, q0_ref, q1_ref, d0_ref, d1_ref, ka_ref, kb_ref,
                    sa_ref, sb_ref, *rest):
    blk = q0_ref.shape[0]
    scale = LOG2E / math.sqrt(hd)
    back = 1.0 / math.sqrt(hd)
    if share == 1:
        ga_ref, gb_ref, dq_ref = rest[:3]
        work = rest[3:]
        dq_ref[...] = jnp.zeros(dq_ref.shape, jnp.float32)
    else:
        mine_ref, theirs_ref, dq_in, ga_ref, gb_ref, att_ref, dq0_ref, dq1_ref = rest[:8]
        work = rest[8:-1]
        dq_ref = rest[-1]
        dq_ref[...] = dq_in[...]
    q_ref, d_ref, window_ref, grad_ref, log_ref, delta_ref = work
    grad_ref[...] = jnp.zeros(grad_ref.shape, jnp.float32)
    fill(window_ref, (ka_ref, kb_ref), blk)
    fill_heads(q_ref, (q0_ref, q1_ref), heads, hd)
    fill_heads(d_ref, (d0_ref, d1_ref), heads, hd)
    for r in range(2):
        for h in range(heads):
            x = r * heads + h
            log_total, wa, wb, delta = merge_stats(sa_ref[x], sb_ref[(1 - r) * heads + h])
            log_ref[x] = log_total
            delta_ref[x] = delta
            if share == 0 and r == 0:
                att = mine_ref[h] * wa + theirs_ref[h].astype(jnp.float32) * wb
                att_ref[:, h * hd:(h + 1) * hd] = att.T.astype(jnp.bfloat16)

    def tile(j, xs, mask):
        kb = window_ref[0, j]
        vb = window_ref[1, j]
        kt = kb.T
        qs = [q_ref[x] for x in xs]
        ds = [d_ref[x] for x in xs]
        rows = [(log_ref[x], delta_ref[x]) for x in xs]
        sums = [dq_ref[x] for x in xs]
        dk, dv = grad_ref[0, j], grad_ref[1, j]
        found = [nt(kb, q) for q in qs]
        pushed = [nt(vb, d) for d in ds]
        weights, slopes = [], []
        for s, dp, (log_total, delta) in zip(found, pushed, rows):
            s = s * scale
            if mask is not None:
                s = jnp.where(mask, s, BIG_NEG)
            p = jnp.exp2(s - log_total)
            weights.append(p.astype(jnp.bfloat16))
            slopes.append((p * (dp - delta)).astype(jnp.bfloat16))
        dv = dv + nn(jnp.concatenate(weights, axis=1), jnp.concatenate(ds, axis=0))
        dk = dk + nn(jnp.concatenate(slopes, axis=1), jnp.concatenate(qs, axis=0))
        sums = [dq + nn(kt, slope) for dq, slope in zip(sums, slopes)]
        for x, dq in zip(xs, sums):
            dq_ref[x] = dq
        grad_ref[0, j] = dk
        grad_ref[1, j] = dv

    over_tiles(info_ref, start_ref, blk, heads, tile)
    for a, g_ref in enumerate((ga_ref, gb_ref)):
        for j in range(PART):
            rows = slice(j * blk, (j + 1) * blk)
            g_ref[0, rows, :] = (grad_ref[0, a * PART + j] * back).astype(jnp.bfloat16)
            g_ref[1, rows, :] = grad_ref[1, a * PART + j].astype(jnp.bfloat16)
    if share == 0:
        for h in range(heads):
            columns = slice(h * hd, (h + 1) * hd)
            dq0_ref[:, columns] = (dq_ref[h] * back).T
            dq1_ref[:, columns] = (dq_ref[heads + h] * back).T.astype(jnp.bfloat16)


def backward(info, starts, q0, q1, d0, d1, part_a, part_b, s_mine, s_theirs, share, sums=()):
    blk, width = q0.shape
    hd = part_a.shape[2]
    heads = width // hd
    n = 2 * heads
    f32 = jnp.float32
    grad = jax.ShapeDtypeStruct(part_a.shape, jnp.bfloat16)
    two = pltpu.VMEM((n, blk, hd), q0.dtype)
    row = pltpu.VMEM((n, 1, blk), f32)
    work = [two, two, pltpu.VMEM((2, 2 * PART, blk, hd), part_a.dtype), pltpu.VMEM((2, 2 * PART, blk, hd), f32), row, row]
    if share == 1:
        shapes = (grad, grad, jax.ShapeDtypeStruct((n, hd, blk), f32))
    else:
        out = jax.ShapeDtypeStruct((blk, width), jnp.bfloat16)
        shapes = (grad, grad, out, jax.ShapeDtypeStruct((blk, width), f32), out)
        work += [pltpu.VMEM((n, hd, blk), f32)]
    args = (info, starts, q0, q1, d0, d1, part_a, part_b, s_mine, s_theirs) + tuple(sums)
    return pl.pallas_call(
        functools.partial(backward_kernel, heads, hd, share),
        out_shape=shapes,
        in_specs=[sm()] + [vm()] * (len(args) - 1),
        out_specs=(vm(),) * len(shapes),
        scratch_shapes=work,
        compiler_params=params(),
        cost_estimate=pl.CostEstimate(flops=20 * PART * n * blk * blk * hd, bytes_accessed=4 << 20, transcendentals=0),
        name="backward_part",
    )(*args)


def per_device(queries, keys, values, dout, doc_lengths):
    blk = queries.shape[0]
    seqs, subs = lax.axis_size("seq"), lax.axis_size("sub")
    seq, sub = lax.axis_index("seq"), lax.axis_index("sub")
    f32, bf16 = jnp.float32, jnp.bfloat16
    chip, core = seq // 2, seq % 2
    mate = sub + 1 - 2 * (sub % 2)
    far = (sub + 2 * (sub % 2) - 1 + subs) % subs
    ids = jnp.stack([chip, core, sub, mate, far]).astype(jnp.int32)
    *infos, starts = tables(ids, doc_lengths, blk, subs)

    def swap_core(value):
        return lax.ppermute(value, "seq", [(s, s ^ 1) for s in range(seqs)])

    def swap_mate(value):
        return lax.ppermute(value, "sub", [(s, s ^ 1) for s in range(subs)])

    def swap_far(value):
        return lax.ppermute(value, "sub", [(s, (s + 2 * (s % 2) - 1) % subs) for s in range(subs)])

    def route(step, sign):
        pairs = [(s, s + 2 * (1 + step + 2 * (s % 2))) for s in range(seqs)]
        return [(a, b)[::sign] for a, b in pairs if b < seqs]

    tie = lax.optimization_barrier
    own = tie(jnp.stack([keys, values]))
    q_mate = swap_mate(queries)
    pair = jnp.concatenate([own, swap_core(own)], axis=1)
    near = lax.ppermute(pair, "seq", route(0, 1))
    away = lax.ppermute(pair, "seq", route(1, 1))
    near, away, infos, starts, q_mate = tie((near, away, infos, starts, q_mate))
    part_a = jnp.concatenate([away, near, own], axis=1)
    part_c = swap_far(part_a)
    part_b = swap_core(part_a)
    d_mate = swap_mate(dout)
    state = forward(infos[0], starts, queries, q_mate, part_a, part_b, 0)
    part_c, state, d_mate = tie((part_c, state, d_mate))
    part_d = swap_core(part_c)
    stats, mine, theirs = forward(infos[1], starts, queries, q_mate, part_c, part_d, 1, state, (dout, d_mate))
    stats_mate = swap_mate(stats)
    theirs = swap_mate(theirs)
    common = (queries, q_mate, dout, d_mate)
    grad_c, grad_d, dq = backward(infos[1], starts, *common, part_c, part_d, stats, stats_mate, 1)
    grad_d, theirs = tie((grad_d, theirs))
    grad_c = (grad_c.astype(f32) + swap_core(grad_d).astype(f32)).astype(bf16)
    grad_c, dq = tie((grad_c, dq))
    grad_far = swap_far(grad_c)
    grad_a, grad_b, attended, dq_mine, dq_mate = backward(
        infos[0], starts, *common, part_a, part_b, stats, stats_mate, 0, (mine, theirs, dq)
    )
    dq_back = swap_mate(dq_mate)
    grad_b, grad_far = tie((grad_b, grad_far))
    grad = grad_a.astype(f32) + swap_core(grad_b).astype(f32) + grad_far.astype(f32)
    home = grad[:, : 4 * blk].astype(bf16)
    near = lax.ppermute(home[:, 2 * blk :], "seq", route(0, -1)).astype(f32)
    away = lax.ppermute(home[:, : 2 * blk], "seq", route(1, -1)).astype(f32)
    query_grad = (dq_mine + dq_back.astype(f32)).astype(bf16)
    near, query_grad = tie((near, query_grad))
    back = near + away
    other = swap_core(back[:, blk:].astype(bf16)).astype(f32)
    total = [(grad[i, 4 * blk :] + back[i, :blk] + other[i]).astype(bf16) for i in range(2)]
    return attended, query_grad, total[0], total[1]


def solution(mesh):
    rows = P(("seq", "sub"), None)
    return jax.shard_map(
        per_device,
        mesh=mesh,
        in_specs=(rows, rows, rows, rows, P()),
        out_specs=(rows, rows, rows, rows),
        check_vma=False,
    )
```

```python
import functools
import math

import jax
import jax.numpy as jnp
from jax import lax
from jax.experimental import pallas as pl
from jax.experimental.pallas import tpu as pltpu
from jax.sharding import PartitionSpec as P

BIG_NEG = -1e30
LOG2E = 1.4426950408889634
PART = 5


def nt(a, b):
    return lax.dot_general(a, b, (((1,), (1,)), ((), ())), preferred_element_type=jnp.float32)


def nn(a, b):
    return lax.dot_general(a, b, (((1,), (0,)), ((), ())), preferred_element_type=jnp.float32)


def table_kernel(blk, subs, ids_ref, len_ref, near_ref, far_ref, start_ref):
    chip, core, sub, mate, far = (ids_ref[i] for i in range(5))
    q0 = [((2 * chip + core) * subs + side) * blk for side in (sub, mate)]
    qpos = [q + lax.broadcasted_iota(jnp.int32, (1, blk), 1) for q in q0]
    zero = jnp.int32(0)
    begin, first, last = zero, [zero] * 2, [zero] * 2
    found = [jnp.zeros((1, blk), jnp.int32)] * 2
    for d in range(len_ref.shape[0]):
        for r in range(2):
            first[r] = jnp.where(begin <= q0[r], begin, first[r])
            last[r] = jnp.where(begin <= q0[r] + blk - 1, begin, last[r])
            found[r] = jnp.where(begin <= qpos[r], begin, found[r])
        begin = begin + len_ref[d]
    for r in range(2):
        start_ref[r] = found[r]
    list2 = 4 + 2 * PART
    list1 = list2 + 2 * PART
    for info_ref, share in ((near_ref, sub), (far_ref, far)):
        count2, count1 = zero, zero
        for j in range(2 * PART):
            owner = core if j < PART else 1 - core
            jj = j % PART
            back = 2 + 2 * owner if jj < 2 else 1 + 2 * owner if jj < 4 else 0
            parity = owner if jj % 2 == 0 else 1 - owner
            kstart = ((2 * (chip - back) + parity) * subs + share) * blk
            kend = kstart + blk - 1
            active = [(kend >= first[r]) & (kstart <= q0[r] + blk - 1) for r in range(2)]
            whole = [(kstart >= last[r]) & (kend <= q0[r]) for r in range(2)]
            clear = active[0] & whole[0] & active[1] & whole[1]
            mixed = (active[0] | active[1]) & jnp.logical_not(clear)
            info_ref[4 + j] = kstart
            info_ref[list2 + count2] = j
            count2 = count2 + clear.astype(jnp.int32)
            info_ref[list1 + count1] = j
            count1 = count1 + mixed.astype(jnp.int32)
        info_ref[0] = count2
        info_ref[1] = count1
        info_ref[2] = q0[0]
        info_ref[3] = q0[1]


def tables(ids, doc_lengths, blk, subs):
    info = jax.ShapeDtypeStruct((4 + 2 * PART + 2 * PART + 2 * PART + 1,), jnp.int32)
    return pl.pallas_call(
        functools.partial(table_kernel, blk, subs),
        out_shape=(info, info, jax.ShapeDtypeStruct((2, 1, blk), jnp.int32)),
        in_specs=[sm(), sm()],
        out_specs=(sm(), sm(), vm()),
        name="tile_tables",
    )(ids, doc_lengths)


def fill(window_ref, part_refs, blk):
    for a, part in enumerate(part_refs):
        for kind in range(2):
            for j in range(PART):
                window_ref[kind, a * PART + j] = part[kind, j * blk:(j + 1) * blk, :]


def fill_heads(dest_ref, sources, heads, hd):
    for r, source in enumerate(sources):
        for h in range(heads):
            dest_ref[r * heads + h] = source[:, h * hd:(h + 1) * hd]


def fill_scaled(dest_ref, sources, heads, hd, scale):
    for r, source in enumerate(sources):
        for h in range(heads):
            whole = source[:, h * hd:(h + 1) * hd].astype(jnp.float32) * scale
            high = whole.astype(jnp.bfloat16)
            dest_ref[r * heads + h, :, :hd] = high
            dest_ref[r * heads + h, :, hd:] = (whole - high.astype(jnp.float32)).astype(jnp.bfloat16)


def over_tiles(info_ref, start_ref, bias_ref, blk, tile, pairs=None):
    list2 = 4 + 2 * PART
    list1 = list2 + 2 * PART

    def clear(i, _):
        tile(info_ref[list2 + i], None)
        return 0

    def mixed(i, _):
        j = info_ref[list1 + i]
        kpos = info_ref[4 + j] + lax.broadcasted_iota(jnp.int32, (blk, blk), 0)
        for r in range(2):
            qpos = info_ref[2 + r] + lax.broadcasted_iota(jnp.int32, (1, blk), 1)
            bias_ref[r] = jnp.where((kpos <= qpos) & (kpos >= start_ref[r]), 0.0, BIG_NEG)
        tile(j, bias_ref)
        return 0

    count = info_ref[0]
    if pairs is None:
        lax.fori_loop(0, count, clear, 0)
    else:
        half = lax.shift_right_logical(count, 1)

        def two(i, _):
            pairs(info_ref[list2 + 2 * i], info_ref[list2 + 2 * i + 1])
            return 0

        lax.fori_loop(0, half, two, 0)
        lax.fori_loop(2 * half, count, clear, 0)
    lax.fori_loop(0, info_ref[1], mixed, 0)


def forward_kernel(heads, hd, share, info_ref, start_ref, q0_ref, q1_ref, ka_ref, kb_ref, *rest):
    blk = q0_ref.shape[0]
    scale = LOG2E / math.sqrt(hd)
    if share == 0:
        m_ref, l_ref, a_ref, qs_ref, window_ref, bias_ref = rest
        m_ref[...] = jnp.full(m_ref.shape, BIG_NEG, jnp.float32)
        l_ref[...] = jnp.zeros(l_ref.shape, jnp.float32)
        a_ref[...] = jnp.zeros(a_ref.shape, jnp.float32)
    else:
        m_in, l_in, a_in, d0_ref, d1_ref, stat_ref, mine_ref, theirs_ref = rest[:8]
        qs_ref, window_ref, bias_ref, m_ref, l_ref, a_ref = rest[8:]
        m_ref[...] = m_in[...]
        l_ref[...] = l_in[...]
        a_ref[...] = a_in[...]
    fill(window_ref, (ka_ref, kb_ref), blk)
    fill_scaled(qs_ref, (q0_ref, q1_ref), heads, hd, scale)

    def update(kb, vb, masks):
        xs = range(2 * heads)
        vt = jnp.concatenate([vb.T, jnp.ones((16, vb.shape[0]), jnp.bfloat16)], axis=0)
        k2 = jnp.concatenate([kb, kb], axis=1)
        old = [(m_ref[x], l_ref[x], a_ref[x]) for x in xs]
        found = [nt(k2, qs_ref[x]) for x in xs]
        if masks is not None:
            found = [s + masks[x // heads] for x, s in zip(xs, found)]
        new = []
        for s, (m_old, l_old, a_old) in zip(found, old):
            m_new = jnp.maximum(m_old, jnp.max(s, axis=0, keepdims=True))
            p = jnp.exp2(s - m_new)
            f = jnp.exp2(m_old - m_new)
            both = nn(vt, p.astype(jnp.bfloat16))
            new.append((m_new, l_old * f + both[hd:hd + 1], a_old * f + both[:hd]))
        for x, (m_new, total, acc) in zip(xs, new):
            m_ref[x] = m_new
            l_ref[x] = total
            a_ref[x] = acc

    def tile(j, masks):
        update(window_ref[0, j], window_ref[1, j], masks)

    def pairs(j1, j2):
        kb, vb = [jnp.concatenate([window_ref[i, j1], window_ref[i, j2]], axis=0) for i in range(2)]
        update(kb, vb, None)

    over_tiles(info_ref, start_ref, bias_ref, blk, tile, pairs)
    if share == 1:
        for r, d_ref in enumerate((d0_ref, d1_ref)):
            for h in range(heads):
                x = r * heads + h
                dt = d_ref[:, h * hd:(h + 1) * hd].astype(jnp.float32).T
                stat_ref[x, 0:1] = m_ref[x]
                stat_ref[x, 1:2] = l_ref[x]
                stat_ref[x, 2:3] = jnp.sum(dt * a_ref[x], axis=0, keepdims=True)
        mine_ref[...] = a_ref[:heads]
        theirs_ref[...] = a_ref[heads:].astype(jnp.bfloat16)


def vm():
    return pl.BlockSpec(memory_space=pltpu.VMEM)


def sm():
    return pl.BlockSpec(memory_space=pltpu.SMEM)


def params():
    return pltpu.CompilerParams(vmem_limit_bytes=24 << 20)


def forward(info, starts, q0, q1, part_a, part_b, share, state=(), douts=()):
    blk, width = q0.shape
    hd = part_a.shape[2]
    heads = width // hd
    n = 2 * heads
    f32 = jnp.float32
    row = jax.ShapeDtypeStruct((n, 1, blk), f32)
    work = [pltpu.VMEM((n, blk, 2 * hd), q0.dtype), pltpu.VMEM((2, 2 * PART, blk, hd), part_a.dtype),
            pltpu.VMEM((2, blk, blk), f32)]
    if share == 0:
        shapes = (row, row, jax.ShapeDtypeStruct((n, hd, blk), f32))
    else:
        shapes = (jax.ShapeDtypeStruct((n, 3, blk), f32), jax.ShapeDtypeStruct((heads, hd, blk), f32),
                  jax.ShapeDtypeStruct((heads, hd, blk), jnp.bfloat16))
        work += [pltpu.VMEM((n, 1, blk), f32), pltpu.VMEM((n, 1, blk), f32), pltpu.VMEM((n, hd, blk), f32)]
    args = (info, starts, q0, q1, part_a, part_b) + tuple(state) + tuple(douts)
    return pl.pallas_call(
        functools.partial(forward_kernel, heads, hd, share),
        out_shape=shapes,
        in_specs=[sm()] + [vm()] * (len(args) - 1),
        out_specs=(vm(),) * 3,
        scratch_shapes=work,
        compiler_params=params(),
        cost_estimate=pl.CostEstimate(flops=8 * PART * n * blk * blk * hd, bytes_accessed=4 << 20, transcendentals=0),
        name="forward_part",
    )(*args)


def merge_stats(s_mine, s_theirs):
    m = jnp.maximum(s_mine[0:1], s_theirs[0:1])
    fa = jnp.exp2(s_mine[0:1] - m)
    fb = jnp.exp2(s_theirs[0:1] - m)
    total = s_mine[1:2] * fa + s_theirs[1:2] * fb
    delta = (s_mine[2:3] * fa + s_theirs[2:3] * fb) / total
    return m + jnp.log2(total), fa / total, fb / total, delta


def backward_kernel(heads, hd, share, info_ref, start_ref, q0_ref, q1_ref, d0_ref, d1_ref, ka_ref, kb_ref,
                    sa_ref, sb_ref, *rest):
    blk = q0_ref.shape[0]
    scale = LOG2E / math.sqrt(hd)
    back = 1.0 / math.sqrt(hd)
    if share == 1:
        ga_ref, gb_ref, dq_ref = rest[:3]
        work = rest[3:]
        dq_ref[...] = jnp.zeros(dq_ref.shape, jnp.float32)
    else:
        mine_ref, theirs_ref, dq_in, ga_ref, gb_ref, att_ref, dq0_ref, dq1_ref = rest[:8]
        work = rest[8:-1]
        dq_ref = rest[-1]
        dq_ref[...] = dq_in[...]
    q_ref, d_ref, window_ref, grad_ref, log_ref, delta_ref, qs_ref, bias_ref = work
    grad_ref[...] = jnp.zeros(grad_ref.shape, jnp.float32)
    fill(window_ref, (ka_ref, kb_ref), blk)
    fill_heads(q_ref, (q0_ref, q1_ref), heads, hd)
    fill_heads(d_ref, (d0_ref, d1_ref), heads, hd)
    fill_scaled(qs_ref, (q0_ref, q1_ref), heads, hd, scale)
    for r in range(2):
        for h in range(heads):
            x = r * heads + h
            log_total, wa, wb, delta = merge_stats(sa_ref[x], sb_ref[(1 - r) * heads + h])
            log_ref[x] = log_total
            delta_ref[x] = delta
            if share == 0 and r == 0:
                att = mine_ref[h] * wa + theirs_ref[h].astype(jnp.float32) * wb
                att_ref[:, h * hd:(h + 1) * hd] = att.T.astype(jnp.bfloat16)

    def tile(j, masks):
        xs = range(2 * heads)
        kb = window_ref[0, j]
        vb = window_ref[1, j]
        kt = kb.T
        qs = [q_ref[x] for x in xs]
        ds = [d_ref[x] for x in xs]
        rows = [(log_ref[x], delta_ref[x]) for x in xs]
        sums = [dq_ref[x] for x in xs]
        dk, dv = grad_ref[0, j], grad_ref[1, j]
        k2 = jnp.concatenate([kb, kb], axis=1)
        found = [nt(k2, qs_ref[x]) for x in xs]
        pushed = [nt(vb, d) for d in ds]
        weights, slopes = [], []
        for x, s, dp, (log_total, delta) in zip(xs, found, pushed, rows):
            if masks is not None:
                s = s + masks[x // heads]
            p = jnp.exp2(s - log_total)
            weights.append(p.astype(jnp.bfloat16))
            slopes.append((p * (dp - delta)).astype(jnp.bfloat16))
        dv = dv + nn(jnp.concatenate(weights, axis=1), jnp.concatenate(ds, axis=0))
        dk = dk + nn(jnp.concatenate(slopes, axis=1), jnp.concatenate(qs, axis=0))
        sums = [dq + nn(kt, slope) for dq, slope in zip(sums, slopes)]
        for x, dq in zip(xs, sums):
            dq_ref[x] = dq
        grad_ref[0, j] = dk
        grad_ref[1, j] = dv

    def pairs(j1, j2):
        xs = range(2 * heads)
        kb = jnp.concatenate([window_ref[0, j1], window_ref[0, j2]], axis=0)
        vb = jnp.concatenate([window_ref[1, j1], window_ref[1, j2]], axis=0)
        kt = kb.T
        qs = [q_ref[x] for x in xs]
        ds = [d_ref[x] for x in xs]
        rows = [(log_ref[x], delta_ref[x]) for x in xs]
        sums = [dq_ref[x] for x in xs]
        k2 = jnp.concatenate([kb, kb], axis=1)
        found = [nt(k2, qs_ref[x]) for x in xs]
        pushed = [nt(vb, d) for d in ds]
        weights, slopes = [], []
        for x, s, dp, (log_total, delta) in zip(xs, found, pushed, rows):
            p = jnp.exp2(s - log_total)
            weights.append(p.astype(jnp.bfloat16))
            slopes.append((p * (dp - delta)).astype(jnp.bfloat16))
        dv = nn(jnp.concatenate(weights, axis=1), jnp.concatenate(ds, axis=0))
        dk = nn(jnp.concatenate(slopes, axis=1), jnp.concatenate(qs, axis=0))
        sums = [dq + nn(kt, slope) for dq, slope in zip(sums, slopes)]
        for x, dq in zip(xs, sums):
            dq_ref[x] = dq
        grad_ref[0, j1] = dk[:blk]
        grad_ref[0, j2] = dk[blk:]
        grad_ref[1, j1] = dv[:blk]
        grad_ref[1, j2] = dv[blk:]

    over_tiles(info_ref, start_ref, bias_ref, blk, tile, pairs)
    for a, g_ref in enumerate((ga_ref, gb_ref)):
        for j in range(PART):
            rows = slice(j * blk, (j + 1) * blk)
            g_ref[0, rows, :] = (grad_ref[0, a * PART + j] * back).astype(jnp.bfloat16)
            g_ref[1, rows, :] = grad_ref[1, a * PART + j].astype(jnp.bfloat16)
    if share == 0:
        for h in range(heads):
            columns = slice(h * hd, (h + 1) * hd)
            dq0_ref[:, columns] = (dq_ref[h] * back).T
            dq1_ref[:, columns] = (dq_ref[heads + h] * back).T.astype(jnp.bfloat16)


def backward(info, starts, q0, q1, d0, d1, part_a, part_b, s_mine, s_theirs, share, sums=()):
    blk, width = q0.shape
    hd = part_a.shape[2]
    heads = width // hd
    n = 2 * heads
    f32 = jnp.float32
    grad = jax.ShapeDtypeStruct(part_a.shape, jnp.bfloat16)
    two = pltpu.VMEM((n, blk, hd), q0.dtype)
    row = pltpu.VMEM((n, 1, blk), f32)
    work = [two, two, pltpu.VMEM((2, 2 * PART, blk, hd), part_a.dtype), pltpu.VMEM((2, 2 * PART, blk, hd), f32), row, row,
            pltpu.VMEM((n, blk, 2 * hd), q0.dtype), pltpu.VMEM((2, blk, blk), f32)]
    if share == 1:
        shapes = (grad, grad, jax.ShapeDtypeStruct((n, hd, blk), f32))
    else:
        out = jax.ShapeDtypeStruct((blk, width), jnp.bfloat16)
        shapes = (grad, grad, out, jax.ShapeDtypeStruct((blk, width), f32), out)
        work += [pltpu.VMEM((n, hd, blk), f32)]
    args = (info, starts, q0, q1, d0, d1, part_a, part_b, s_mine, s_theirs) + tuple(sums)
    return pl.pallas_call(
        functools.partial(backward_kernel, heads, hd, share),
        out_shape=shapes,
        in_specs=[sm()] + [vm()] * (len(args) - 1),
        out_specs=(vm(),) * len(shapes),
        scratch_shapes=work,
        compiler_params=params(),
        cost_estimate=pl.CostEstimate(flops=20 * PART * n * blk * blk * hd, bytes_accessed=4 << 20, transcendentals=0),
        name="backward_part",
    )(*args)


def per_device(queries, keys, values, dout, doc_lengths):
    blk = queries.shape[0]
    seqs, subs = lax.axis_size("seq"), lax.axis_size("sub")
    seq, sub = lax.axis_index("seq"), lax.axis_index("sub")
    f32, bf16 = jnp.float32, jnp.bfloat16
    chip, core = seq // 2, seq % 2
    mate = sub + 1 - 2 * (sub % 2)
    far = (sub + 2 * (sub % 2) - 1 + subs) % subs
    ids = jnp.stack([chip, core, sub, mate, far]).astype(jnp.int32)
    *infos, starts = tables(ids, doc_lengths, blk, subs)

    def swap_core(value):
        return lax.ppermute(value, "seq", [(s, s ^ 1) for s in range(seqs)])

    def swap_mate(value):
        return lax.ppermute(value, "sub", [(s, s ^ 1) for s in range(subs)])

    def swap_far(value):
        return lax.ppermute(value, "sub", [(s, (s + 2 * (s % 2) - 1) % subs) for s in range(subs)])

    def route(step, sign):
        pairs = [(s, s + 2 * (1 + step + 2 * (s % 2))) for s in range(seqs)]
        return [(a, b)[::sign] for a, b in pairs if b < seqs]

    tie = lax.optimization_barrier
    other_keys, other_values = swap_core(keys), swap_core(values)
    q_mate, d_mate = swap_mate(queries), swap_mate(dout)
    own = jnp.stack([keys, values])
    pair = tie(jnp.concatenate([own, jnp.stack([other_keys, other_values])], axis=1))
    own = pair[:, :blk]
    near = lax.ppermute(pair, "seq", route(0, 1))
    away = lax.ppermute(pair, "seq", route(1, 1))
    near, away, infos, starts, q_mate, d_mate = tie((near, away, infos, starts, q_mate, d_mate))
    part_a = jnp.concatenate([away, near, own], axis=1)
    part_c = swap_far(part_a)
    part_b = swap_core(part_a)
    state = forward(infos[0], starts, queries, q_mate, part_a, part_b, 0)
    part_c, state = tie((part_c, state))
    part_d = swap_core(part_c)
    stats, mine, theirs = forward(infos[1], starts, queries, q_mate, part_c, part_d, 1, state, (dout, d_mate))
    stats_mate = swap_mate(stats)
    theirs = swap_mate(theirs)
    common = (queries, q_mate, dout, d_mate)
    grad_c, grad_d, dq = backward(infos[1], starts, *common, part_c, part_d, stats, stats_mate, 1)
    grad_d, theirs = tie((grad_d, theirs))
    grad_c = (grad_c.astype(f32) + swap_core(grad_d).astype(f32)).astype(bf16)
    grad_c, dq = tie((grad_c, dq))
    grad_far = swap_far(grad_c)
    grad_a, grad_b, attended, dq_mine, dq_mate = backward(
        infos[0], starts, *common, part_a, part_b, stats, stats_mate, 0, (mine, theirs, dq)
    )
    grad_b, grad_far = tie((grad_b, grad_far))
    grad = grad_a.astype(f32) + swap_core(grad_b).astype(f32) + grad_far.astype(f32)
    home, dq_mate = tie((grad[:, : 4 * blk].astype(bf16), dq_mate))
    dq_back = swap_mate(dq_mate)
    near = lax.ppermute(home[:, 2 * blk :], "seq", route(0, -1)).astype(f32)
    away = lax.ppermute(home[:, : 2 * blk], "seq", route(1, -1)).astype(f32)
    query_grad = (dq_mine + dq_back.astype(f32)).astype(bf16)
    near, query_grad = tie((near, query_grad))
    back = near + away
    other = swap_core(back[:, blk:].astype(bf16)).astype(f32)
    total = [(grad[i, 4 * blk :] + back[i, :blk] + other[i]).astype(bf16) for i in range(2)]
    return attended, query_grad, total[0], total[1]


def solution(mesh):
    rows = P(("seq", "sub"), None)
    return jax.shard_map(
        per_device,
        mesh=mesh,
        in_specs=(rows, rows, rows, rows, P()),
        out_specs=(rows, rows, rows, rows),
        check_vma=False,
    )
```

```python
import functools
import math

import jax
import jax.numpy as jnp
from jax import lax
from jax.experimental import pallas as pl
from jax.experimental.pallas import tpu as pltpu
from jax.sharding import PartitionSpec as P

BIG_NEG = -1e30
LOG2E = 1.4426950408889634
HALF = 4
WINDOW = 2 * HALF + 2
LIST = 6 + WINDOW


def nt(a, b):
    return lax.dot_general(a, b, (((1,), (1,)), ((), ())), preferred_element_type=jnp.float32)


def nn(a, b):
    return lax.dot_general(a, b, (((1,), (0,)), ((), ())), preferred_element_type=jnp.float32)


def table_kernel(blk, subs, ids_ref, len_ref, near_ref, far_ref, start_ref):
    chip, core, sub, mate, far = (ids_ref[i] for i in range(5))
    q0 = [((2 * chip + core) * subs + side) * blk for side in (sub, mate)]
    qpos = [q + lax.broadcasted_iota(jnp.int32, (1, blk), 1) for q in q0]
    zero = jnp.int32(0)
    begin, first, last = zero, [zero] * 2, [zero] * 2
    found = [jnp.zeros((1, blk), jnp.int32)] * 2
    for d in range(len_ref.shape[0]):
        for r in range(2):
            first[r] = jnp.where(begin <= q0[r], begin, first[r])
            last[r] = jnp.where(begin <= q0[r] + blk - 1, begin, last[r])
            found[r] = jnp.where(begin <= qpos[r], begin, found[r])
        begin = begin + len_ref[d]
    for r in range(2):
        start_ref[r] = found[r]
    for info_ref, share in ((near_ref, sub), (far_ref, far)):
        count2, count1 = zero, zero
        for j in range(WINDOW):
            if j == 2 * HALF:
                info_ref[2] = count2
                info_ref[3] = count1
            owner = core if j < HALF or j == 2 * HALF else 1 - core
            jj = j % HALF
            back = 0 if j >= 2 * HALF else 1 + 2 * owner if jj < 2 else 2 + 2 * owner
            parity = owner if j >= 2 * HALF or jj % 2 == 0 else 1 - owner
            kstart = ((2 * (chip - back) + parity) * subs + share) * blk
            kend = kstart + blk - 1
            active = [(kend >= first[r]) & (kstart <= q0[r] + blk - 1) for r in range(2)]
            whole = [(kstart >= last[r]) & (kend <= q0[r]) for r in range(2)]
            clear = active[0] & whole[0] & active[1] & whole[1]
            mixed = (active[0] | active[1]) & jnp.logical_not(clear)
            info_ref[6 + j] = kstart
            info_ref[LIST + count2] = j
            count2 = count2 + clear.astype(jnp.int32)
            info_ref[LIST + WINDOW + count1] = j
            count1 = count1 + mixed.astype(jnp.int32)
        info_ref[0] = count2
        info_ref[1] = count1
        info_ref[4] = q0[0]
        info_ref[5] = q0[1]


def tables(ids, doc_lengths, blk, subs):
    info = jax.ShapeDtypeStruct((LIST + 2 * WINDOW,), jnp.int32)
    return pl.pallas_call(
        functools.partial(table_kernel, blk, subs),
        out_shape=(info, info, jax.ShapeDtypeStruct((2, 1, blk), jnp.int32)),
        in_specs=[sm(), sm()],
        out_specs=(sm(), sm(), vm()),
        name="tile_tables",
    )(ids, doc_lengths)


def fill(window_ref, part_refs, pieces, blk):
    at = 0
    for part, begin, count in pieces:
        for i in range(count):
            for kind in range(2):
                window_ref[kind, at] = part_refs[part][kind, (begin + i) * blk:(begin + i + 1) * blk, :]
            at += 1


def fill_heads(dest_ref, sources, heads, hd):
    for r, source in enumerate(sources):
        for h in range(heads):
            dest_ref[r * heads + h] = source[:, h * hd:(h + 1) * hd]


def fill_scaled(dest_ref, sources, heads, hd, scale):
    for r, source in enumerate(sources):
        for h in range(heads):
            whole = source[:, h * hd:(h + 1) * hd].astype(jnp.float32) * scale
            high = whole.astype(jnp.bfloat16)
            dest_ref[r * heads + h, :, :hd] = high
            dest_ref[r * heads + h, :, hd:] = (whole - high.astype(jnp.float32)).astype(jnp.bfloat16)


def over_tiles(info_ref, start_ref, bias_ref, blk, span, tile, pairs):
    begin2 = info_ref[2] if span == "own" else 0
    begin1 = info_ref[3] if span == "own" else 0
    end2 = info_ref[2] if span == "half" else info_ref[0]
    end1 = info_ref[3] if span == "half" else info_ref[1]
    base = 2 * HALF if span == "own" else 0

    def two(i, _):
        at = LIST + begin2 + 2 * i
        pairs(info_ref[at] - base, info_ref[at + 1] - base)
        return 0

    def clear(i, _):
        tile(info_ref[LIST + i] - base, None)
        return 0

    def mixed(i, _):
        j = info_ref[LIST + WINDOW + i]
        kpos = info_ref[6 + j] + lax.broadcasted_iota(jnp.int32, (blk, blk), 0)
        for r in range(2):
            qpos = info_ref[4 + r] + lax.broadcasted_iota(jnp.int32, (1, blk), 1)
            bias_ref[r] = jnp.where((kpos <= qpos) & (kpos >= start_ref[r]), 0.0, BIG_NEG)
        tile(j - base, bias_ref)
        return 0

    half = 0
    if span != "own":
        half = lax.shift_right_logical(end2 - begin2, 1)
        lax.fori_loop(0, half, two, 0)
    lax.fori_loop(begin2 + 2 * half, end2, clear, 0)
    lax.fori_loop(begin1, end1, mixed, 0)


def forward_kernel(heads, hd, share, pieces, info_ref, start_ref, q0_ref, q1_ref, *rest):
    blk = q0_ref.shape[0]
    parts = 1 + max(piece[0] for piece in pieces)
    part_refs, rest = rest[:parts], rest[parts:]
    scale = LOG2E / math.sqrt(hd)
    if share == 0:
        m_ref, l_ref, a_ref, qs_ref, window_ref, bias_ref = rest
        m_ref[...] = jnp.full(m_ref.shape, BIG_NEG, jnp.float32)
        l_ref[...] = jnp.zeros(l_ref.shape, jnp.float32)
        a_ref[...] = jnp.zeros(a_ref.shape, jnp.float32)
    else:
        m_in, l_in, a_in, d0_ref, d1_ref, stat_ref, mine_ref, theirs_ref = rest[:8]
        qs_ref, window_ref, bias_ref, m_ref, l_ref, a_ref = rest[8:]
        m_ref[...] = m_in[...]
        l_ref[...] = l_in[...]
        a_ref[...] = a_in[...]
    fill(window_ref, part_refs, pieces, blk)
    fill_scaled(qs_ref, (q0_ref, q1_ref), heads, hd, scale)

    def update(kb, vb, masks):
        xs = range(2 * heads)
        vt = jnp.concatenate([vb.T, jnp.ones((16, vb.shape[0]), jnp.bfloat16)], axis=0)
        k2 = jnp.concatenate([kb, kb], axis=1)
        old = [(m_ref[x], l_ref[x], a_ref[x]) for x in xs]
        found = [nt(k2, qs_ref[x]) for x in xs]
        if masks is not None:
            found = [s + masks[x // heads] for x, s in zip(xs, found)]
        new = []
        for s, (m_old, l_old, a_old) in zip(found, old):
            m_new = jnp.maximum(m_old, jnp.max(s, axis=0, keepdims=True))
            p = jnp.exp2(s - m_new)
            f = jnp.exp2(m_old - m_new)
            both = nn(vt, p.astype(jnp.bfloat16))
            new.append((m_new, l_old * f + both[hd:hd + 1], a_old * f + both[:hd]))
        for x, (m_new, total, acc) in zip(xs, new):
            m_ref[x] = m_new
            l_ref[x] = total
            a_ref[x] = acc

    def tile(j, masks):
        update(window_ref[0, j], window_ref[1, j], masks)

    def pairs(j1, j2):
        kb, vb = [jnp.concatenate([window_ref[i, j1], window_ref[i, j2]], axis=0) for i in range(2)]
        update(kb, vb, None)

    over_tiles(info_ref, start_ref, bias_ref, blk, "all", tile, pairs)
    if share == 1:
        for r, d_ref in enumerate((d0_ref, d1_ref)):
            for h in range(heads):
                x = r * heads + h
                dt = d_ref[:, h * hd:(h + 1) * hd].astype(jnp.float32).T
                stat_ref[x, 0:1] = m_ref[x]
                stat_ref[x, 1:2] = l_ref[x]
                stat_ref[x, 2:3] = jnp.sum(dt * a_ref[x], axis=0, keepdims=True)
        mine_ref[...] = a_ref[:heads]
        theirs_ref[...] = a_ref[heads:].astype(jnp.bfloat16)


def vm():
    return pl.BlockSpec(memory_space=pltpu.VMEM)


def sm():
    return pl.BlockSpec(memory_space=pltpu.SMEM)


def params():
    return pltpu.CompilerParams(vmem_limit_bytes=24 << 20)


def forward(info, starts, q0, q1, parts, pieces, share, state=(), douts=()):
    blk, width = q0.shape
    hd = parts[0].shape[2]
    heads = width // hd
    n = 2 * heads
    f32 = jnp.float32
    row = jax.ShapeDtypeStruct((n, 1, blk), f32)
    work = [pltpu.VMEM((n, blk, 2 * hd), q0.dtype), pltpu.VMEM((2, WINDOW, blk, hd), q0.dtype),
            pltpu.VMEM((2, blk, blk), f32)]
    if share == 0:
        shapes = (row, row, jax.ShapeDtypeStruct((n, hd, blk), f32))
    else:
        shapes = (jax.ShapeDtypeStruct((n, 3, blk), f32), jax.ShapeDtypeStruct((heads, hd, blk), f32),
                  jax.ShapeDtypeStruct((heads, hd, blk), jnp.bfloat16))
        work += [pltpu.VMEM((n, 1, blk), f32), pltpu.VMEM((n, 1, blk), f32), pltpu.VMEM((n, hd, blk), f32)]
    args = (info, starts, q0, q1) + tuple(parts) + tuple(state) + tuple(douts)
    return pl.pallas_call(
        functools.partial(forward_kernel, heads, hd, share, pieces),
        out_shape=shapes,
        in_specs=[sm()] + [vm()] * (len(args) - 1),
        out_specs=(vm(),) * 3,
        scratch_shapes=work,
        compiler_params=params(),
        cost_estimate=pl.CostEstimate(flops=4 * WINDOW * n * blk * blk * hd, bytes_accessed=4 << 20, transcendentals=0),
        name="forward_part",
    )(*args)


def merge_stats(s_mine, s_theirs):
    m = jnp.maximum(s_mine[0:1], s_theirs[0:1])
    fa = jnp.exp2(s_mine[0:1] - m)
    fb = jnp.exp2(s_theirs[0:1] - m)
    total = s_mine[1:2] * fa + s_theirs[1:2] * fb
    delta = (s_mine[2:3] * fa + s_theirs[2:3] * fb) / total
    return m + jnp.log2(total), fa / total, fb / total, delta


def backward_kernel(heads, hd, span, pieces, info_ref, start_ref, q0_ref, q1_ref, d0_ref, d1_ref, sa_ref, sb_ref, *rest):
    blk = q0_ref.shape[0]
    scale = LOG2E / math.sqrt(hd)
    back = 1.0 / math.sqrt(hd)
    parts = 1 + max(piece[0] for piece in pieces)
    part_refs, rest = rest[:parts], rest[parts:]
    if span == "all":
        ga_ref, gb_ref, dq_ref = rest[:3]
        work = rest[3:]
        dq_ref[...] = jnp.zeros(dq_ref.shape, jnp.float32)
    elif span == "half":
        dq_in, ga_ref, gb_ref, dq_ref = rest[:4]
        work = rest[4:]
        dq_ref[...] = dq_in[...]
    else:
        dq_in, mine_ref, theirs_ref, ga_ref, gb_ref, att_ref, dq0_ref, dq1_ref = rest[:8]
        work = rest[8:-1]
        dq_ref = rest[-1]
        dq_ref[...] = dq_in[...]
    q_ref, d_ref, window_ref, grad_ref, log_ref, delta_ref, qs_ref, bias_ref = work
    grad_ref[...] = jnp.zeros(grad_ref.shape, jnp.float32)
    fill(window_ref, part_refs, pieces, blk)
    fill_heads(q_ref, (q0_ref, q1_ref), heads, hd)
    fill_heads(d_ref, (d0_ref, d1_ref), heads, hd)
    fill_scaled(qs_ref, (q0_ref, q1_ref), heads, hd, scale)
    for r in range(2):
        for h in range(heads):
            x = r * heads + h
            log_total, wa, wb, delta = merge_stats(sa_ref[x], sb_ref[(1 - r) * heads + h])
            log_ref[x] = log_total
            delta_ref[x] = delta
            if span == "own" and r == 0:
                att = mine_ref[h] * wa + theirs_ref[h].astype(jnp.float32) * wb
                att_ref[:, h * hd:(h + 1) * hd] = att.T.astype(jnp.bfloat16)

    def tile(j, masks):
        xs = range(2 * heads)
        kb = window_ref[0, j]
        vb = window_ref[1, j]
        kt = kb.T
        qs = [q_ref[x] for x in xs]
        ds = [d_ref[x] for x in xs]
        rows = [(log_ref[x], delta_ref[x]) for x in xs]
        sums = [dq_ref[x] for x in xs]
        dk, dv = grad_ref[0, j], grad_ref[1, j]
        k2 = jnp.concatenate([kb, kb], axis=1)
        found = [nt(k2, qs_ref[x]) for x in xs]
        pushed = [nt(vb, d) for d in ds]
        weights, slopes = [], []
        for x, s, dp, (log_total, delta) in zip(xs, found, pushed, rows):
            if masks is not None:
                s = s + masks[x // heads]
            p = jnp.exp2(s - log_total)
            weights.append(p.astype(jnp.bfloat16))
            slopes.append((p * (dp - delta)).astype(jnp.bfloat16))
        dv = dv + nn(jnp.concatenate(weights, axis=1), jnp.concatenate(ds, axis=0))
        dk = dk + nn(jnp.concatenate(slopes, axis=1), jnp.concatenate(qs, axis=0))
        sums = [dq + nn(kt, slope) for dq, slope in zip(sums, slopes)]
        for x, dq in zip(xs, sums):
            dq_ref[x] = dq
        grad_ref[0, j] = dk
        grad_ref[1, j] = dv

    def pairs(j1, j2):
        xs = range(2 * heads)
        kb = jnp.concatenate([window_ref[0, j1], window_ref[0, j2]], axis=0)
        vb = jnp.concatenate([window_ref[1, j1], window_ref[1, j2]], axis=0)
        kt = kb.T
        qs = [q_ref[x] for x in xs]
        ds = [d_ref[x] for x in xs]
        rows = [(log_ref[x], delta_ref[x]) for x in xs]
        sums = [dq_ref[x] for x in xs]
        k2 = jnp.concatenate([kb, kb], axis=1)
        found = [nt(k2, qs_ref[x]) for x in xs]
        pushed = [nt(vb, d) for d in ds]
        weights, slopes = [], []
        for x, s, dp, (log_total, delta) in zip(xs, found, pushed, rows):
            p = jnp.exp2(s - log_total)
            weights.append(p.astype(jnp.bfloat16))
            slopes.append((p * (dp - delta)).astype(jnp.bfloat16))
        dv = nn(jnp.concatenate(weights, axis=1), jnp.concatenate(ds, axis=0))
        dk = nn(jnp.concatenate(slopes, axis=1), jnp.concatenate(qs, axis=0))
        sums = [dq + nn(kt, slope) for dq, slope in zip(sums, slopes)]
        for x, dq in zip(xs, sums):
            dq_ref[x] = dq
        grad_ref[0, j1] = dk[:blk]
        grad_ref[0, j2] = dk[blk:]
        grad_ref[1, j1] = dv[:blk]
        grad_ref[1, j2] = dv[blk:]

    over_tiles(info_ref, start_ref, bias_ref, blk, span, tile, pairs)
    lists = {"all": ([0, 1, 2, 3, 8], [4, 5, 6, 7, 9]), "half": ([0, 1, 2, 3], [4, 5, 6, 7]), "own": ([0], [1])}
    for chunks, g_ref in zip(lists[span], (ga_ref, gb_ref)):
        for i, j in enumerate(chunks):
            rows = slice(i * blk, (i + 1) * blk)
            g_ref[0, rows, :] = (grad_ref[0, j] * back).astype(jnp.bfloat16)
            g_ref[1, rows, :] = grad_ref[1, j].astype(jnp.bfloat16)
    if span == "own":
        for h in range(heads):
            columns = slice(h * hd, (h + 1) * hd)
            dq0_ref[:, columns] = (dq_ref[h] * back).T
            dq1_ref[:, columns] = (dq_ref[heads + h] * back).T.astype(jnp.bfloat16)


def backward(info, starts, q0, q1, d0, d1, s_mine, s_theirs, parts, pieces, span, sums=()):
    blk, width = q0.shape
    hd = parts[0].shape[2]
    heads = width // hd
    n = 2 * heads
    f32 = jnp.float32
    count = {"all": WINDOW, "half": 2 * HALF, "own": 2}[span]
    grad = jax.ShapeDtypeStruct((2, count // 2 * blk, hd), jnp.bfloat16)
    two = pltpu.VMEM((n, blk, hd), q0.dtype)
    row = pltpu.VMEM((n, 1, blk), f32)
    work = [two, two, pltpu.VMEM((2, count, blk, hd), q0.dtype), pltpu.VMEM((2, count, blk, hd), f32), row, row,
            pltpu.VMEM((n, blk, 2 * hd), q0.dtype), pltpu.VMEM((2, blk, blk), f32)]
    if span == "own":
        out = jax.ShapeDtypeStruct((blk, width), jnp.bfloat16)
        shapes = (grad, grad, out, jax.ShapeDtypeStruct((blk, width), f32), out)
        work += [pltpu.VMEM((n, hd, blk), f32)]
    else:
        shapes = (grad, grad, jax.ShapeDtypeStruct((n, hd, blk), f32))
    args = (info, starts, q0, q1, d0, d1, s_mine, s_theirs) + tuple(parts) + tuple(sums)
    return pl.pallas_call(
        functools.partial(backward_kernel, heads, hd, span, pieces),
        out_shape=shapes,
        in_specs=[sm()] + [vm()] * (len(args) - 1),
        out_specs=(vm(),) * len(shapes),
        scratch_shapes=work,
        compiler_params=params(),
        cost_estimate=pl.CostEstimate(flops=10 * count * n * blk * blk * hd, bytes_accessed=4 << 20, transcendentals=0),
        name="backward_part",
    )(*args)


def per_device(queries, keys, values, dout, doc_lengths):
    blk = queries.shape[0]
    seqs, subs = lax.axis_size("seq"), lax.axis_size("sub")
    seq, sub = lax.axis_index("seq"), lax.axis_index("sub")
    f32, bf16 = jnp.float32, jnp.bfloat16
    chip, core = seq // 2, seq % 2
    mate = sub + 1 - 2 * (sub % 2)
    far = (sub + 2 * (sub % 2) - 1 + subs) % subs
    ids = jnp.stack([chip, core, sub, mate, far]).astype(jnp.int32)
    *infos, starts = tables(ids, doc_lengths, blk, subs)

    def swap_core(value):
        return lax.ppermute(value, "seq", [(s, s ^ 1) for s in range(seqs)])

    def swap_mate(value):
        return lax.ppermute(value, "sub", [(s, s ^ 1) for s in range(subs)])

    def swap_far(value):
        return lax.ppermute(value, "sub", [(s, (s + 2 * (s % 2) - 1) % subs) for s in range(subs)])

    def route(step, sign):
        pairs = [(s, s + 2 * (1 + step + 2 * (s % 2))) for s in range(seqs)]
        return [(a, b)[::sign] for a, b in pairs if b < seqs]

    tie = lax.optimization_barrier
    other_keys, other_values = swap_core(keys), swap_core(values)
    q_mate, d_mate = swap_mate(queries), swap_mate(dout)
    pair = tie(jnp.concatenate([jnp.stack([keys, values]), jnp.stack([other_keys, other_values])], axis=1))
    pair_far = swap_far(pair)
    near = lax.ppermute(pair, "seq", route(0, 1))
    away = lax.ppermute(pair, "seq", route(1, 1))
    near, infos, starts = tie((near, infos, starts))
    near_far = swap_far(near)
    away, q_mate, d_mate, pair_far, near_far = tie((away, q_mate, d_mate, pair_far, near_far))
    most = jnp.concatenate([near, away, near_far], axis=1)
    most_x = swap_core(most)
    away_far = swap_far(away)
    near_pieces = ((0, 0, HALF), (1, 0, HALF), (2, 0, 2))
    far_pieces = ((0, HALF, 2), (2, 0, 2), (1, HALF, 2), (3, 0, 2), (4, 0, 2))
    state = forward(infos[0], starts, queries, q_mate, (most, most_x, pair), near_pieces, 0)
    away_far, state = tie((away_far, state))
    away_far_x = swap_core(away_far)
    far_parts = (most, most_x, away_far, away_far_x, pair_far)
    stats, mine, theirs = forward(infos[1], starts, queries, q_mate, far_parts, far_pieces, 1, state, (dout, d_mate))
    common = (starts, queries, q_mate, dout, d_mate, stats, swap_mate(stats))
    grad_a, grad_b, dq = backward(infos[1], *common, far_parts, far_pieces, "all")
    grad_b, theirs = tie((grad_b, theirs))
    theirs = swap_mate(theirs)
    grad_a = (grad_a.astype(f32) + swap_core(grad_b).astype(f32)).astype(bf16)
    grad_a, dq = tie((grad_a, dq))
    grad_far = swap_far(grad_a)
    grad_a, grad_b, dq = backward(infos[0], *common, (most, most_x), near_pieces[:2], "half", (dq,))
    grad_b, grad_far, theirs = tie((grad_b, grad_far, theirs))
    home = (grad_a.astype(f32) + swap_core(grad_b).astype(f32) + grad_far[:, : HALF * blk].astype(f32)).astype(bf16)
    home, dq = tie((home, dq))
    near = lax.ppermute(home[:, : 2 * blk], "seq", route(0, -1))
    away = lax.ppermute(home[:, 2 * blk :], "seq", route(1, -1))
    grad_own, grad_other, attended, dq_mine, dq_mate = backward(
        infos[0], *common, (pair,), ((0, 0, 2),), "own", (dq, mine, theirs)
    )
    dq_back = swap_mate(dq_mate)
    near, away, grad_own, grad_other = tie((near, away, grad_own, grad_other))
    back = near.astype(f32) + away.astype(f32)
    other = swap_core((back[:, blk:] + grad_other.astype(f32)).astype(bf16))
    query_grad = (dq_mine + dq_back.astype(f32)).astype(bf16)
    total = [
        (grad_own[i].astype(f32) + grad_far[i, HALF * blk :].astype(f32) + back[i, :blk] + other[i].astype(f32)).astype(bf16)
        for i in range(2)
    ]
    return attended, query_grad, total[0], total[1]


def solution(mesh):
    rows = P(("seq", "sub"), None)
    return jax.shard_map(
        per_device,
        mesh=mesh,
        in_specs=(rows, rows, rows, rows, P()),
        out_specs=(rows, rows, rows, rows),
        check_vma=False,
    )
```

```python
import functools
import math

import jax
import jax.numpy as jnp
from jax import lax
from jax.experimental import pallas as pl
from jax.experimental.pallas import tpu as pltpu
from jax.sharding import PartitionSpec as P

BIG_NEG = -1e30
LOG2E = 1.4426950408889634
HALF = 4
WINDOW = 2 * HALF + 2
LIST = 6 + WINDOW


def nt(a, b):
    return lax.dot_general(a, b, (((1,), (1,)), ((), ())), preferred_element_type=jnp.float32)


def nn(a, b):
    return lax.dot_general(a, b, (((1,), (0,)), ((), ())), preferred_element_type=jnp.float32)


def table_kernel(blk, subs, ids_ref, len_ref, near_ref, far_ref, start_ref):
    chip, core, sub, mate, far = (ids_ref[i] for i in range(5))
    q0 = [((2 * chip + core) * subs + side) * blk for side in (sub, mate)]
    qpos = [q + lax.broadcasted_iota(jnp.int32, (1, blk), 1) for q in q0]
    zero = jnp.int32(0)
    begin, first, last = zero, [zero] * 2, [zero] * 2
    found = [jnp.zeros((1, blk), jnp.int32)] * 2
    for d in range(len_ref.shape[0]):
        for r in range(2):
            first[r] = jnp.where(begin <= q0[r], begin, first[r])
            last[r] = jnp.where(begin <= q0[r] + blk - 1, begin, last[r])
            found[r] = jnp.where(begin <= qpos[r], begin, found[r])
        begin = begin + len_ref[d]
    for r in range(2):
        start_ref[r] = found[r]
    for info_ref, share in ((near_ref, sub), (far_ref, far)):
        count2, count1 = zero, zero
        for j in range(WINDOW):
            if j == 2 * HALF:
                info_ref[2] = count2
                info_ref[3] = count1
            owner = core if j < HALF or j == 2 * HALF else 1 - core
            jj = j % HALF
            back = 0 if j >= 2 * HALF else 1 + 2 * owner if jj < 2 else 2 + 2 * owner
            parity = owner if j >= 2 * HALF or jj % 2 == 0 else 1 - owner
            kstart = ((2 * (chip - back) + parity) * subs + share) * blk
            kend = kstart + blk - 1
            active = [(kend >= first[r]) & (kstart <= q0[r] + blk - 1) for r in range(2)]
            whole = [(kstart >= last[r]) & (kend <= q0[r]) for r in range(2)]
            clear = active[0] & whole[0] & active[1] & whole[1]
            mixed = (active[0] | active[1]) & jnp.logical_not(clear)
            info_ref[6 + j] = kstart
            info_ref[LIST + count2] = j
            count2 = count2 + clear.astype(jnp.int32)
            info_ref[LIST + WINDOW + count1] = j
            count1 = count1 + mixed.astype(jnp.int32)
        info_ref[0] = count2
        info_ref[1] = count1
        info_ref[4] = q0[0]
        info_ref[5] = q0[1]


def tables(ids, doc_lengths, blk, subs):
    info = jax.ShapeDtypeStruct((LIST + 2 * WINDOW,), jnp.int32)
    return pl.pallas_call(
        functools.partial(table_kernel, blk, subs),
        out_shape=(info, info, jax.ShapeDtypeStruct((2, 1, blk), jnp.int32)),
        in_specs=[sm(), sm()],
        out_specs=(sm(), sm(), vm()),
        name="tile_tables",
    )(ids, doc_lengths)


def fill(window_ref, part_refs, pieces, blk):
    at = 0
    for part, begin, count in pieces:
        for i in range(count):
            for kind in range(2):
                window_ref[kind, at] = part_refs[part][kind, (begin + i) * blk:(begin + i + 1) * blk, :]
            at += 1


def fill_heads(dest_ref, sources, heads, hd):
    for r, source in enumerate(sources):
        for h in range(heads):
            dest_ref[r * heads + h] = source[:, h * hd:(h + 1) * hd]


def fill_scaled(dest_ref, sources, heads, hd, scale):
    for r, source in enumerate(sources):
        for h in range(heads):
            whole = source[:, h * hd:(h + 1) * hd].astype(jnp.float32) * scale
            high = whole.astype(jnp.bfloat16)
            dest_ref[r * heads + h, :, :hd] = high
            dest_ref[r * heads + h, :, hd:] = (whole - high.astype(jnp.float32)).astype(jnp.bfloat16)


def over_tiles(info_ref, start_ref, bias_ref, blk, span, tile, pairs):
    begin2 = info_ref[2] if span == "own" else 0
    begin1 = info_ref[3] if span == "own" else 0
    end2 = info_ref[2] if span == "half" else info_ref[0]
    end1 = info_ref[3] if span == "half" else info_ref[1]
    base = 2 * HALF if span == "own" else 0

    def two(i, _):
        at = LIST + begin2 + 2 * i
        pairs(info_ref[at] - base, info_ref[at + 1] - base)
        return 0

    def clear(i, _):
        tile(info_ref[LIST + i] - base, None)
        return 0

    def mixed(i, _):
        j = info_ref[LIST + WINDOW + i]
        kpos = info_ref[6 + j] + lax.broadcasted_iota(jnp.int32, (blk, blk), 0)
        for r in range(2):
            qpos = info_ref[4 + r] + lax.broadcasted_iota(jnp.int32, (1, blk), 1)
            bias_ref[r] = jnp.where((kpos <= qpos) & (kpos >= start_ref[r]), 0.0, BIG_NEG)
        tile(j - base, bias_ref)
        return 0

    half = 0
    if span != "own":
        half = lax.shift_right_logical(end2 - begin2, 1)
        lax.fori_loop(0, half, two, 0)
    lax.fori_loop(begin2 + 2 * half, end2, clear, 0)
    lax.fori_loop(begin1, end1, mixed, 0)


def forward_kernel(heads, hd, share, pieces, info_ref, start_ref, q0_ref, q1_ref, *rest):
    blk = q0_ref.shape[0]
    parts = 1 + max(piece[0] for piece in pieces)
    part_refs, rest = rest[:parts], rest[parts:]
    scale = LOG2E / math.sqrt(hd)
    if share == 0:
        m_ref, l_ref, a_ref, qs_ref, window_ref, bias_ref = rest
        m_ref[...] = jnp.full(m_ref.shape, BIG_NEG, jnp.float32)
        l_ref[...] = jnp.zeros(l_ref.shape, jnp.float32)
        a_ref[...] = jnp.zeros(a_ref.shape, jnp.float32)
    else:
        m_in, l_in, a_in, d0_ref, d1_ref, stat_ref, mine_ref, theirs_ref = rest[:8]
        qs_ref, window_ref, bias_ref, m_ref, l_ref, a_ref = rest[8:]
        m_ref[...] = m_in[...]
        l_ref[...] = l_in[...]
        a_ref[...] = a_in[...]
    fill(window_ref, part_refs, pieces, blk)
    fill_scaled(qs_ref, (q0_ref, q1_ref), heads, hd, scale)

    def update(kb, vb, masks):
        xs = range(2 * heads)
        vt = jnp.concatenate([vb.T, jnp.ones((16, vb.shape[0]), jnp.bfloat16)], axis=0)
        k2 = jnp.concatenate([kb, kb], axis=1)
        old = [(m_ref[x], l_ref[x], a_ref[x]) for x in xs]
        found = [nt(k2, qs_ref[x]) for x in xs]
        if masks is not None:
            found = [s + masks[x // heads] for x, s in zip(xs, found)]
        new = []
        for s, (m_old, l_old, a_old) in zip(found, old):
            m_new = jnp.maximum(m_old, jnp.max(s, axis=0, keepdims=True))
            p = jnp.exp2(s - m_new)
            f = jnp.exp2(m_old - m_new)
            both = nn(vt, p.astype(jnp.bfloat16))
            new.append((m_new, l_old * f + both[hd:hd + 1], a_old * f + both[:hd]))
        for x, (m_new, total, acc) in zip(xs, new):
            m_ref[x] = m_new
            l_ref[x] = total
            a_ref[x] = acc

    def tile(j, masks):
        update(window_ref[0, j], window_ref[1, j], masks)

    def pairs(j1, j2):
        kb, vb = [jnp.concatenate([window_ref[i, j1], window_ref[i, j2]], axis=0) for i in range(2)]
        update(kb, vb, None)

    over_tiles(info_ref, start_ref, bias_ref, blk, "all", tile, pairs)
    if share == 1:
        for r, d_ref in enumerate((d0_ref, d1_ref)):
            for h in range(heads):
                x = r * heads + h
                dt = d_ref[:, h * hd:(h + 1) * hd].astype(jnp.float32).T
                stat_ref[x, 0:1] = m_ref[x]
                stat_ref[x, 1:2] = l_ref[x]
                stat_ref[x, 2:3] = jnp.sum(dt * a_ref[x], axis=0, keepdims=True)
        mine_ref[...] = a_ref[:heads]
        theirs_ref[...] = a_ref[heads:].astype(jnp.bfloat16)


def vm():
    return pl.BlockSpec(memory_space=pltpu.VMEM)


def sm():
    return pl.BlockSpec(memory_space=pltpu.SMEM)


def params():
    return pltpu.CompilerParams(vmem_limit_bytes=24 << 20)


def forward(info, starts, q0, q1, parts, pieces, share, state=(), douts=()):
    blk, width = q0.shape
    hd = parts[0].shape[2]
    heads = width // hd
    n = 2 * heads
    f32 = jnp.float32
    row = jax.ShapeDtypeStruct((n, 1, blk), f32)
    work = [pltpu.VMEM((n, blk, 2 * hd), q0.dtype), pltpu.VMEM((2, WINDOW, blk, hd), q0.dtype),
            pltpu.VMEM((2, blk, blk), f32)]
    if share == 0:
        shapes = (row, row, jax.ShapeDtypeStruct((n, hd, blk), f32))
    else:
        shapes = (jax.ShapeDtypeStruct((n, 3, blk), f32), jax.ShapeDtypeStruct((heads, hd, blk), f32),
                  jax.ShapeDtypeStruct((heads, hd, blk), jnp.bfloat16))
        work += [pltpu.VMEM((n, 1, blk), f32), pltpu.VMEM((n, 1, blk), f32), pltpu.VMEM((n, hd, blk), f32)]
    args = (info, starts, q0, q1) + tuple(parts) + tuple(state) + tuple(douts)
    return pl.pallas_call(
        functools.partial(forward_kernel, heads, hd, share, pieces),
        out_shape=shapes,
        in_specs=[sm()] + [vm()] * (len(args) - 1),
        out_specs=(vm(),) * 3,
        scratch_shapes=work,
        compiler_params=params(),
        cost_estimate=pl.CostEstimate(flops=4 * WINDOW * n * blk * blk * hd, bytes_accessed=4 << 20, transcendentals=0),
        name="forward_part",
    )(*args)


def merge_stats(s_mine, s_theirs):
    m = jnp.maximum(s_mine[0:1], s_theirs[0:1])
    fa = jnp.exp2(s_mine[0:1] - m)
    fb = jnp.exp2(s_theirs[0:1] - m)
    total = s_mine[1:2] * fa + s_theirs[1:2] * fb
    delta = (s_mine[2:3] * fa + s_theirs[2:3] * fb) / total
    return m + jnp.log2(total), fa / total, fb / total, delta


def backward_kernel(heads, hd, span, pieces, info_ref, start_ref, q0_ref, q1_ref, d0_ref, d1_ref, sa_ref, sb_ref, *rest):
    blk = q0_ref.shape[0]
    scale = LOG2E / math.sqrt(hd)
    back = 1.0 / math.sqrt(hd)
    parts = 1 + max(piece[0] for piece in pieces)
    part_refs, rest = rest[:parts], rest[parts:]
    if span == "all":
        ga_ref, gb_ref, dq_ref = rest[:3]
        work = rest[3:]
        dq_ref[...] = jnp.zeros(dq_ref.shape, jnp.float32)
    elif span == "half":
        dq_in, ga_ref, gb_ref, dq_ref = rest[:4]
        work = rest[4:]
        dq_ref[...] = dq_in[...]
    else:
        dq_in, ga_ref, gb_ref, dq_out, send_ref = rest[:5]
        work = rest[5:-1]
        dq_ref = rest[-1]
        dq_ref[...] = dq_in[...]
    q_ref, d_ref, window_ref, grad_ref, log_ref, delta_ref, qs_ref, bias_ref = work
    grad_ref[...] = jnp.zeros(grad_ref.shape, jnp.float32)
    fill(window_ref, part_refs, pieces, blk)
    fill_heads(q_ref, (q0_ref, q1_ref), heads, hd)
    fill_heads(d_ref, (d0_ref, d1_ref), heads, hd)
    fill_scaled(qs_ref, (q0_ref, q1_ref), heads, hd, scale)
    for r in range(2):
        for h in range(heads):
            x = r * heads + h
            log_total, _, _, delta = merge_stats(sa_ref[x], sb_ref[(1 - r) * heads + h])
            log_ref[x] = log_total
            delta_ref[x] = delta

    def tile(j, masks):
        xs = range(2 * heads)
        kb = window_ref[0, j]
        vb = window_ref[1, j]
        kt = kb.T
        qs = [q_ref[x] for x in xs]
        ds = [d_ref[x] for x in xs]
        rows = [(log_ref[x], delta_ref[x]) for x in xs]
        sums = [dq_ref[x] for x in xs]
        dk, dv = grad_ref[0, j], grad_ref[1, j]
        k2 = jnp.concatenate([kb, kb], axis=1)
        found = [nt(k2, qs_ref[x]) for x in xs]
        pushed = [nt(vb, d) for d in ds]
        weights, slopes = [], []
        for x, s, dp, (log_total, delta) in zip(xs, found, pushed, rows):
            if masks is not None:
                s = s + masks[x // heads]
            p = jnp.exp2(s - log_total)
            weights.append(p.astype(jnp.bfloat16))
            slopes.append((p * (dp - delta)).astype(jnp.bfloat16))
        dv = dv + nn(jnp.concatenate(weights, axis=1), jnp.concatenate(ds, axis=0))
        dk = dk + nn(jnp.concatenate(slopes, axis=1), jnp.concatenate(qs, axis=0))
        sums = [dq + nn(kt, slope) for dq, slope in zip(sums, slopes)]
        for x, dq in zip(xs, sums):
            dq_ref[x] = dq
        grad_ref[0, j] = dk
        grad_ref[1, j] = dv

    def pairs(j1, j2):
        xs = range(2 * heads)
        kb = jnp.concatenate([window_ref[0, j1], window_ref[0, j2]], axis=0)
        vb = jnp.concatenate([window_ref[1, j1], window_ref[1, j2]], axis=0)
        kt = kb.T
        qs = [q_ref[x] for x in xs]
        ds = [d_ref[x] for x in xs]
        rows = [(log_ref[x], delta_ref[x]) for x in xs]
        sums = [dq_ref[x] for x in xs]
        k2 = jnp.concatenate([kb, kb], axis=1)
        found = [nt(k2, qs_ref[x]) for x in xs]
        pushed = [nt(vb, d) for d in ds]
        weights, slopes = [], []
        for x, s, dp, (log_total, delta) in zip(xs, found, pushed, rows):
            p = jnp.exp2(s - log_total)
            weights.append(p.astype(jnp.bfloat16))
            slopes.append((p * (dp - delta)).astype(jnp.bfloat16))
        dv = nn(jnp.concatenate(weights, axis=1), jnp.concatenate(ds, axis=0))
        dk = nn(jnp.concatenate(slopes, axis=1), jnp.concatenate(qs, axis=0))
        sums = [dq + nn(kt, slope) for dq, slope in zip(sums, slopes)]
        for x, dq in zip(xs, sums):
            dq_ref[x] = dq
        grad_ref[0, j1] = dk[:blk]
        grad_ref[0, j2] = dk[blk:]
        grad_ref[1, j1] = dv[:blk]
        grad_ref[1, j2] = dv[blk:]

    over_tiles(info_ref, start_ref, bias_ref, blk, span, tile, pairs)
    lists = {"all": ([0, 1, 2, 3, 8], [4, 5, 6, 7, 9]), "half": ([0, 1, 2, 3], [4, 5, 6, 7]), "own": ([0], [1])}
    for chunks, g_ref in zip(lists[span], (ga_ref, gb_ref)):
        for i, j in enumerate(chunks):
            rows = slice(i * blk, (i + 1) * blk)
            g_ref[0, rows, :] = (grad_ref[0, j] * back).astype(jnp.bfloat16)
            g_ref[1, rows, :] = grad_ref[1, j].astype(jnp.bfloat16)
    if span == "own":
        dq_out[...] = dq_ref[:heads]
        send_ref[...] = (dq_ref[heads:] * back).astype(jnp.bfloat16)


def backward(info, starts, q0, q1, d0, d1, s_mine, s_theirs, parts, pieces, span, sums=()):
    blk, width = q0.shape
    hd = parts[0].shape[2]
    heads = width // hd
    n = 2 * heads
    f32 = jnp.float32
    count = {"all": WINDOW, "half": 2 * HALF, "own": 2}[span]
    grad = jax.ShapeDtypeStruct((2, count // 2 * blk, hd), jnp.bfloat16)
    two = pltpu.VMEM((n, blk, hd), q0.dtype)
    row = pltpu.VMEM((n, 1, blk), f32)
    work = [two, two, pltpu.VMEM((2, count, blk, hd), q0.dtype), pltpu.VMEM((2, count, blk, hd), f32), row, row,
            pltpu.VMEM((n, blk, 2 * hd), q0.dtype), pltpu.VMEM((2, blk, blk), f32)]
    if span == "own":
        shapes = (grad, grad, jax.ShapeDtypeStruct((heads, hd, blk), f32),
                  jax.ShapeDtypeStruct((heads, hd, blk), jnp.bfloat16))
        work += [pltpu.VMEM((n, hd, blk), f32)]
    else:
        shapes = (grad, grad, jax.ShapeDtypeStruct((n, hd, blk), f32))
    args = (info, starts, q0, q1, d0, d1, s_mine, s_theirs) + tuple(parts) + tuple(sums)
    return pl.pallas_call(
        functools.partial(backward_kernel, heads, hd, span, pieces),
        out_shape=shapes,
        in_specs=[sm()] + [vm()] * (len(args) - 1),
        out_specs=(vm(),) * len(shapes),
        scratch_shapes=work,
        compiler_params=params(),
        cost_estimate=pl.CostEstimate(flops=10 * count * n * blk * blk * hd, bytes_accessed=4 << 20, transcendentals=0),
        name="backward_part",
    )(*args)


def output_kernel(heads, hd, sa_ref, sb_ref, mine_ref, theirs_ref, att_ref):
    for h in range(heads):
        _, wa, wb, _ = merge_stats(sa_ref[h], sb_ref[heads + h])
        att = mine_ref[h] * wa + theirs_ref[h].astype(jnp.float32) * wb
        att_ref[:, h * hd:(h + 1) * hd] = att.T.astype(jnp.bfloat16)


def query_grad_kernel(heads, hd, mine_ref, theirs_ref, out_ref):
    back = 1.0 / math.sqrt(hd)
    for h in range(heads):
        total = mine_ref[h] * back + theirs_ref[h].astype(jnp.float32)
        out_ref[:, h * hd:(h + 1) * hd] = total.T.astype(jnp.bfloat16)


def finish(kernel, name, *args):
    heads, hd, blk = args[-1].shape
    return pl.pallas_call(
        functools.partial(kernel, heads, hd),
        out_shape=jax.ShapeDtypeStruct((blk, heads * hd), jnp.bfloat16),
        in_specs=[vm()] * len(args),
        out_specs=vm(),
        name=name,
    )(*args)


def per_device(queries, keys, values, dout, doc_lengths):
    blk = queries.shape[0]
    seqs, subs = lax.axis_size("seq"), lax.axis_size("sub")
    seq, sub = lax.axis_index("seq"), lax.axis_index("sub")
    f32, bf16 = jnp.float32, jnp.bfloat16
    chip, core = seq // 2, seq % 2
    mate = sub + 1 - 2 * (sub % 2)
    far = (sub + 2 * (sub % 2) - 1 + subs) % subs
    def swap_core(value):
        return lax.ppermute(value, "seq", [(s, s ^ 1) for s in range(seqs)])

    def swap_mate(value):
        return lax.ppermute(value, "sub", [(s, s ^ 1) for s in range(subs)])

    def swap_far(value):
        return lax.ppermute(value, "sub", [(s, (s + 2 * (s % 2) - 1) % subs) for s in range(subs)])

    def route(step, sign):
        pairs = [(s, s + 2 * (1 + step + 2 * (s % 2))) for s in range(seqs)]
        return [(a, b)[::sign] for a, b in pairs if b < seqs]

    tie = lax.optimization_barrier
    other_keys, other_values = swap_core(keys), swap_core(values)
    ids = jnp.stack([chip, core, sub, mate, far]).astype(jnp.int32)
    pair = jnp.concatenate([jnp.stack([keys, values]), jnp.stack([other_keys, other_values])], axis=1)
    pair, ids = tie((pair, ids))
    near = lax.ppermute(pair, "seq", route(0, 1))
    away = lax.ppermute(pair, "seq", route(1, 1))
    *infos, starts = tables(ids, doc_lengths, blk, subs)
    q_send, d_send, pair_send, infos, starts = tie((queries, dout, pair, infos, starts))
    q_mate, d_mate = swap_mate(q_send), swap_mate(d_send)
    pair_far = swap_far(pair_send)
    near_far = swap_far(near)
    away, q_mate, d_mate, pair_far, near_far = tie((away, q_mate, d_mate, pair_far, near_far))
    most = jnp.concatenate([near, away, near_far], axis=1)
    most_x = swap_core(most)
    away_far = swap_far(away)
    near_pieces = ((0, 0, HALF), (1, 0, HALF), (2, 0, 2))
    far_pieces = ((0, HALF, 2), (2, 0, 2), (1, HALF, 2), (3, 0, 2), (4, 0, 2))
    state = forward(infos[0], starts, queries, q_mate, (most, most_x, pair), near_pieces, 0)
    away_far, state = tie((away_far, state))
    away_far_x = swap_core(away_far)
    far_parts = (most, most_x, away_far, away_far_x, pair_far)
    stats, mine, theirs = forward(infos[1], starts, queries, q_mate, far_parts, far_pieces, 1, state, (dout, d_mate))
    common = (starts, queries, q_mate, dout, d_mate, stats, swap_mate(stats))
    grad_a, grad_b, dq = backward(infos[1], *common, far_parts, far_pieces, "all")
    grad_b, theirs = tie((grad_b, theirs))
    theirs = swap_mate(theirs)
    grad_a = (grad_a.astype(f32) + swap_core(grad_b).astype(f32)).astype(bf16)
    grad_a, dq = tie((grad_a, dq))
    grad_far = swap_far(grad_a[:, : HALF * blk])
    far_own = grad_a[:, HALF * blk :]
    grad_a, grad_b, dq = backward(infos[0], *common, (most, most_x), near_pieces[:2], "half", (dq,))
    grad_b, grad_far, theirs = tie((grad_b, grad_far, theirs))
    home = (grad_a.astype(f32) + swap_core(grad_b).astype(f32) + grad_far.astype(f32)).astype(bf16)
    home, dq = tie((home, dq))
    near = lax.ppermute(home[:, : 2 * blk], "seq", route(0, -1))
    away = lax.ppermute(home[:, 2 * blk :], "seq", route(1, -1))
    grad_own, grad_other, dq, dq_send = backward(infos[0], *common, (pair,), ((0, 0, 2),), "own", (dq,))
    dq_send, far_own = tie((dq_send, far_own))
    dq_back = swap_mate(dq_send)
    grad_far_own = swap_far(far_own)
    near, away, grad_own, grad_other, theirs = tie((near, away, grad_own, grad_other, theirs))
    attended = finish(output_kernel, "output", stats, common[-1], mine, theirs)
    back = near.astype(f32) + away.astype(f32)
    other = swap_core((back[:, blk:] + grad_other.astype(f32)).astype(bf16))
    dq_back, attended = tie((dq_back, attended))
    query_grad = finish(query_grad_kernel, "query_grad", dq, dq_back)
    total = [
        (grad_own[i].astype(f32) + grad_far_own[i].astype(f32) + back[i, :blk] + other[i].astype(f32)).astype(bf16)
        for i in range(2)
    ]
    return attended, query_grad, total[0], total[1]


def solution(mesh):
    rows = P(("seq", "sub"), None)
    return jax.shard_map(
        per_device,
        mesh=mesh,
        in_specs=(rows, rows, rows, rows, P()),
        out_specs=(rows, rows, rows, rows),
        check_vma=False,
    )
```

```python
import functools
import math

import jax
import jax.numpy as jnp
from jax import lax
from jax.experimental import pallas as pl
from jax.experimental.pallas import tpu as pltpu
from jax.sharding import PartitionSpec as P

BIG_NEG = -1e30
LOG2E = 1.4426950408889634
HALF = 4
WINDOW = 2 * HALF + 2
LIST = 6 + WINDOW


def nt(a, b):
    return lax.dot_general(a, b, (((1,), (1,)), ((), ())), preferred_element_type=jnp.float32)


def nn(a, b):
    return lax.dot_general(a, b, (((1,), (0,)), ((), ())), preferred_element_type=jnp.float32)


def table_kernel(blk, subs, ids_ref, len_ref, near_ref, far_ref, start_ref):
    chip, core, sub, mate, far = (ids_ref[i] for i in range(5))
    q0 = [((2 * chip + core) * subs + side) * blk for side in (sub, mate)]
    qpos = [q + lax.broadcasted_iota(jnp.int32, (1, blk), 1) for q in q0]
    zero = jnp.int32(0)
    begin, first, last = zero, [zero] * 2, [zero] * 2
    found = [jnp.zeros((1, blk), jnp.int32)] * 2
    for d in range(len_ref.shape[0]):
        for r in range(2):
            first[r] = jnp.where(begin <= q0[r], begin, first[r])
            last[r] = jnp.where(begin <= q0[r] + blk - 1, begin, last[r])
            found[r] = jnp.where(begin <= qpos[r], begin, found[r])
        begin = begin + len_ref[d]
    for r in range(2):
        start_ref[r] = found[r]
    for info_ref, share in ((near_ref, sub), (far_ref, far)):
        count2, count1 = zero, zero
        for j in range(WINDOW):
            if j == 2 * HALF:
                info_ref[2] = count2
                info_ref[3] = count1
            owner = core if j < HALF or j == 2 * HALF else 1 - core
            jj = j % HALF
            back = 0 if j >= 2 * HALF else 1 + 2 * owner if jj < 2 else 2 + 2 * owner
            parity = owner if j >= 2 * HALF or jj % 2 == 0 else 1 - owner
            kstart = ((2 * (chip - back) + parity) * subs + share) * blk
            kend = kstart + blk - 1
            active = [(kend >= first[r]) & (kstart <= q0[r] + blk - 1) for r in range(2)]
            whole = [(kstart >= last[r]) & (kend <= q0[r]) for r in range(2)]
            clear = active[0] & whole[0] & active[1] & whole[1]
            mixed = (active[0] | active[1]) & jnp.logical_not(clear)
            info_ref[6 + j] = kstart
            info_ref[LIST + count2] = j
            count2 = count2 + clear.astype(jnp.int32)
            info_ref[LIST + WINDOW + count1] = j
            count1 = count1 + mixed.astype(jnp.int32)
        info_ref[0] = count2
        info_ref[1] = count1
        info_ref[4] = q0[0]
        info_ref[5] = q0[1]


def tables(ids, doc_lengths, blk, subs):
    info = jax.ShapeDtypeStruct((LIST + 2 * WINDOW,), jnp.int32)
    return pl.pallas_call(
        functools.partial(table_kernel, blk, subs),
        out_shape=(info, info, jax.ShapeDtypeStruct((2, 1, blk), jnp.int32)),
        in_specs=[sm(), sm()],
        out_specs=(sm(), sm(), vm()),
        name="tile_tables",
    )(ids, doc_lengths)


def fill(window_ref, part_refs, pieces, blk):
    at = 0
    for part, begin, count in pieces:
        for i in range(count):
            for kind in range(2):
                window_ref[kind, at] = part_refs[part][kind, (begin + i) * blk:(begin + i + 1) * blk, :]
            at += 1


def fill_heads(dest_ref, sources, heads, hd):
    for r, source in enumerate(sources):
        for h in range(heads):
            dest_ref[r * heads + h] = source[:, h * hd:(h + 1) * hd]


def fill_scaled(dest_ref, sources, heads, hd, scale):
    for r, source in enumerate(sources):
        for h in range(heads):
            whole = source[:, h * hd:(h + 1) * hd].astype(jnp.float32) * scale
            high = whole.astype(jnp.bfloat16)
            dest_ref[r * heads + h, :, :hd] = high
            dest_ref[r * heads + h, :, hd:] = (whole - high.astype(jnp.float32)).astype(jnp.bfloat16)


def over_tiles(info_ref, start_ref, bias_ref, blk, span, tile, pairs):
    end2 = info_ref[2] if span == "half" else info_ref[0]
    end1 = info_ref[3] if span == "half" else info_ref[1]

    def two(i, _):
        pairs(info_ref[LIST + 2 * i], info_ref[LIST + 2 * i + 1])
        return 0

    def clear(i, _):
        tile(info_ref[LIST + i], None)
        return 0

    def mixed(i, _):
        j = info_ref[LIST + WINDOW + i]
        kpos = info_ref[6 + j] + lax.broadcasted_iota(jnp.int32, (blk, blk), 0)
        for r in range(2):
            qpos = info_ref[4 + r] + lax.broadcasted_iota(jnp.int32, (1, blk), 1)
            bias_ref[r] = jnp.where((kpos <= qpos) & (kpos >= start_ref[r]), 0.0, BIG_NEG)
        tile(j, bias_ref)
        return 0

    half = lax.shift_right_logical(end2, 1)
    lax.fori_loop(0, half, two, 0)
    lax.fori_loop(2 * half, end2, clear, 0)
    lax.fori_loop(0, end1, mixed, 0)


def over_own(info_ref, start_ref, bias_ref, blk, r, base, tile):
    def one(i, _):
        j = info_ref[i]
        kpos = info_ref[6 + j] + lax.broadcasted_iota(jnp.int32, (blk, blk), 0)
        qpos = info_ref[4 + r] + lax.broadcasted_iota(jnp.int32, (1, blk), 1)
        bias_ref[r] = jnp.where((kpos <= qpos) & (kpos >= start_ref[r]), 0.0, BIG_NEG)
        tile(j - base, bias_ref)
        return 0

    lax.fori_loop(LIST + info_ref[2], LIST + info_ref[0], one, 0)
    lax.fori_loop(LIST + WINDOW + info_ref[3], LIST + WINDOW + info_ref[1], one, 0)


def forward_kernel(heads, hd, share, pieces, info_ref, start_ref, q0_ref, q1_ref, *rest):
    blk = q0_ref.shape[0]
    parts = 1 + max(piece[0] for piece in pieces)
    part_refs, rest = rest[:parts], rest[parts:]
    scale = LOG2E / math.sqrt(hd)
    if share == 0:
        m_ref, l_ref, a_ref, qs_ref, window_ref, bias_ref = rest
        m_ref[...] = jnp.full(m_ref.shape, BIG_NEG, jnp.float32)
        l_ref[...] = jnp.zeros(l_ref.shape, jnp.float32)
        a_ref[...] = jnp.zeros(a_ref.shape, jnp.float32)
    else:
        m_in, l_in, a_in, d0_ref, d1_ref, stat_ref, mine_ref, theirs_ref = rest[:8]
        qs_ref, window_ref, bias_ref, m_ref, l_ref, a_ref = rest[8:]
        m_ref[...] = m_in[...]
        l_ref[...] = l_in[...]
        a_ref[...] = a_in[...]
    fill(window_ref, part_refs, pieces, blk)
    fill_scaled(qs_ref, (q0_ref, q1_ref), heads, hd, scale)

    def update(kb, vb, masks):
        xs = range(2 * heads)
        vt = jnp.concatenate([vb.T, jnp.ones((16, vb.shape[0]), jnp.bfloat16)], axis=0)
        k2 = jnp.concatenate([kb, kb], axis=1)
        old = [(m_ref[x], l_ref[x], a_ref[x]) for x in xs]
        found = [nt(k2, qs_ref[x]) for x in xs]
        if masks is not None:
            found = [s + masks[x // heads] for x, s in zip(xs, found)]
        new = []
        for s, (m_old, l_old, a_old) in zip(found, old):
            m_new = jnp.maximum(m_old, jnp.max(s, axis=0, keepdims=True))
            p = jnp.exp2(s - m_new)
            f = jnp.exp2(m_old - m_new)
            both = nn(vt, p.astype(jnp.bfloat16))
            new.append((m_new, l_old * f + both[hd:hd + 1], a_old * f + both[:hd]))
        for x, (m_new, total, acc) in zip(xs, new):
            m_ref[x] = m_new
            l_ref[x] = total
            a_ref[x] = acc

    def tile(j, masks):
        update(window_ref[0, j], window_ref[1, j], masks)

    def pairs(j1, j2):
        kb, vb = [jnp.concatenate([window_ref[i, j1], window_ref[i, j2]], axis=0) for i in range(2)]
        update(kb, vb, None)

    over_tiles(info_ref, start_ref, bias_ref, blk, "all", tile, pairs)
    if share == 1:
        for r, d_ref in enumerate((d0_ref, d1_ref)):
            for h in range(heads):
                x = r * heads + h
                dt = d_ref[:, h * hd:(h + 1) * hd].astype(jnp.float32).T
                stat_ref[x, 0:1] = m_ref[x]
                stat_ref[x, 1:2] = l_ref[x]
                stat_ref[x, 2:3] = jnp.sum(dt * a_ref[x], axis=0, keepdims=True)
        mine_ref[...] = a_ref[:heads]
        theirs_ref[...] = a_ref[heads:].astype(jnp.bfloat16)


def vm():
    return pl.BlockSpec(memory_space=pltpu.VMEM)


def sm():
    return pl.BlockSpec(memory_space=pltpu.SMEM)


def params():
    return pltpu.CompilerParams(vmem_limit_bytes=24 << 20)


def forward(info, starts, q0, q1, parts, pieces, share, state=(), douts=()):
    blk, width = q0.shape
    hd = parts[0].shape[2]
    heads = width // hd
    n = 2 * heads
    f32 = jnp.float32
    row = jax.ShapeDtypeStruct((n, 1, blk), f32)
    work = [pltpu.VMEM((n, blk, 2 * hd), q0.dtype), pltpu.VMEM((2, WINDOW, blk, hd), q0.dtype),
            pltpu.VMEM((2, blk, blk), f32)]
    if share == 0:
        shapes = (row, row, jax.ShapeDtypeStruct((n, hd, blk), f32))
    else:
        shapes = (jax.ShapeDtypeStruct((n, 3, blk), f32), jax.ShapeDtypeStruct((heads, hd, blk), f32),
                  jax.ShapeDtypeStruct((heads, hd, blk), jnp.bfloat16))
        work += [pltpu.VMEM((n, 1, blk), f32), pltpu.VMEM((n, 1, blk), f32), pltpu.VMEM((n, hd, blk), f32)]
    args = (info, starts, q0, q1) + tuple(parts) + tuple(state) + tuple(douts)
    return pl.pallas_call(
        functools.partial(forward_kernel, heads, hd, share, pieces),
        out_shape=shapes,
        in_specs=[sm()] + [vm()] * (len(args) - 1),
        out_specs=(vm(),) * 3,
        scratch_shapes=work,
        compiler_params=params(),
        cost_estimate=pl.CostEstimate(flops=4 * WINDOW * n * blk * blk * hd, bytes_accessed=4 << 20, transcendentals=0),
        name="forward_part",
    )(*args)


def merge_stats(s_mine, s_theirs):
    m = jnp.maximum(s_mine[0:1], s_theirs[0:1])
    fa = jnp.exp2(s_mine[0:1] - m)
    fb = jnp.exp2(s_theirs[0:1] - m)
    total = s_mine[1:2] * fa + s_theirs[1:2] * fb
    delta = (s_mine[2:3] * fa + s_theirs[2:3] * fb) / total
    return m + jnp.log2(total), fa / total, fb / total, delta


def backward_kernel(heads, hd, span, pieces, info_ref, start_ref, q0_ref, q1_ref, d0_ref, d1_ref, sa_ref, sb_ref, *rest):
    blk = q0_ref.shape[0]
    scale = LOG2E / math.sqrt(hd)
    back = 1.0 / math.sqrt(hd)
    parts = 1 + max(piece[0] for piece in pieces)
    part_refs, rest = rest[:parts], rest[parts:]
    if span == "all":
        ga_ref, gb_ref, dq_ref = rest[:3]
        work = rest[3:]
        dq_ref[...] = jnp.zeros(dq_ref.shape, jnp.float32)
    elif span == "half":
        dq_in, ga_ref, gb_ref, own_ref, dq_out, send_ref = rest[:6]
        work = rest[6:-1]
        dq_ref = rest[-1]
        dq_ref[...] = dq_in[...]
    else:
        dq_in, own_ref, mine_ref, theirs_ref, ga_ref, gb_ref, att_ref, dq0_ref = rest[:8]
        work = rest[8:-1]
        dq_ref = rest[-1]
        dq_ref[...] = dq_in[...]
    q_ref, d_ref, window_ref, grad_ref, log_ref, delta_ref, qs_ref, bias_ref = work
    if span == "own":
        grad_ref[...] = own_ref[...]
    else:
        grad_ref[...] = jnp.zeros(grad_ref.shape, jnp.float32)
    fill(window_ref, part_refs, pieces, blk)
    fill_heads(q_ref, (q0_ref, q1_ref), heads, hd)
    fill_heads(d_ref, (d0_ref, d1_ref), heads, hd)
    fill_scaled(qs_ref, (q0_ref, q1_ref), heads, hd, scale)
    for r in range(1 if span == "own" else 2):
        for h in range(heads):
            x = r * heads + h
            log_total, wa, wb, delta = merge_stats(sa_ref[x], sb_ref[(1 - r) * heads + h])
            log_ref[x] = log_total
            delta_ref[x] = delta
            if span == "own" and r == 0:
                att = mine_ref[h] * wa + theirs_ref[h].astype(jnp.float32) * wb
                att_ref[:, h * hd:(h + 1) * hd] = att.T.astype(jnp.bfloat16)

    def tile(j, masks, xs=range(2 * heads)):
        kb = window_ref[0, j]
        vb = window_ref[1, j]
        kt = kb.T
        qs = [q_ref[x] for x in xs]
        ds = [d_ref[x] for x in xs]
        rows = [(log_ref[x], delta_ref[x]) for x in xs]
        sums = [dq_ref[x] for x in xs]
        dk, dv = grad_ref[0, j], grad_ref[1, j]
        k2 = jnp.concatenate([kb, kb], axis=1)
        found = [nt(k2, qs_ref[x]) for x in xs]
        pushed = [nt(vb, d) for d in ds]
        weights, slopes = [], []
        for x, s, dp, (log_total, delta) in zip(xs, found, pushed, rows):
            if masks is not None:
                s = s + masks[x // heads]
            p = jnp.exp2(s - log_total)
            weights.append(p.astype(jnp.bfloat16))
            slopes.append((p * (dp - delta)).astype(jnp.bfloat16))
        dv = dv + nn(jnp.concatenate(weights, axis=1), jnp.concatenate(ds, axis=0))
        dk = dk + nn(jnp.concatenate(slopes, axis=1), jnp.concatenate(qs, axis=0))
        sums = [dq + nn(kt, slope) for dq, slope in zip(sums, slopes)]
        for x, dq in zip(xs, sums):
            dq_ref[x] = dq
        grad_ref[0, j] = dk
        grad_ref[1, j] = dv

    def pairs(j1, j2):
        xs = range(2 * heads)
        kb = jnp.concatenate([window_ref[0, j1], window_ref[0, j2]], axis=0)
        vb = jnp.concatenate([window_ref[1, j1], window_ref[1, j2]], axis=0)
        kt = kb.T
        qs = [q_ref[x] for x in xs]
        ds = [d_ref[x] for x in xs]
        rows = [(log_ref[x], delta_ref[x]) for x in xs]
        sums = [dq_ref[x] for x in xs]
        k2 = jnp.concatenate([kb, kb], axis=1)
        found = [nt(k2, qs_ref[x]) for x in xs]
        pushed = [nt(vb, d) for d in ds]
        weights, slopes = [], []
        for x, s, dp, (log_total, delta) in zip(xs, found, pushed, rows):
            p = jnp.exp2(s - log_total)
            weights.append(p.astype(jnp.bfloat16))
            slopes.append((p * (dp - delta)).astype(jnp.bfloat16))
        dv = nn(jnp.concatenate(weights, axis=1), jnp.concatenate(ds, axis=0))
        dk = nn(jnp.concatenate(slopes, axis=1), jnp.concatenate(qs, axis=0))
        sums = [dq + nn(kt, slope) for dq, slope in zip(sums, slopes)]
        for x, dq in zip(xs, sums):
            dq_ref[x] = dq
        grad_ref[0, j1] = dk[:blk]
        grad_ref[0, j2] = dk[blk:]
        grad_ref[1, j1] = dv[:blk]
        grad_ref[1, j2] = dv[blk:]

    if span != "own":
        over_tiles(info_ref, start_ref, bias_ref, blk, span, tile, pairs)
    if span != "all":
        r = 1 if span == "half" else 0
        over_own(info_ref, start_ref, bias_ref, blk, r, 0 if span == "half" else 2 * HALF,
                 functools.partial(tile, xs=range(r * heads, (r + 1) * heads)))
    lists = {"all": ([0, 1, 2, 3, 8], [4, 5, 6, 7, 9]), "half": ([0, 1, 2, 3], [4, 5, 6, 7]), "own": ([0], [1])}
    for chunks, g_ref in zip(lists[span], (ga_ref, gb_ref)):
        for i, j in enumerate(chunks):
            rows = slice(i * blk, (i + 1) * blk)
            g_ref[0, rows, :] = (grad_ref[0, j] * back).astype(jnp.bfloat16)
            g_ref[1, rows, :] = grad_ref[1, j].astype(jnp.bfloat16)
    if span == "half":
        own_ref[...] = grad_ref[:, 2 * HALF:]
        dq_out[...] = dq_ref[:heads]
        for h in range(heads):
            send_ref[:, h * hd:(h + 1) * hd] = (dq_ref[heads + h] * back).T.astype(jnp.bfloat16)
    if span == "own":
        for h in range(heads):
            dq0_ref[:, h * hd:(h + 1) * hd] = (dq_ref[h] * back).T


def backward(info, starts, q0, q1, d0, d1, s_mine, s_theirs, parts, pieces, span, sums=()):
    blk, width = q0.shape
    hd = parts[0].shape[2]
    heads = width // hd
    n = 2 * heads
    f32 = jnp.float32
    count = 2 if span == "own" else WINDOW
    sent = {"all": WINDOW // 2, "half": HALF, "own": 1}[span]
    grad = jax.ShapeDtypeStruct((2, sent * blk, hd), jnp.bfloat16)
    two = pltpu.VMEM((n, blk, hd), q0.dtype)
    row = pltpu.VMEM((n, 1, blk), f32)
    work = [two, two, pltpu.VMEM((2, count, blk, hd), q0.dtype), pltpu.VMEM((2, count, blk, hd), f32), row, row,
            pltpu.VMEM((n, blk, 2 * hd), q0.dtype), pltpu.VMEM((2, blk, blk), f32)]
    out = jax.ShapeDtypeStruct((blk, width), jnp.bfloat16)
    if span == "all":
        shapes = (grad, grad, jax.ShapeDtypeStruct((n, hd, blk), f32))
    elif span == "half":
        shapes = (grad, grad, jax.ShapeDtypeStruct((2, 2, blk, hd), f32),
                  jax.ShapeDtypeStruct((heads, hd, blk), f32), out)
        work += [pltpu.VMEM((n, hd, blk), f32)]
    else:
        shapes = (grad, grad, out, jax.ShapeDtypeStruct((blk, width), f32))
        work += [pltpu.VMEM((heads, hd, blk), f32)]
    args = (info, starts, q0, q1, d0, d1, s_mine, s_theirs) + tuple(parts) + tuple(sums)
    return pl.pallas_call(
        functools.partial(backward_kernel, heads, hd, span, pieces),
        out_shape=shapes,
        in_specs=[sm()] + [vm()] * (len(args) - 1),
        out_specs=(vm(),) * len(shapes),
        scratch_shapes=work,
        compiler_params=params(),
        cost_estimate=pl.CostEstimate(flops=10 * count * n * blk * blk * hd, bytes_accessed=4 << 20, transcendentals=0),
        name="backward_part",
    )(*args)


def per_device(queries, keys, values, dout, doc_lengths):
    blk = queries.shape[0]
    seqs, subs = lax.axis_size("seq"), lax.axis_size("sub")
    seq, sub = lax.axis_index("seq"), lax.axis_index("sub")
    f32, bf16 = jnp.float32, jnp.bfloat16
    chip, core = seq // 2, seq % 2
    mate = sub + 1 - 2 * (sub % 2)
    far = (sub + 2 * (sub % 2) - 1 + subs) % subs
    def swap_core(value):
        return lax.ppermute(value, "seq", [(s, s ^ 1) for s in range(seqs)])

    def swap_mate(value):
        return lax.ppermute(value, "sub", [(s, s ^ 1) for s in range(subs)])

    def swap_far(value):
        return lax.ppermute(value, "sub", [(s, (s + 2 * (s % 2) - 1) % subs) for s in range(subs)])

    def route(step, sign):
        pairs = [(s, s + 2 * (1 + step + 2 * (s % 2))) for s in range(seqs)]
        return [(a, b)[::sign] for a, b in pairs if b < seqs]

    tie = lax.optimization_barrier
    other_keys, other_values = swap_core(keys), swap_core(values)
    q_mate = swap_mate(queries)
    ids = jnp.stack([chip, core, sub, mate, far]).astype(jnp.int32)
    pair = jnp.concatenate([jnp.stack([keys, values]), jnp.stack([other_keys, other_values])], axis=1)
    pair, ids = tie((pair, ids))
    near = lax.ppermute(pair, "seq", route(0, 1))
    away = lax.ppermute(pair, "seq", route(1, 1))
    *infos, starts = tables(ids, doc_lengths, blk, subs)
    near, infos, starts = tie((near, infos, starts))
    near_far = swap_far(near)
    away, q_mate, near_far, d_send = tie((away, q_mate, near_far, dout))
    d_mate = swap_mate(d_send)
    most = jnp.concatenate([near, away, near_far], axis=1)
    most_x = swap_core(most)
    away_far = swap_far(jnp.concatenate([away, pair], axis=1))
    near_pieces = ((0, 0, HALF), (1, 0, HALF), (2, 0, 2))
    far_pieces = ((0, HALF, 2), (2, 0, 2), (1, HALF, 2), (3, 0, 2), (2, 2, 2))
    state = forward(infos[0], starts, queries, q_mate, (most, most_x, pair), near_pieces, 0)
    away_far, state, d_mate = tie((away_far, state, d_mate))
    away_far_x = swap_core(away_far[:, : 2 * blk])
    far_parts = (most, most_x, away_far, away_far_x)
    stats, mine, theirs = forward(infos[1], starts, queries, q_mate, far_parts, far_pieces, 1, state, (dout, d_mate))
    common = (starts, queries, q_mate, dout, d_mate, stats, swap_mate(stats))
    grad_a, grad_b, dq = backward(infos[1], *common, far_parts, far_pieces, "all")
    grad_b, theirs = tie((grad_b, theirs))
    theirs = swap_mate(theirs)
    grad_a = (grad_a.astype(f32) + swap_core(grad_b).astype(f32)).astype(bf16)
    grad_a, dq = tie((grad_a, dq))
    grad_far = swap_far(grad_a[:, : HALF * blk])
    near_parts = (most, most_x, pair)
    far_own = grad_a[:, HALF * blk :]
    grad_a, grad_b, own, dq, dq_send = backward(infos[0], *common, near_parts, near_pieces, "half", (dq,))
    grad_b, grad_far, theirs = tie((grad_b, grad_far, theirs))
    home = (grad_a.astype(f32) + swap_core(grad_b).astype(f32) + grad_far.astype(f32)).astype(bf16)
    home, dq, dq_send = tie((home, dq, dq_send))
    near = lax.ppermute(home[:, : 2 * blk], "seq", route(0, -1))
    away = lax.ppermute(home[:, 2 * blk :], "seq", route(1, -1))
    dq_back = swap_mate(dq_send)
    grad_own, grad_other, attended, dq_mine = backward(
        infos[0], *common, (pair,), ((0, 0, 2),), "own", (dq, own, mine, theirs)
    )
    grad_own, far_own = tie((grad_own, far_own))
    grad_far_own = swap_far(far_own)
    near, away, dq_back, grad_own, grad_other = tie((near, away, dq_back, grad_own, grad_other))
    back = near.astype(f32) + away.astype(f32)
    other = swap_core((back[:, blk:] + grad_other.astype(f32)).astype(bf16))
    query_grad = (dq_mine + dq_back.astype(f32)).astype(bf16)
    total = [
        (grad_own[i].astype(f32) + grad_far_own[i].astype(f32) + back[i, :blk] + other[i].astype(f32)).astype(bf16)
        for i in range(2)
    ]
    return attended, query_grad, total[0], total[1]


def solution(mesh):
    rows = P(("seq", "sub"), None)
    return jax.shard_map(
        per_device,
        mesh=mesh,
        in_specs=(rows, rows, rows, rows, P()),
        out_specs=(rows, rows, rows, rows),
        check_vma=False,
    )
```

```python
import functools
import math

import jax
import jax.numpy as jnp
from jax import lax
from jax.experimental import pallas as pl
from jax.experimental.pallas import tpu as pltpu
from jax.sharding import PartitionSpec as P

BIG_NEG = -1e30
LOG2E = 1.4426950408889634
HALF = 4
WINDOW = 2 * HALF + 2
LIST = 6 + WINDOW


def nt(a, b):
    return lax.dot_general(a, b, (((1,), (1,)), ((), ())), preferred_element_type=jnp.float32)


def nn(a, b):
    return lax.dot_general(a, b, (((1,), (0,)), ((), ())), preferred_element_type=jnp.float32)


def table_kernel(blk, subs, ids_ref, len_ref, near_ref, far_ref, start_ref):
    chip, core, sub, mate, far = (ids_ref[i] for i in range(5))
    q0 = [((2 * chip + core) * subs + side) * blk for side in (sub, mate)]
    qpos = [q + lax.broadcasted_iota(jnp.int32, (1, blk), 1) for q in q0]
    zero = jnp.int32(0)
    begin, first, last = zero, [zero] * 2, [zero] * 2
    found = [jnp.zeros((1, blk), jnp.int32)] * 2
    for d in range(len_ref.shape[0]):
        for r in range(2):
            first[r] = jnp.where(begin <= q0[r], begin, first[r])
            last[r] = jnp.where(begin <= q0[r] + blk - 1, begin, last[r])
            found[r] = jnp.where(begin <= qpos[r], begin, found[r])
        begin = begin + len_ref[d]
    for r in range(2):
        start_ref[r] = found[r]
    for info_ref, share in ((near_ref, sub), (far_ref, far)):
        count2, count1 = zero, zero
        for j in range(WINDOW):
            if j == 2 * HALF:
                info_ref[2] = count2
                info_ref[3] = count1
            owner = core if j < HALF or j == 2 * HALF else 1 - core
            jj = j % HALF
            back = 0 if j >= 2 * HALF else 1 + 2 * owner if jj < 2 else 2 + 2 * owner
            parity = owner if j >= 2 * HALF or jj % 2 == 0 else 1 - owner
            kstart = ((2 * (chip - back) + parity) * subs + share) * blk
            kend = kstart + blk - 1
            active = [(kend >= first[r]) & (kstart <= q0[r] + blk - 1) for r in range(2)]
            whole = [(kstart >= last[r]) & (kend <= q0[r]) for r in range(2)]
            clear = active[0] & whole[0] & active[1] & whole[1]
            mixed = (active[0] | active[1]) & jnp.logical_not(clear)
            info_ref[6 + j] = kstart
            info_ref[LIST + count2] = j
            count2 = count2 + clear.astype(jnp.int32)
            info_ref[LIST + WINDOW + count1] = j
            count1 = count1 + mixed.astype(jnp.int32)
        info_ref[0] = count2
        info_ref[1] = count1
        info_ref[4] = q0[0]
        info_ref[5] = q0[1]


def tables(ids, doc_lengths, blk, subs):
    info = jax.ShapeDtypeStruct((LIST + 2 * WINDOW,), jnp.int32)
    return pl.pallas_call(
        functools.partial(table_kernel, blk, subs),
        out_shape=(info, info, jax.ShapeDtypeStruct((2, 1, blk), jnp.int32)),
        in_specs=[sm(), sm()],
        out_specs=(sm(), sm(), vm()),
        name="tile_tables",
    )(ids, doc_lengths)


def fill(window_ref, part_refs, pieces, blk):
    at = 0
    for part, begin, count in pieces:
        for i in range(count):
            for kind in range(2):
                window_ref[kind, at] = part_refs[part][kind, (begin + i) * blk:(begin + i + 1) * blk, :]
            at += 1


def fill_heads(dest_ref, sources, heads, hd):
    for r, source in enumerate(sources):
        for h in range(heads):
            dest_ref[r * heads + h] = source[:, h * hd:(h + 1) * hd]


def fill_scaled(dest_ref, sources, heads, hd, scale):
    for r, source in enumerate(sources):
        for h in range(heads):
            whole = source[:, h * hd:(h + 1) * hd].astype(jnp.float32) * scale
            high = whole.astype(jnp.bfloat16)
            dest_ref[r * heads + h, :, :hd] = high
            dest_ref[r * heads + h, :, hd:] = (whole - high.astype(jnp.float32)).astype(jnp.bfloat16)


def over_tiles(info_ref, start_ref, bias_ref, blk, span, tile, pairs):
    end2 = info_ref[2] if span == "half" else info_ref[0]
    end1 = info_ref[3] if span == "half" else info_ref[1]

    def two(i, _):
        pairs(info_ref[LIST + 2 * i], info_ref[LIST + 2 * i + 1])
        return 0

    def clear(i, _):
        tile(info_ref[LIST + i], None)
        return 0

    def mixed(i, _):
        j = info_ref[LIST + WINDOW + i]
        kpos = info_ref[6 + j] + lax.broadcasted_iota(jnp.int32, (blk, blk), 0)
        for r in range(2):
            qpos = info_ref[4 + r] + lax.broadcasted_iota(jnp.int32, (1, blk), 1)
            bias_ref[r] = jnp.where((kpos <= qpos) & (kpos >= start_ref[r]), 0.0, BIG_NEG)
        tile(j, bias_ref)
        return 0

    half = lax.shift_right_logical(end2, 1)
    lax.fori_loop(0, half, two, 0)
    lax.fori_loop(2 * half, end2, clear, 0)
    lax.fori_loop(0, end1, mixed, 0)


def over_own(info_ref, start_ref, bias_ref, blk, r, base, tile):
    def one(i, _):
        j = info_ref[i]
        kpos = info_ref[6 + j] + lax.broadcasted_iota(jnp.int32, (blk, blk), 0)
        qpos = info_ref[4 + r] + lax.broadcasted_iota(jnp.int32, (1, blk), 1)
        bias_ref[r] = jnp.where((kpos <= qpos) & (kpos >= start_ref[r]), 0.0, BIG_NEG)
        tile(j - base, bias_ref, at=j - 2 * HALF)
        return 0

    lax.fori_loop(LIST + info_ref[2], LIST + info_ref[0], one, 0)
    lax.fori_loop(LIST + WINDOW + info_ref[3], LIST + WINDOW + info_ref[1], one, 0)


def forward_kernel(heads, hd, share, pieces, info_ref, start_ref, q0_ref, q1_ref, *rest):
    blk = q0_ref.shape[0]
    parts = 1 + max(piece[0] for piece in pieces)
    part_refs, rest = rest[:parts], rest[parts:]
    scale = LOG2E / math.sqrt(hd)
    if share == 0:
        m_ref, l_ref, a_ref, qs_ref, window_ref, bias_ref = rest
        m_ref[...] = jnp.full(m_ref.shape, BIG_NEG, jnp.float32)
        l_ref[...] = jnp.zeros(l_ref.shape, jnp.float32)
        a_ref[...] = jnp.zeros(a_ref.shape, jnp.float32)
    else:
        m_in, l_in, a_in, d0_ref, d1_ref, stat_ref, mine_ref, theirs_ref = rest[:8]
        qs_ref, window_ref, bias_ref, m_ref, l_ref, a_ref = rest[8:]
        m_ref[...] = m_in[...]
        l_ref[...] = l_in[...]
        a_ref[...] = a_in[...]
    fill(window_ref, part_refs, pieces, blk)
    fill_scaled(qs_ref, (q0_ref, q1_ref), heads, hd, scale)

    def update(kb, vb, masks):
        xs = range(2 * heads)
        vt = jnp.concatenate([vb.T, jnp.ones((16, vb.shape[0]), jnp.bfloat16)], axis=0)
        k2 = jnp.concatenate([kb, kb], axis=1)
        old = [(m_ref[x], l_ref[x], a_ref[x]) for x in xs]
        found = [nt(k2, qs_ref[x]) for x in xs]
        if masks is not None:
            found = [s + masks[x // heads] for x, s in zip(xs, found)]
        new = []
        for s, (m_old, l_old, a_old) in zip(found, old):
            m_new = jnp.maximum(m_old, jnp.max(s, axis=0, keepdims=True))
            p = jnp.exp2(s - m_new)
            f = jnp.exp2(m_old - m_new)
            both = nn(vt, p.astype(jnp.bfloat16))
            new.append((m_new, l_old * f + both[hd:hd + 1], a_old * f + both[:hd]))
        for x, (m_new, total, acc) in zip(xs, new):
            m_ref[x] = m_new
            l_ref[x] = total
            a_ref[x] = acc

    def tile(j, masks):
        update(window_ref[0, j], window_ref[1, j], masks)

    def pairs(j1, j2):
        kb, vb = [jnp.concatenate([window_ref[i, j1], window_ref[i, j2]], axis=0) for i in range(2)]
        update(kb, vb, None)

    over_tiles(info_ref, start_ref, bias_ref, blk, "all", tile, pairs)
    if share == 1:
        for r, d_ref in enumerate((d0_ref, d1_ref)):
            for h in range(heads):
                x = r * heads + h
                dt = d_ref[:, h * hd:(h + 1) * hd].astype(jnp.float32).T
                stat_ref[x, 0:1] = m_ref[x]
                stat_ref[x, 1:2] = l_ref[x]
                stat_ref[x, 2:3] = jnp.sum(dt * a_ref[x], axis=0, keepdims=True)
        mine_ref[...] = a_ref[:heads]
        theirs_ref[...] = a_ref[heads:].astype(jnp.bfloat16)


def vm():
    return pl.BlockSpec(memory_space=pltpu.VMEM)


def sm():
    return pl.BlockSpec(memory_space=pltpu.SMEM)


def params():
    return pltpu.CompilerParams(vmem_limit_bytes=24 << 20)


def forward(info, starts, q0, q1, parts, pieces, share, state=(), douts=()):
    blk, width = q0.shape
    hd = parts[0].shape[2]
    heads = width // hd
    n = 2 * heads
    f32 = jnp.float32
    row = jax.ShapeDtypeStruct((n, 1, blk), f32)
    work = [pltpu.VMEM((n, blk, 2 * hd), q0.dtype), pltpu.VMEM((2, WINDOW, blk, hd), q0.dtype),
            pltpu.VMEM((2, blk, blk), f32)]
    if share == 0:
        shapes = (row, row, jax.ShapeDtypeStruct((n, hd, blk), f32))
    else:
        shapes = (jax.ShapeDtypeStruct((n, 3, blk), f32), jax.ShapeDtypeStruct((heads, hd, blk), f32),
                  jax.ShapeDtypeStruct((heads, hd, blk), jnp.bfloat16))
        work += [pltpu.VMEM((n, 1, blk), f32), pltpu.VMEM((n, 1, blk), f32), pltpu.VMEM((n, hd, blk), f32)]
    args = (info, starts, q0, q1) + tuple(parts) + tuple(state) + tuple(douts)
    return pl.pallas_call(
        functools.partial(forward_kernel, heads, hd, share, pieces),
        out_shape=shapes,
        in_specs=[sm()] + [vm()] * (len(args) - 1),
        out_specs=(vm(),) * 3,
        scratch_shapes=work,
        compiler_params=params(),
        cost_estimate=pl.CostEstimate(flops=4 * WINDOW * n * blk * blk * hd, bytes_accessed=4 << 20, transcendentals=0),
        name="forward_part",
    )(*args)


def merge_stats(s_mine, s_theirs):
    m = jnp.maximum(s_mine[0:1], s_theirs[0:1])
    fa = jnp.exp2(s_mine[0:1] - m)
    fb = jnp.exp2(s_theirs[0:1] - m)
    total = s_mine[1:2] * fa + s_theirs[1:2] * fb
    delta = (s_mine[2:3] * fa + s_theirs[2:3] * fb) / total
    return m + jnp.log2(total), fa / total, fb / total, delta


def backward_kernel(heads, hd, span, pieces, info_ref, start_ref, q0_ref, q1_ref, d0_ref, d1_ref, sa_ref, sb_ref, *rest):
    blk = q0_ref.shape[0]
    scale = LOG2E / math.sqrt(hd)
    back = 1.0 / math.sqrt(hd)
    parts = 1 + max(piece[0] for piece in pieces)
    part_refs, rest = rest[:parts], rest[parts:]
    if span == "all":
        ga_ref, gb_ref, dq_ref = rest[:3]
        work = rest[3:]
        dq_ref[...] = jnp.zeros(dq_ref.shape, jnp.float32)
    elif span == "half":
        dq_in, ga_ref, gb_ref, own_ref, dq_out, send_ref = rest[:6]
        work = rest[6:-1]
        dq_ref = rest[-1]
        dq_ref[...] = dq_in[...]
    else:
        dq_in, own_ref, mine_ref, theirs_ref, ga_ref, gb_ref, att_ref, dq0_ref = rest[:8]
        work = rest[8:-1]
        dq_ref = rest[-1]
        dq_ref[...] = dq_in[...]
    q_ref, d_ref, window_ref, log_ref, delta_ref, qs_ref, bias_ref, grad_ref = work
    if span == "own":
        grad_ref[...] = own_ref[...]
    else:
        grad_ref[...] = jnp.zeros(grad_ref.shape, jnp.bfloat16)
    if span == "half":
        own_ref[...] = jnp.zeros(own_ref.shape, jnp.float32)
    fill(window_ref, part_refs, pieces, blk)
    fill_heads(q_ref, (q0_ref, q1_ref), heads, hd)
    fill_heads(d_ref, (d0_ref, d1_ref), heads, hd)
    fill_scaled(qs_ref, (q0_ref, q1_ref), heads, hd, scale)
    for r in range(1 if span == "own" else 2):
        for h in range(heads):
            x = r * heads + h
            log_total, wa, wb, delta = merge_stats(sa_ref[x], sb_ref[(1 - r) * heads + h])
            log_ref[x] = log_total
            delta_ref[x] = delta
            if span == "own" and r == 0:
                att = mine_ref[h] * wa + theirs_ref[h].astype(jnp.float32) * wb
                att_ref[:, h * hd:(h + 1) * hd] = att.T.astype(jnp.bfloat16)

    def tile(j, masks, xs=range(2 * heads), add_ref=None, at=None):
        kb = window_ref[0, j]
        vb = window_ref[1, j]
        kt = kb.T
        qs = [q_ref[x] for x in xs]
        ds = [d_ref[x] for x in xs]
        rows = [(log_ref[x], delta_ref[x]) for x in xs]
        sums = [dq_ref[x] for x in xs]
        k2 = jnp.concatenate([kb, kb], axis=1)
        found = [nt(k2, qs_ref[x]) for x in xs]
        pushed = [nt(vb, d) for d in ds]
        weights, slopes = [], []
        for x, s, dp, (log_total, delta) in zip(xs, found, pushed, rows):
            if masks is not None:
                s = s + masks[x // heads]
            p = jnp.exp2(s - log_total)
            weights.append(p.astype(jnp.bfloat16))
            slopes.append((p * (dp - delta)).astype(jnp.bfloat16))
        dv = nn(jnp.concatenate(weights, axis=1), jnp.concatenate(ds, axis=0))
        dk = nn(jnp.concatenate(slopes, axis=1), jnp.concatenate(qs, axis=0)) * back
        sums = [dq + nn(kt, slope) for dq, slope in zip(sums, slopes)]
        for x, dq in zip(xs, sums):
            dq_ref[x] = dq
        if add_ref is None:
            grad_ref[0, j] = dk.astype(jnp.bfloat16)
            grad_ref[1, j] = dv.astype(jnp.bfloat16)
        else:
            add_ref[0, at] += dk
            add_ref[1, at] += dv

    def pairs(j1, j2):
        xs = range(2 * heads)
        kb = jnp.concatenate([window_ref[0, j1], window_ref[0, j2]], axis=0)
        vb = jnp.concatenate([window_ref[1, j1], window_ref[1, j2]], axis=0)
        kt = kb.T
        qs = [q_ref[x] for x in xs]
        ds = [d_ref[x] for x in xs]
        rows = [(log_ref[x], delta_ref[x]) for x in xs]
        sums = [dq_ref[x] for x in xs]
        k2 = jnp.concatenate([kb, kb], axis=1)
        found = [nt(k2, qs_ref[x]) for x in xs]
        pushed = [nt(vb, d) for d in ds]
        weights, slopes = [], []
        for x, s, dp, (log_total, delta) in zip(xs, found, pushed, rows):
            p = jnp.exp2(s - log_total)
            weights.append(p.astype(jnp.bfloat16))
            slopes.append((p * (dp - delta)).astype(jnp.bfloat16))
        dv = nn(jnp.concatenate(weights, axis=1), jnp.concatenate(ds, axis=0))
        dk = nn(jnp.concatenate(slopes, axis=1), jnp.concatenate(qs, axis=0)) * back
        sums = [dq + nn(kt, slope) for dq, slope in zip(sums, slopes)]
        for x, dq in zip(xs, sums):
            dq_ref[x] = dq
        for i, g in enumerate((dk, dv)):
            grad_ref[i, j1] = g[:blk].astype(jnp.bfloat16)
            grad_ref[i, j2] = g[blk:].astype(jnp.bfloat16)

    if span != "own":
        over_tiles(info_ref, start_ref, bias_ref, blk, span, tile, pairs)
    if span != "all":
        r = 1 if span == "half" else 0
        xs = range(r * heads, (r + 1) * heads)
        over_own(info_ref, start_ref, bias_ref, blk, r, 0 if span == "half" else 2 * HALF,
                 functools.partial(tile, xs=xs, add_ref=own_ref if span == "half" else grad_ref))
    lists = {"all": ([0, 1, 2, 3, 8], [4, 5, 6, 7, 9]), "half": ([0, 1, 2, 3], [4, 5, 6, 7]), "own": ([0], [1])}
    for chunks, g_ref in zip(lists[span], (ga_ref, gb_ref)):
        for i, j in enumerate(chunks):
            rows = slice(i * blk, (i + 1) * blk)
            for kind in range(2):
                g_ref[kind, rows, :] = grad_ref[kind, j].astype(jnp.bfloat16)
    if span == "half":
        dq_out[...] = dq_ref[:heads]
        for h in range(heads):
            send_ref[:, h * hd:(h + 1) * hd] = (dq_ref[heads + h] * back).T.astype(jnp.bfloat16)
    if span == "own":
        for h in range(heads):
            dq0_ref[:, h * hd:(h + 1) * hd] = (dq_ref[h] * back).T


def backward(info, starts, q0, q1, d0, d1, s_mine, s_theirs, parts, pieces, span, sums=()):
    blk, width = q0.shape
    hd = parts[0].shape[2]
    heads = width // hd
    n = 2 * heads
    f32 = jnp.float32
    count = 2 if span == "own" else WINDOW
    sent = {"all": WINDOW // 2, "half": HALF, "own": 1}[span]
    grad = jax.ShapeDtypeStruct((2, sent * blk, hd), jnp.bfloat16)
    two = pltpu.VMEM((n, blk, hd), q0.dtype)
    row = pltpu.VMEM((n, 1, blk), f32)
    grads = pltpu.VMEM((2, 2 * sent, blk, hd), f32 if span == "own" else jnp.bfloat16)
    work = [two, two, pltpu.VMEM((2, count, blk, hd), q0.dtype), row, row,
            pltpu.VMEM((n, blk, 2 * hd), q0.dtype), pltpu.VMEM((2, blk, blk), f32), grads]
    out = jax.ShapeDtypeStruct((blk, width), jnp.bfloat16)
    if span == "all":
        shapes = (grad, grad, jax.ShapeDtypeStruct((n, hd, blk), f32))
    elif span == "half":
        shapes = (grad, grad, jax.ShapeDtypeStruct((2, 2, blk, hd), f32),
                  jax.ShapeDtypeStruct((heads, hd, blk), f32), out)
        work += [pltpu.VMEM((n, hd, blk), f32)]
    else:
        shapes = (grad, grad, out, jax.ShapeDtypeStruct((blk, width), f32))
        work += [pltpu.VMEM((heads, hd, blk), f32)]
    args = (info, starts, q0, q1, d0, d1, s_mine, s_theirs) + tuple(parts) + tuple(sums)
    return pl.pallas_call(
        functools.partial(backward_kernel, heads, hd, span, pieces),
        out_shape=shapes,
        in_specs=[sm()] + [vm()] * (len(args) - 1),
        out_specs=(vm(),) * len(shapes),
        scratch_shapes=work,
        compiler_params=params(),
        cost_estimate=pl.CostEstimate(flops=10 * count * n * blk * blk * hd, bytes_accessed=4 << 20, transcendentals=0),
        name="backward_part",
    )(*args)


def per_device(queries, keys, values, dout, doc_lengths):
    blk = queries.shape[0]
    seqs, subs = lax.axis_size("seq"), lax.axis_size("sub")
    seq, sub = lax.axis_index("seq"), lax.axis_index("sub")
    f32, bf16 = jnp.float32, jnp.bfloat16
    chip, core = seq // 2, seq % 2
    mate = sub + 1 - 2 * (sub % 2)
    far = (sub + 2 * (sub % 2) - 1 + subs) % subs
    def swap_core(value):
        return lax.ppermute(value, "seq", [(s, s ^ 1) for s in range(seqs)])

    def swap_mate(value):
        return lax.ppermute(value, "sub", [(s, s ^ 1) for s in range(subs)])

    def swap_far(value):
        return lax.ppermute(value, "sub", [(s, (s + 2 * (s % 2) - 1) % subs) for s in range(subs)])

    def route(step, sign):
        pairs = [(s, s + 2 * (1 + step + 2 * (s % 2))) for s in range(seqs)]
        return [(a, b)[::sign] for a, b in pairs if b < seqs]

    tie = lax.optimization_barrier
    other_keys, other_values = swap_core(keys), swap_core(values)
    q_mate = swap_mate(queries)
    ids = jnp.stack([chip, core, sub, mate, far]).astype(jnp.int32)
    pair = jnp.concatenate([jnp.stack([keys, values]), jnp.stack([other_keys, other_values])], axis=1)
    pair, ids = tie((pair, ids))
    near = lax.ppermute(pair, "seq", route(0, 1))
    away = lax.ppermute(pair, "seq", route(1, 1))
    *infos, starts = tables(ids, doc_lengths, blk, subs)
    near, infos, starts = tie((near, infos, starts))
    near_far = swap_far(near)
    away, q_mate, near_far, d_send = tie((away, q_mate, near_far, dout))
    d_mate = swap_mate(d_send)
    most = jnp.concatenate([near, away, near_far], axis=1)
    most_x = swap_core(most)
    away_far = swap_far(jnp.concatenate([away, pair[:, :blk]], axis=1))
    near_pieces = ((0, 0, HALF), (1, 0, HALF), (2, 0, 2))
    far_pieces = ((0, HALF, 2), (2, 0, 2), (1, HALF, 2), (3, 0, 2), (2, 2, 1), (3, 2, 1))
    state = forward(infos[0], starts, queries, q_mate, (most, most_x, pair), near_pieces, 0)
    away_far, state, d_mate = tie((away_far, state, d_mate))
    away_far_x = swap_core(away_far)
    far_parts = (most, most_x, away_far, away_far_x)
    stats, mine, theirs = forward(infos[1], starts, queries, q_mate, far_parts, far_pieces, 1, state, (dout, d_mate))
    common = (starts, queries, q_mate, dout, d_mate, stats, swap_mate(stats))
    grad_a, grad_b, dq = backward(infos[1], *common, far_parts, far_pieces, "all")
    grad_b, theirs = tie((grad_b, theirs))
    theirs = swap_mate(theirs)
    grad_a = (grad_a.astype(f32) + swap_core(grad_b).astype(f32)).astype(bf16)
    grad_a, dq = tie((grad_a, dq))
    grad_far = swap_far(grad_a[:, : HALF * blk])
    near_parts = (most, most_x, pair)
    far_own = grad_a[:, HALF * blk :]
    grad_a, grad_b, own, dq, dq_send = backward(infos[0], *common, near_parts, near_pieces, "half", (dq,))
    grad_b, grad_far, theirs = tie((grad_b, grad_far, theirs))
    home = (grad_a.astype(f32) + swap_core(grad_b).astype(f32) + grad_far.astype(f32)).astype(bf16)
    home, dq, dq_send = tie((home, dq, dq_send))
    near = lax.ppermute(home[:, : 2 * blk], "seq", route(0, -1))
    away = lax.ppermute(home[:, 2 * blk :], "seq", route(1, -1))
    dq_back = swap_mate(dq_send)
    grad_own, grad_other, attended, dq_mine = backward(
        infos[0], *common, (pair,), ((0, 0, 2),), "own", (dq, own, mine, theirs)
    )
    grad_own, far_own = tie((grad_own, far_own))
    grad_far_own = swap_far(far_own)
    near, away, dq_back, grad_own, grad_other = tie((near, away, dq_back, grad_own, grad_other))
    back = near.astype(f32) + away.astype(f32)
    other = swap_core((back[:, blk:] + grad_other.astype(f32)).astype(bf16))
    query_grad = (dq_mine + dq_back.astype(f32)).astype(bf16)
    total = [
        (grad_own[i].astype(f32) + grad_far_own[i].astype(f32) + back[i, :blk] + other[i].astype(f32)).astype(bf16)
        for i in range(2)
    ]
    return attended, query_grad, total[0], total[1]


def solution(mesh):
    rows = P(("seq", "sub"), None)
    return jax.shard_map(
        per_device,
        mesh=mesh,
        in_specs=(rows, rows, rows, rows, P()),
        out_specs=(rows, rows, rows, rows),
        check_vma=False,
    )
```

```python
import functools
import math

import jax
import jax.numpy as jnp
from jax import lax
from jax.experimental import pallas as pl
from jax.experimental.pallas import tpu as pltpu
from jax.sharding import PartitionSpec as P

BIG_NEG = -1e30
LOG2E = 1.4426950408889634
HALF = 4
WINDOW = 2 * HALF + 2
LIST = 6 + WINDOW


def nt(a, b):
    return lax.dot_general(a, b, (((1,), (1,)), ((), ())), preferred_element_type=jnp.float32)


def nn(a, b):
    return lax.dot_general(a, b, (((1,), (0,)), ((), ())), preferred_element_type=jnp.float32)


def table_kernel(blk, subs, len_ref, near_ref, far_ref, start_ref):
    seq, sub = lax.axis_index("seq"), lax.axis_index("sub")
    chip, core = seq // 2, seq % 2
    mate = sub + 1 - 2 * (sub % 2)
    far = (sub + 2 * (sub % 2) - 1 + subs) % subs
    q0 = [((2 * chip + core) * subs + side) * blk for side in (sub, mate)]
    qpos = [q + lax.broadcasted_iota(jnp.int32, (1, blk), 1) for q in q0]
    zero = jnp.int32(0)
    begin, first, last = zero, [zero] * 2, [zero] * 2
    found = [jnp.zeros((1, blk), jnp.int32)] * 2
    for d in range(len_ref.shape[0]):
        for r in range(2):
            first[r] = jnp.where(begin <= q0[r], begin, first[r])
            last[r] = jnp.where(begin <= q0[r] + blk - 1, begin, last[r])
            found[r] = jnp.where(begin <= qpos[r], begin, found[r])
        begin = begin + len_ref[d]
    for r in range(2):
        start_ref[r] = found[r]
    for info_ref, share in ((near_ref, sub), (far_ref, far)):
        count2, count1 = zero, zero
        for j in range(WINDOW):
            if j == 2 * HALF:
                info_ref[2] = count2
                info_ref[3] = count1
            owner = core if j < HALF or j == 2 * HALF else 1 - core
            jj = j % HALF
            back = 0 if j >= 2 * HALF else 1 + 2 * owner if jj < 2 else 2 + 2 * owner
            parity = owner if j >= 2 * HALF or jj % 2 == 0 else 1 - owner
            kstart = ((2 * (chip - back) + parity) * subs + share) * blk
            kend = kstart + blk - 1
            active = [(kend >= first[r]) & (kstart <= q0[r] + blk - 1) for r in range(2)]
            whole = [(kstart >= last[r]) & (kend <= q0[r]) for r in range(2)]
            clear = active[0] & whole[0] & active[1] & whole[1]
            mixed = (active[0] | active[1]) & jnp.logical_not(clear)
            info_ref[6 + j] = kstart
            info_ref[LIST + count2] = j
            count2 = count2 + clear.astype(jnp.int32)
            info_ref[LIST + WINDOW + count1] = j
            count1 = count1 + mixed.astype(jnp.int32)
        info_ref[0] = count2
        info_ref[1] = count1
        info_ref[4] = q0[0]
        info_ref[5] = q0[1]


def tables(doc_lengths, blk, subs):
    info = jax.ShapeDtypeStruct((LIST + 2 * WINDOW,), jnp.int32)
    return pl.pallas_call(
        functools.partial(table_kernel, blk, subs),
        out_shape=(info, info, jax.ShapeDtypeStruct((2, 1, blk), jnp.int32)),
        in_specs=[sm()],
        out_specs=(sm(), sm(), vm()),
        name="tile_tables",
    )(doc_lengths)


def fill(window_ref, part_refs, pieces, blk):
    at = 0
    for part, begin, count in pieces:
        for i in range(count):
            for kind in range(2):
                window_ref[kind, at] = part_refs[part][kind, (begin + i) * blk:(begin + i + 1) * blk, :]
            at += 1


def fill_heads(dest_ref, sources, heads, hd):
    for r, source in enumerate(sources):
        for h in range(heads):
            dest_ref[r * heads + h] = source[:, h * hd:(h + 1) * hd]


def fill_scaled(dest_ref, sources, heads, hd, scale):
    for r, source in enumerate(sources):
        for h in range(heads):
            whole = source[:, h * hd:(h + 1) * hd].astype(jnp.float32) * scale
            high = whole.astype(jnp.bfloat16)
            dest_ref[r * heads + h, :, :hd] = high
            dest_ref[r * heads + h, :, hd:] = (whole - high.astype(jnp.float32)).astype(jnp.bfloat16)


def over_tiles(info_ref, start_ref, bias_ref, blk, span, tile, pairs):
    end2 = info_ref[2] if span == "half" else info_ref[0]
    end1 = info_ref[3] if span == "half" else info_ref[1]

    def two(i, _):
        pairs(info_ref[LIST + 2 * i], info_ref[LIST + 2 * i + 1])
        return 0

    def clear(i, _):
        tile(info_ref[LIST + i], None)
        return 0

    def mixed(i, _):
        j = info_ref[LIST + WINDOW + i]
        kpos = info_ref[6 + j] + lax.broadcasted_iota(jnp.int32, (blk, blk), 0)
        for r in range(2):
            qpos = info_ref[4 + r] + lax.broadcasted_iota(jnp.int32, (1, blk), 1)
            bias_ref[r] = jnp.where((kpos <= qpos) & (kpos >= start_ref[r]), 0.0, BIG_NEG)
        tile(j, bias_ref)
        return 0

    half = lax.shift_right_logical(end2, 1)
    lax.fori_loop(0, half, two, 0)
    lax.fori_loop(2 * half, end2, clear, 0)
    lax.fori_loop(0, end1, mixed, 0)


def over_own(info_ref, start_ref, bias_ref, blk, r, base, tile):
    def one(i, _):
        j = info_ref[i]
        kpos = info_ref[6 + j] + lax.broadcasted_iota(jnp.int32, (blk, blk), 0)
        qpos = info_ref[4 + r] + lax.broadcasted_iota(jnp.int32, (1, blk), 1)
        bias_ref[r] = jnp.where((kpos <= qpos) & (kpos >= start_ref[r]), 0.0, BIG_NEG)
        tile(j - base, bias_ref, at=j - 2 * HALF)
        return 0

    lax.fori_loop(LIST + info_ref[2], LIST + info_ref[0], one, 0)
    lax.fori_loop(LIST + WINDOW + info_ref[3], LIST + WINDOW + info_ref[1], one, 0)


def forward_kernel(heads, hd, share, pieces, info_ref, start_ref, q0_ref, q1_ref, *rest):
    blk = q0_ref.shape[0]
    parts = 1 + max(piece[0] for piece in pieces)
    part_refs, rest = rest[:parts], rest[parts:]
    scale = LOG2E / math.sqrt(hd)
    if share == 0:
        m_ref, l_ref, a_ref, qs_ref, window_ref, bias_ref = rest
        m_ref[...] = jnp.full(m_ref.shape, BIG_NEG, jnp.float32)
        l_ref[...] = jnp.zeros(l_ref.shape, jnp.float32)
        a_ref[...] = jnp.zeros(a_ref.shape, jnp.float32)
    else:
        m_in, l_in, a_in, d0_ref, d1_ref, stat_ref, mine_ref, theirs_ref = rest[:8]
        qs_ref, window_ref, bias_ref, m_ref, l_ref, a_ref = rest[8:]
        m_ref[...] = m_in[...]
        l_ref[...] = l_in[...]
        a_ref[...] = a_in[...]
    fill(window_ref, part_refs, pieces, blk)
    fill_scaled(qs_ref, (q0_ref, q1_ref), heads, hd, scale)

    def update(kb, vb, masks):
        xs = range(2 * heads)
        vt = jnp.concatenate([vb.T, jnp.ones((16, vb.shape[0]), jnp.bfloat16)], axis=0)
        k2 = jnp.concatenate([kb, kb], axis=1)
        old = [(m_ref[x], l_ref[x], a_ref[x]) for x in xs]
        found = [nt(k2, qs_ref[x]) for x in xs]
        if masks is not None:
            found = [s + masks[x // heads] for x, s in zip(xs, found)]
        new = []
        for s, (m_old, l_old, a_old) in zip(found, old):
            m_new = jnp.maximum(m_old, jnp.max(s, axis=0, keepdims=True))
            p = jnp.exp2(s - m_new)
            f = jnp.exp2(m_old - m_new)
            both = nn(vt, p.astype(jnp.bfloat16))
            new.append((m_new, l_old * f + both[hd:hd + 1], a_old * f + both[:hd]))
        for x, (m_new, total, acc) in zip(xs, new):
            m_ref[x] = m_new
            l_ref[x] = total
            a_ref[x] = acc

    def tile(j, masks):
        update(window_ref[0, j], window_ref[1, j], masks)

    def pairs(j1, j2):
        kb, vb = [jnp.concatenate([window_ref[i, j1], window_ref[i, j2]], axis=0) for i in range(2)]
        update(kb, vb, None)

    over_tiles(info_ref, start_ref, bias_ref, blk, "all", tile, pairs)
    if share == 1:
        for r, d_ref in enumerate((d0_ref, d1_ref)):
            for h in range(heads):
                x = r * heads + h
                dt = d_ref[:, h * hd:(h + 1) * hd].astype(jnp.float32).T
                stat_ref[x, 0:1] = m_ref[x]
                stat_ref[x, 1:2] = l_ref[x]
                stat_ref[x, 2:3] = jnp.sum(dt * a_ref[x], axis=0, keepdims=True)
        mine_ref[...] = a_ref[:heads]
        theirs_ref[...] = a_ref[heads:].astype(jnp.bfloat16)


def vm():
    return pl.BlockSpec(memory_space=pltpu.VMEM)


def sm():
    return pl.BlockSpec(memory_space=pltpu.SMEM)


def params():
    return pltpu.CompilerParams(vmem_limit_bytes=24 << 20)


def forward(info, starts, q0, q1, parts, pieces, share, state=(), douts=()):
    blk, width = q0.shape
    hd = parts[0].shape[2]
    heads = width // hd
    n = 2 * heads
    f32 = jnp.float32
    row = jax.ShapeDtypeStruct((n, 1, blk), f32)
    work = [pltpu.VMEM((n, blk, 2 * hd), q0.dtype), pltpu.VMEM((2, WINDOW, blk, hd), q0.dtype),
            pltpu.VMEM((2, blk, blk), f32)]
    if share == 0:
        shapes = (row, row, jax.ShapeDtypeStruct((n, hd, blk), f32))
    else:
        shapes = (jax.ShapeDtypeStruct((n, 3, blk), f32), jax.ShapeDtypeStruct((heads, hd, blk), f32),
                  jax.ShapeDtypeStruct((heads, hd, blk), jnp.bfloat16))
        work += [pltpu.VMEM((n, 1, blk), f32), pltpu.VMEM((n, 1, blk), f32), pltpu.VMEM((n, hd, blk), f32)]
    args = (info, starts, q0, q1) + tuple(parts) + tuple(state) + tuple(douts)
    return pl.pallas_call(
        functools.partial(forward_kernel, heads, hd, share, pieces),
        out_shape=shapes,
        in_specs=[sm()] + [vm()] * (len(args) - 1),
        out_specs=(vm(),) * 3,
        scratch_shapes=work,
        compiler_params=params(),
        cost_estimate=pl.CostEstimate(flops=4 * WINDOW * n * blk * blk * hd, bytes_accessed=4 << 20, transcendentals=0),
        name="forward_part",
    )(*args)


def merge_stats(s_mine, s_theirs):
    m = jnp.maximum(s_mine[0:1], s_theirs[0:1])
    fa = jnp.exp2(s_mine[0:1] - m)
    fb = jnp.exp2(s_theirs[0:1] - m)
    total = s_mine[1:2] * fa + s_theirs[1:2] * fb
    delta = (s_mine[2:3] * fa + s_theirs[2:3] * fb) / total
    return m + jnp.log2(total), fa / total, fb / total, delta


def backward_kernel(heads, hd, span, pieces, info_ref, start_ref, q0_ref, q1_ref, d0_ref, d1_ref, sa_ref, sb_ref, *rest):
    blk = q0_ref.shape[0]
    scale = LOG2E / math.sqrt(hd)
    back = 1.0 / math.sqrt(hd)
    parts = 1 + max(piece[0] for piece in pieces)
    part_refs, rest = rest[:parts], rest[parts:]
    if span == "all":
        ga_ref, gb_ref, dq_ref = rest[:3]
        work = rest[3:]
        dq_ref[...] = jnp.zeros(dq_ref.shape, jnp.float32)
    elif span == "half":
        dq_in, ga_ref, gb_ref, own_ref, dq_out, send_ref = rest[:6]
        work = rest[6:-1]
        dq_ref = rest[-1]
        dq_ref[...] = dq_in[...]
    else:
        dq_in, own_ref, mine_ref, theirs_ref, ga_ref, gb_ref, att_ref, dq0_ref = rest[:8]
        work = rest[8:-1]
        dq_ref = rest[-1]
        dq_ref[...] = dq_in[...]
    q_ref, d_ref, window_ref, log_ref, delta_ref, qs_ref, bias_ref, grad_ref = work
    if span == "own":
        grad_ref[...] = own_ref[...]
    else:
        grad_ref[...] = jnp.zeros(grad_ref.shape, jnp.bfloat16)
    if span == "half":
        own_ref[...] = jnp.zeros(own_ref.shape, jnp.float32)
    fill(window_ref, part_refs, pieces, blk)
    fill_heads(q_ref, (q0_ref, q1_ref), heads, hd)
    fill_heads(d_ref, (d0_ref, d1_ref), heads, hd)
    fill_scaled(qs_ref, (q0_ref, q1_ref), heads, hd, scale)
    for r in range(1 if span == "own" else 2):
        for h in range(heads):
            x = r * heads + h
            log_total, wa, wb, delta = merge_stats(sa_ref[x], sb_ref[(1 - r) * heads + h])
            log_ref[x] = log_total
            delta_ref[x] = delta
            if span == "own" and r == 0:
                att = mine_ref[h] * wa + theirs_ref[h].astype(jnp.float32) * wb
                att_ref[:, h * hd:(h + 1) * hd] = att.T.astype(jnp.bfloat16)

    def tile(j, masks, xs=range(2 * heads), add_ref=None, at=None):
        kb = window_ref[0, j]
        vb = window_ref[1, j]
        kt = kb.T
        qs = [q_ref[x] for x in xs]
        ds = [d_ref[x] for x in xs]
        rows = [(log_ref[x], delta_ref[x]) for x in xs]
        sums = [dq_ref[x] for x in xs]
        k2 = jnp.concatenate([kb, kb], axis=1)
        found = [nt(k2, qs_ref[x]) for x in xs]
        pushed = [nt(vb, d) for d in ds]
        weights, slopes = [], []
        for x, s, dp, (log_total, delta) in zip(xs, found, pushed, rows):
            if masks is not None:
                s = s + masks[x // heads]
            p = jnp.exp2(s - log_total)
            weights.append(p.astype(jnp.bfloat16))
            slopes.append((p * (dp - delta)).astype(jnp.bfloat16))
        dv = nn(jnp.concatenate(weights, axis=1), jnp.concatenate(ds, axis=0))
        dk = nn(jnp.concatenate(slopes, axis=1), jnp.concatenate(qs, axis=0)) * back
        sums = [dq + nn(kt, slope) for dq, slope in zip(sums, slopes)]
        for x, dq in zip(xs, sums):
            dq_ref[x] = dq
        if add_ref is None:
            grad_ref[0, j] = dk.astype(jnp.bfloat16)
            grad_ref[1, j] = dv.astype(jnp.bfloat16)
        else:
            add_ref[0, at] += dk
            add_ref[1, at] += dv

    def pairs(j1, j2):
        xs = range(2 * heads)
        kb = jnp.concatenate([window_ref[0, j1], window_ref[0, j2]], axis=0)
        vb = jnp.concatenate([window_ref[1, j1], window_ref[1, j2]], axis=0)
        kt = kb.T
        qs = [q_ref[x] for x in xs]
        ds = [d_ref[x] for x in xs]
        rows = [(log_ref[x], delta_ref[x]) for x in xs]
        sums = [dq_ref[x] for x in xs]
        k2 = jnp.concatenate([kb, kb], axis=1)
        found = [nt(k2, qs_ref[x]) for x in xs]
        pushed = [nt(vb, d) for d in ds]
        weights, slopes = [], []
        for x, s, dp, (log_total, delta) in zip(xs, found, pushed, rows):
            p = jnp.exp2(s - log_total)
            weights.append(p.astype(jnp.bfloat16))
            slopes.append((p * (dp - delta)).astype(jnp.bfloat16))
        dv = nn(jnp.concatenate(weights, axis=1), jnp.concatenate(ds, axis=0))
        dk = nn(jnp.concatenate(slopes, axis=1), jnp.concatenate(qs, axis=0)) * back
        sums = [dq + nn(kt, slope) for dq, slope in zip(sums, slopes)]
        for x, dq in zip(xs, sums):
            dq_ref[x] = dq
        for i, g in enumerate((dk, dv)):
            grad_ref[i, j1] = g[:blk].astype(jnp.bfloat16)
            grad_ref[i, j2] = g[blk:].astype(jnp.bfloat16)

    if span != "own":
        over_tiles(info_ref, start_ref, bias_ref, blk, span, tile, pairs)
    if span != "all":
        r = 1 if span == "half" else 0
        xs = range(r * heads, (r + 1) * heads)
        over_own(info_ref, start_ref, bias_ref, blk, r, 0 if span == "half" else 2 * HALF,
                 functools.partial(tile, xs=xs, add_ref=own_ref if span == "half" else grad_ref))
    lists = {"all": ([0, 1, 2, 3, 8], [4, 5, 6, 7, 9]), "half": ([0, 1, 2, 3], [4, 5, 6, 7]), "own": ([0], [1])}
    for chunks, g_ref in zip(lists[span], (ga_ref, gb_ref)):
        for i, j in enumerate(chunks):
            rows = slice(i * blk, (i + 1) * blk)
            for kind in range(2):
                g_ref[kind, rows, :] = grad_ref[kind, j].astype(jnp.bfloat16)
    if span == "half":
        dq_out[...] = dq_ref[:heads]
        for h in range(heads):
            send_ref[:, h * hd:(h + 1) * hd] = (dq_ref[heads + h] * back).T.astype(jnp.bfloat16)
    if span == "own":
        for h in range(heads):
            dq0_ref[:, h * hd:(h + 1) * hd] = (dq_ref[h] * back).T


def backward(info, starts, q0, q1, d0, d1, s_mine, s_theirs, parts, pieces, span, sums=()):
    blk, width = q0.shape
    hd = parts[0].shape[2]
    heads = width // hd
    n = 2 * heads
    f32 = jnp.float32
    count = 2 if span == "own" else WINDOW
    sent = {"all": WINDOW // 2, "half": HALF, "own": 1}[span]
    grad = jax.ShapeDtypeStruct((2, sent * blk, hd), jnp.bfloat16)
    two = pltpu.VMEM((n, blk, hd), q0.dtype)
    row = pltpu.VMEM((n, 1, blk), f32)
    grads = pltpu.VMEM((2, 2 * sent, blk, hd), f32 if span == "own" else jnp.bfloat16)
    work = [two, two, pltpu.VMEM((2, count, blk, hd), q0.dtype), row, row,
            pltpu.VMEM((n, blk, 2 * hd), q0.dtype), pltpu.VMEM((2, blk, blk), f32), grads]
    out = jax.ShapeDtypeStruct((blk, width), jnp.bfloat16)
    if span == "all":
        shapes = (grad, grad, jax.ShapeDtypeStruct((n, hd, blk), f32))
    elif span == "half":
        shapes = (grad, grad, jax.ShapeDtypeStruct((2, 2, blk, hd), f32),
                  jax.ShapeDtypeStruct((heads, hd, blk), f32), out)
        work += [pltpu.VMEM((n, hd, blk), f32)]
    else:
        shapes = (grad, grad, out, jax.ShapeDtypeStruct((blk, width), f32))
        work += [pltpu.VMEM((heads, hd, blk), f32)]
    args = (info, starts, q0, q1, d0, d1, s_mine, s_theirs) + tuple(parts) + tuple(sums)
    return pl.pallas_call(
        functools.partial(backward_kernel, heads, hd, span, pieces),
        out_shape=shapes,
        in_specs=[sm()] + [vm()] * (len(args) - 1),
        out_specs=(vm(),) * len(shapes),
        scratch_shapes=work,
        compiler_params=params(),
        cost_estimate=pl.CostEstimate(flops=10 * count * n * blk * blk * hd, bytes_accessed=4 << 20, transcendentals=0),
        name="backward_part",
    )(*args)


def per_device(queries, keys, values, dout, doc_lengths):
    blk = queries.shape[0]
    seqs, subs = lax.axis_size("seq"), lax.axis_size("sub")
    f32, bf16 = jnp.float32, jnp.bfloat16

    def swap_core(value):
        return lax.ppermute(value, "seq", [(s, s ^ 1) for s in range(seqs)])

    def swap_mate(value):
        return lax.ppermute(value, "sub", [(s, s ^ 1) for s in range(subs)])

    def swap_far(value):
        return lax.ppermute(value, "sub", [(s, (s + 2 * (s % 2) - 1) % subs) for s in range(subs)])

    def route(step, sign):
        pairs = [(s, s + 2 * (1 + step + 2 * (s % 2))) for s in range(seqs)]
        return [(a, b)[::sign] for a, b in pairs if b < seqs]

    tie = lax.optimization_barrier
    other_keys, other_values = swap_core(keys), swap_core(values)
    q_mate = swap_mate(queries)
    pair = jnp.concatenate([jnp.stack([keys, values]), jnp.stack([other_keys, other_values])], axis=1)
    pair, doc_lengths = tie((pair, doc_lengths))
    near = lax.ppermute(pair, "seq", route(0, 1))
    away = lax.ppermute(pair, "seq", route(1, 1))
    *infos, starts = tables(doc_lengths, blk, subs)
    near, infos, starts, q_mate = tie((near, infos, starts, q_mate))
    near_far = swap_far(near)
    away, near_far, d_send = tie((away, near_far, dout))
    d_mate = swap_mate(d_send)
    most = jnp.concatenate([near, away, near_far], axis=1)
    most_x = swap_core(most)
    away_far = swap_far(jnp.concatenate([away, pair[:, :blk]], axis=1))
    near_pieces = ((0, 0, HALF), (1, 0, HALF), (2, 0, 2))
    far_pieces = ((0, HALF, 2), (2, 0, 2), (1, HALF, 2), (3, 0, 2), (2, 2, 1), (3, 2, 1))
    state = forward(infos[0], starts, queries, q_mate, (most, most_x, pair), near_pieces, 0)
    away_far, state, d_mate = tie((away_far, state, d_mate))
    away_far_x = swap_core(away_far)
    far_parts = (most, most_x, away_far, away_far_x)
    stats, mine, theirs = forward(infos[1], starts, queries, q_mate, far_parts, far_pieces, 1, state, (dout, d_mate))
    common = (starts, queries, q_mate, dout, d_mate, stats, swap_mate(stats))
    grad_a, grad_b, dq = backward(infos[1], *common, far_parts, far_pieces, "all")
    grad_b, theirs = tie((grad_b, theirs))
    theirs = swap_mate(theirs)
    grad_a = (grad_a.astype(f32) + swap_core(grad_b).astype(f32)).astype(bf16)
    grad_a, dq = tie((grad_a, dq))
    grad_far = swap_far(grad_a[:, : HALF * blk])
    near_parts = (most, most_x, pair)
    far_own = grad_a[:, HALF * blk :]
    grad_a, grad_b, own, dq, dq_send = backward(infos[0], *common, near_parts, near_pieces, "half", (dq,))
    grad_b, grad_far, theirs = tie((grad_b, grad_far, theirs))
    home = (grad_a.astype(f32) + swap_core(grad_b).astype(f32) + grad_far.astype(f32)).astype(bf16)
    home, dq = tie((home, dq))
    near = lax.ppermute(home[:, : 2 * blk], "seq", route(0, -1))
    away = lax.ppermute(home[:, 2 * blk :], "seq", route(1, -1))
    dq_back = swap_mate(dq_send)
    grad_own, grad_other, attended, dq_mine = backward(
        infos[0], *common, (pair,), ((0, 0, 2),), "own", (dq, own, mine, theirs)
    )
    grad_own, far_own = tie((grad_own, far_own))
    grad_far_own = swap_far(far_own)
    near, away, dq_back, grad_own, grad_other = tie((near, away, dq_back, grad_own, grad_other))
    back = near.astype(f32) + away.astype(f32)
    other = swap_core((back[:, blk:] + grad_other.astype(f32)).astype(bf16))
    query_grad = (dq_mine + dq_back.astype(f32)).astype(bf16)
    total = [
        (grad_own[i].astype(f32) + grad_far_own[i].astype(f32) + back[i, :blk] + other[i].astype(f32)).astype(bf16)
        for i in range(2)
    ]
    return attended, query_grad, total[0], total[1]


def solution(mesh):
    rows = P(("seq", "sub"), None)
    return jax.shard_map(
        per_device,
        mesh=mesh,
        in_specs=(rows, rows, rows, rows, P()),
        out_specs=(rows, rows, rows, rows),
        check_vma=False,
    )
```

```python
import functools
import math

import jax
import jax.numpy as jnp
from jax import lax
from jax.experimental import pallas as pl
from jax.experimental.pallas import tpu as pltpu
from jax.sharding import PartitionSpec as P

BIG_NEG = -1e30
LOG2E = 1.4426950408889634
NEAR, AWAY = (4, 1), (3, 2)
HALF = 4
WINDOW = 2 * HALF + 2
LIST = 6 + WINDOW


def nt(a, b):
    return lax.dot_general(a, b, (((1,), (1,)), ((), ())), preferred_element_type=jnp.float32)


def nn(a, b):
    return lax.dot_general(a, b, (((1,), (0,)), ((), ())), preferred_element_type=jnp.float32)


def table_kernel(blk, subs, len_ref, near_ref, far_ref, start_ref):
    seq, sub = lax.axis_index("seq"), lax.axis_index("sub")
    chip, core = seq // 2, seq % 2
    mate = sub + 1 - 2 * (sub % 2)
    far = (sub + 2 * (sub % 2) - 1 + subs) % subs
    q0 = [((2 * chip + core) * subs + side) * blk for side in (sub, mate)]
    qpos = [q + lax.broadcasted_iota(jnp.int32, (1, blk), 1) for q in q0]
    zero = jnp.int32(0)
    begin, first, last = zero, [zero] * 2, [zero] * 2
    found = [jnp.zeros((1, blk), jnp.int32)] * 2
    for d in range(len_ref.shape[0]):
        for r in range(2):
            first[r] = jnp.where(begin <= q0[r], begin, first[r])
            last[r] = jnp.where(begin <= q0[r] + blk - 1, begin, last[r])
            found[r] = jnp.where(begin <= qpos[r], begin, found[r])
        begin = begin + len_ref[d]
    for r in range(2):
        start_ref[r] = found[r]
    for info_ref, share in ((near_ref, sub), (far_ref, far)):
        count2, count1 = zero, zero
        for j in range(WINDOW):
            if j == 2 * HALF:
                info_ref[2] = count2
                info_ref[3] = count1
            owner = core if j < HALF or j == 2 * HALF else 1 - core
            jj = j % HALF
            chips = NEAR if jj < 2 else AWAY
            back = 0 if j >= 2 * HALF else jnp.where(owner == 0, chips[0], chips[1])
            parity = owner if j >= 2 * HALF or jj % 2 == 0 else 1 - owner
            kstart = ((2 * (chip - back) + parity) * subs + share) * blk
            kend = kstart + blk - 1
            active = [(kend >= first[r]) & (kstart <= q0[r] + blk - 1) for r in range(2)]
            whole = [(kstart >= last[r]) & (kend <= q0[r]) for r in range(2)]
            clear = active[0] & whole[0] & active[1] & whole[1]
            mixed = (active[0] | active[1]) & jnp.logical_not(clear)
            info_ref[6 + j] = kstart
            info_ref[LIST + count2] = j
            count2 = count2 + clear.astype(jnp.int32)
            info_ref[LIST + WINDOW + count1] = j
            count1 = count1 + mixed.astype(jnp.int32)
        info_ref[0] = count2
        info_ref[1] = count1
        info_ref[4] = q0[0]
        info_ref[5] = q0[1]


def tables(doc_lengths, blk, subs):
    info = jax.ShapeDtypeStruct((LIST + 2 * WINDOW,), jnp.int32)
    return pl.pallas_call(
        functools.partial(table_kernel, blk, subs),
        out_shape=(info, info, jax.ShapeDtypeStruct((2, 1, blk), jnp.int32)),
        in_specs=[sm()],
        out_specs=(sm(), sm(), vm()),
        name="tile_tables",
    )(doc_lengths)


def fill(window_ref, part_refs, pieces, blk):
    at = 0
    for part, begin, count in pieces:
        for i in range(count):
            for kind in range(2):
                window_ref[kind, at] = part_refs[part][kind, (begin + i) * blk:(begin + i + 1) * blk, :]
            at += 1


def fill_heads(dest_ref, sources, heads, hd):
    for r, source in enumerate(sources):
        for h in range(heads):
            dest_ref[r * heads + h] = source[:, h * hd:(h + 1) * hd]


def fill_scaled(dest_ref, sources, heads, hd, scale):
    for r, source in enumerate(sources):
        for h in range(heads):
            whole = source[:, h * hd:(h + 1) * hd].astype(jnp.float32) * scale
            high = whole.astype(jnp.bfloat16)
            dest_ref[r * heads + h, :, :hd] = high
            dest_ref[r * heads + h, :, hd:] = (whole - high.astype(jnp.float32)).astype(jnp.bfloat16)


def over_tiles(info_ref, start_ref, bias_ref, blk, span, tile, pairs):
    end2 = info_ref[2] if span == "half" else info_ref[0]
    end1 = info_ref[3] if span == "half" else info_ref[1]

    def two(i, _):
        pairs(info_ref[LIST + 2 * i], info_ref[LIST + 2 * i + 1])
        return 0

    def clear(i, _):
        tile(info_ref[LIST + i], None)
        return 0

    def mixed(i, _):
        j = info_ref[LIST + WINDOW + i]
        kpos = info_ref[6 + j] + lax.broadcasted_iota(jnp.int32, (blk, blk), 0)
        for r in range(2):
            qpos = info_ref[4 + r] + lax.broadcasted_iota(jnp.int32, (1, blk), 1)
            bias_ref[r] = jnp.where((kpos <= qpos) & (kpos >= start_ref[r]), 0.0, BIG_NEG)
        tile(j, bias_ref)
        return 0

    half = lax.shift_right_logical(end2, 1)
    lax.fori_loop(0, half, two, 0)
    lax.fori_loop(2 * half, end2, clear, 0)
    lax.fori_loop(0, end1, mixed, 0)


def over_own(info_ref, start_ref, bias_ref, blk, r, base, tile):
    def one(i, _):
        j = info_ref[i]
        kpos = info_ref[6 + j] + lax.broadcasted_iota(jnp.int32, (blk, blk), 0)
        qpos = info_ref[4 + r] + lax.broadcasted_iota(jnp.int32, (1, blk), 1)
        bias_ref[r] = jnp.where((kpos <= qpos) & (kpos >= start_ref[r]), 0.0, BIG_NEG)
        tile(j - base, bias_ref, at=j - 2 * HALF)
        return 0

    lax.fori_loop(LIST + info_ref[2], LIST + info_ref[0], one, 0)
    lax.fori_loop(LIST + WINDOW + info_ref[3], LIST + WINDOW + info_ref[1], one, 0)


def forward_kernel(heads, hd, share, pieces, info_ref, start_ref, q0_ref, q1_ref, *rest):
    blk = q0_ref.shape[0]
    parts = 1 + max(piece[0] for piece in pieces)
    part_refs, rest = rest[:parts], rest[parts:]
    scale = LOG2E / math.sqrt(hd)
    if share == 0:
        m_ref, l_ref, a_ref, qs_ref, window_ref, bias_ref = rest
        m_ref[...] = jnp.full(m_ref.shape, BIG_NEG, jnp.float32)
        l_ref[...] = jnp.zeros(l_ref.shape, jnp.float32)
        a_ref[...] = jnp.zeros(a_ref.shape, jnp.float32)
    else:
        m_in, l_in, a_in, d0_ref, d1_ref, stat_ref, mine_ref, theirs_ref = rest[:8]
        qs_ref, window_ref, bias_ref, m_ref, l_ref, a_ref = rest[8:]
        m_ref[...] = m_in[...]
        l_ref[...] = l_in[...]
        a_ref[...] = a_in[...]
    fill(window_ref, part_refs, pieces, blk)
    fill_scaled(qs_ref, (q0_ref, q1_ref), heads, hd, scale)

    def update(kb, vb, masks):
        xs = range(2 * heads)
        vt = jnp.concatenate([vb.T, jnp.ones((16, vb.shape[0]), jnp.bfloat16)], axis=0)
        k2 = jnp.concatenate([kb, kb], axis=1)
        old = [(m_ref[x], l_ref[x], a_ref[x]) for x in xs]
        found = [nt(k2, qs_ref[x]) for x in xs]
        if masks is not None:
            found = [s + masks[x // heads] for x, s in zip(xs, found)]
        new = []
        for s, (m_old, l_old, a_old) in zip(found, old):
            m_new = jnp.maximum(m_old, jnp.max(s, axis=0, keepdims=True))
            p = jnp.exp2(s - m_new)
            f = jnp.exp2(m_old - m_new)
            both = nn(vt, p.astype(jnp.bfloat16))
            new.append((m_new, l_old * f + both[hd:hd + 1], a_old * f + both[:hd]))
        for x, (m_new, total, acc) in zip(xs, new):
            m_ref[x] = m_new
            l_ref[x] = total
            a_ref[x] = acc

    def tile(j, masks):
        update(window_ref[0, j], window_ref[1, j], masks)

    def pairs(j1, j2):
        kb, vb = [jnp.concatenate([window_ref[i, j1], window_ref[i, j2]], axis=0) for i in range(2)]
        update(kb, vb, None)

    over_tiles(info_ref, start_ref, bias_ref, blk, "all", tile, pairs)
    if share == 1:
        for r, d_ref in enumerate((d0_ref, d1_ref)):
            for h in range(heads):
                x = r * heads + h
                dt = d_ref[:, h * hd:(h + 1) * hd].astype(jnp.float32).T
                stat_ref[x, 0:1] = m_ref[x]
                stat_ref[x, 1:2] = l_ref[x]
                stat_ref[x, 2:3] = jnp.sum(dt * a_ref[x], axis=0, keepdims=True)
        mine_ref[...] = a_ref[:heads]
        theirs_ref[...] = a_ref[heads:].astype(jnp.bfloat16)


def vm():
    return pl.BlockSpec(memory_space=pltpu.VMEM)


def sm():
    return pl.BlockSpec(memory_space=pltpu.SMEM)


def params():
    return pltpu.CompilerParams(vmem_limit_bytes=24 << 20)


def forward(info, starts, q0, q1, parts, pieces, share, state=(), douts=()):
    blk, width = q0.shape
    hd = parts[0].shape[2]
    heads = width // hd
    n = 2 * heads
    f32 = jnp.float32
    row = jax.ShapeDtypeStruct((n, 1, blk), f32)
    work = [pltpu.VMEM((n, blk, 2 * hd), q0.dtype), pltpu.VMEM((2, WINDOW, blk, hd), q0.dtype),
            pltpu.VMEM((2, blk, blk), f32)]
    if share == 0:
        shapes = (row, row, jax.ShapeDtypeStruct((n, hd, blk), f32))
    else:
        shapes = (jax.ShapeDtypeStruct((n, 3, blk), f32), jax.ShapeDtypeStruct((heads, hd, blk), f32),
                  jax.ShapeDtypeStruct((heads, hd, blk), jnp.bfloat16))
        work += [pltpu.VMEM((n, 1, blk), f32), pltpu.VMEM((n, 1, blk), f32), pltpu.VMEM((n, hd, blk), f32)]
    args = (info, starts, q0, q1) + tuple(parts) + tuple(state) + tuple(douts)
    return pl.pallas_call(
        functools.partial(forward_kernel, heads, hd, share, pieces),
        out_shape=shapes,
        in_specs=[sm()] + [vm()] * (len(args) - 1),
        out_specs=(vm(),) * 3,
        scratch_shapes=work,
        compiler_params=params(),
        cost_estimate=pl.CostEstimate(flops=4 * WINDOW * n * blk * blk * hd, bytes_accessed=4 << 20, transcendentals=0),
        name="forward_part",
    )(*args)


def merge_stats(s_mine, s_theirs):
    m = jnp.maximum(s_mine[0:1], s_theirs[0:1])
    fa = jnp.exp2(s_mine[0:1] - m)
    fb = jnp.exp2(s_theirs[0:1] - m)
    total = s_mine[1:2] * fa + s_theirs[1:2] * fb
    delta = (s_mine[2:3] * fa + s_theirs[2:3] * fb) / total
    return m + jnp.log2(total), fa / total, fb / total, delta


def backward_kernel(heads, hd, span, pieces, info_ref, start_ref, q0_ref, q1_ref, d0_ref, d1_ref, sa_ref, sb_ref, *rest):
    blk = q0_ref.shape[0]
    scale = LOG2E / math.sqrt(hd)
    back = 1.0 / math.sqrt(hd)
    parts = 1 + max(piece[0] for piece in pieces)
    part_refs, rest = rest[:parts], rest[parts:]
    if span == "all":
        ga_ref, gb_ref, dq_ref = rest[:3]
        work = rest[3:]
        dq_ref[...] = jnp.zeros(dq_ref.shape, jnp.float32)
    elif span == "half":
        dq_in, ga_ref, gb_ref, own_ref, dq_out, send_ref = rest[:6]
        work = rest[6:-1]
        dq_ref = rest[-1]
        dq_ref[...] = dq_in[...]
    else:
        dq_in, own_ref, mine_ref, theirs_ref, ga_ref, gb_ref, att_ref, dq0_ref = rest[:8]
        work = rest[8:-1]
        dq_ref = rest[-1]
        dq_ref[...] = dq_in[...]
    q_ref, d_ref, window_ref, log_ref, delta_ref, qs_ref, bias_ref, grad_ref = work
    if span == "own":
        grad_ref[...] = own_ref[...]
    else:
        grad_ref[...] = jnp.zeros(grad_ref.shape, jnp.bfloat16)
    if span == "half":
        own_ref[...] = jnp.zeros(own_ref.shape, jnp.float32)
    fill(window_ref, part_refs, pieces, blk)
    fill_heads(q_ref, (q0_ref, q1_ref), heads, hd)
    fill_heads(d_ref, (d0_ref, d1_ref), heads, hd)
    fill_scaled(qs_ref, (q0_ref, q1_ref), heads, hd, scale)
    for r in range(1 if span == "own" else 2):
        for h in range(heads):
            x = r * heads + h
            log_total, wa, wb, delta = merge_stats(sa_ref[x], sb_ref[(1 - r) * heads + h])
            log_ref[x] = log_total
            delta_ref[x] = delta
            if span == "own" and r == 0:
                att = mine_ref[h] * wa + theirs_ref[h].astype(jnp.float32) * wb
                att_ref[:, h * hd:(h + 1) * hd] = att.T.astype(jnp.bfloat16)

    def tile(j, masks, xs=range(2 * heads), add_ref=None, at=None):
        kb = window_ref[0, j]
        vb = window_ref[1, j]
        kt = kb.T
        qs = [q_ref[x] for x in xs]
        ds = [d_ref[x] for x in xs]
        rows = [(log_ref[x], delta_ref[x]) for x in xs]
        sums = [dq_ref[x] for x in xs]
        k2 = jnp.concatenate([kb, kb], axis=1)
        found = [nt(k2, qs_ref[x]) for x in xs]
        pushed = [nt(vb, d) for d in ds]
        weights, slopes = [], []
        for x, s, dp, (log_total, delta) in zip(xs, found, pushed, rows):
            if masks is not None:
                s = s + masks[x // heads]
            p = jnp.exp2(s - log_total)
            weights.append(p.astype(jnp.bfloat16))
            slopes.append((p * (dp - delta)).astype(jnp.bfloat16))
        dv = nn(jnp.concatenate(weights, axis=1), jnp.concatenate(ds, axis=0))
        dk = nn(jnp.concatenate(slopes, axis=1), jnp.concatenate(qs, axis=0)) * back
        sums = [dq + nn(kt, slope) for dq, slope in zip(sums, slopes)]
        for x, dq in zip(xs, sums):
            dq_ref[x] = dq
        if add_ref is None:
            grad_ref[0, j] = dk.astype(jnp.bfloat16)
            grad_ref[1, j] = dv.astype(jnp.bfloat16)
        else:
            add_ref[0, at] += dk
            add_ref[1, at] += dv

    def pairs(j1, j2):
        xs = range(2 * heads)
        kb = jnp.concatenate([window_ref[0, j1], window_ref[0, j2]], axis=0)
        vb = jnp.concatenate([window_ref[1, j1], window_ref[1, j2]], axis=0)
        kt = kb.T
        qs = [q_ref[x] for x in xs]
        ds = [d_ref[x] for x in xs]
        rows = [(log_ref[x], delta_ref[x]) for x in xs]
        sums = [dq_ref[x] for x in xs]
        k2 = jnp.concatenate([kb, kb], axis=1)
        found = [nt(k2, qs_ref[x]) for x in xs]
        pushed = [nt(vb, d) for d in ds]
        weights, slopes = [], []
        for x, s, dp, (log_total, delta) in zip(xs, found, pushed, rows):
            p = jnp.exp2(s - log_total)
            weights.append(p.astype(jnp.bfloat16))
            slopes.append((p * (dp - delta)).astype(jnp.bfloat16))
        dv = nn(jnp.concatenate(weights, axis=1), jnp.concatenate(ds, axis=0))
        dk = nn(jnp.concatenate(slopes, axis=1), jnp.concatenate(qs, axis=0)) * back
        sums = [dq + nn(kt, slope) for dq, slope in zip(sums, slopes)]
        for x, dq in zip(xs, sums):
            dq_ref[x] = dq
        for i, g in enumerate((dk, dv)):
            grad_ref[i, j1] = g[:blk].astype(jnp.bfloat16)
            grad_ref[i, j2] = g[blk:].astype(jnp.bfloat16)

    if span != "own":
        over_tiles(info_ref, start_ref, bias_ref, blk, span, tile, pairs)
    if span != "all":
        r = 1 if span == "half" else 0
        xs = range(r * heads, (r + 1) * heads)
        over_own(info_ref, start_ref, bias_ref, blk, r, 0 if span == "half" else 2 * HALF,
                 functools.partial(tile, xs=xs, add_ref=own_ref if span == "half" else grad_ref))
    lists = {"all": ([0, 1, 2, 3, 8], [4, 5, 6, 7, 9]), "half": ([0, 1, 2, 3], [4, 5, 6, 7]), "own": ([0], [1])}
    for chunks, g_ref in zip(lists[span], (ga_ref, gb_ref)):
        for i, j in enumerate(chunks):
            rows = slice(i * blk, (i + 1) * blk)
            for kind in range(2):
                g_ref[kind, rows, :] = grad_ref[kind, j].astype(jnp.bfloat16)
    if span == "half":
        dq_out[...] = dq_ref[:heads]
        for h in range(heads):
            send_ref[:, h * hd:(h + 1) * hd] = (dq_ref[heads + h] * back).T.astype(jnp.bfloat16)
    if span == "own":
        for h in range(heads):
            dq0_ref[:, h * hd:(h + 1) * hd] = (dq_ref[h] * back).T


def backward(info, starts, q0, q1, d0, d1, s_mine, s_theirs, parts, pieces, span, sums=()):
    blk, width = q0.shape
    hd = parts[0].shape[2]
    heads = width // hd
    n = 2 * heads
    f32 = jnp.float32
    count = 2 if span == "own" else WINDOW
    sent = {"all": WINDOW // 2, "half": HALF, "own": 1}[span]
    grad = jax.ShapeDtypeStruct((2, sent * blk, hd), jnp.bfloat16)
    two = pltpu.VMEM((n, blk, hd), q0.dtype)
    row = pltpu.VMEM((n, 1, blk), f32)
    grads = pltpu.VMEM((2, 2 * sent, blk, hd), f32 if span == "own" else jnp.bfloat16)
    work = [two, two, pltpu.VMEM((2, count, blk, hd), q0.dtype), row, row,
            pltpu.VMEM((n, blk, 2 * hd), q0.dtype), pltpu.VMEM((2, blk, blk), f32), grads]
    out = jax.ShapeDtypeStruct((blk, width), jnp.bfloat16)
    if span == "all":
        shapes = (grad, grad, jax.ShapeDtypeStruct((n, hd, blk), f32))
    elif span == "half":
        shapes = (grad, grad, jax.ShapeDtypeStruct((2, 2, blk, hd), f32),
                  jax.ShapeDtypeStruct((heads, hd, blk), f32), out)
        work += [pltpu.VMEM((n, hd, blk), f32)]
    else:
        shapes = (grad, grad, out, jax.ShapeDtypeStruct((blk, width), f32))
        work += [pltpu.VMEM((heads, hd, blk), f32)]
    args = (info, starts, q0, q1, d0, d1, s_mine, s_theirs) + tuple(parts) + tuple(sums)
    return pl.pallas_call(
        functools.partial(backward_kernel, heads, hd, span, pieces),
        out_shape=shapes,
        in_specs=[sm()] + [vm()] * (len(args) - 1),
        out_specs=(vm(),) * len(shapes),
        scratch_shapes=work,
        compiler_params=params(),
        cost_estimate=pl.CostEstimate(flops=10 * count * n * blk * blk * hd, bytes_accessed=4 << 20, transcendentals=0),
        name="backward_part",
    )(*args)


def per_device(queries, keys, values, dout, doc_lengths):
    blk = queries.shape[0]
    seqs, subs = lax.axis_size("seq"), lax.axis_size("sub")
    f32, bf16 = jnp.float32, jnp.bfloat16

    def swap_core(value):
        return lax.ppermute(value, "seq", [(s, s ^ 1) for s in range(seqs)])

    def swap_mate(value):
        return lax.ppermute(value, "sub", [(s, s ^ 1) for s in range(subs)])

    def swap_far(value):
        return lax.ppermute(value, "sub", [(s, (s + 2 * (s % 2) - 1) % subs) for s in range(subs)])

    def route(step, sign):
        chips = (NEAR, AWAY)[step]
        pairs = [(s, s + 2 * chips[s % 2]) for s in range(seqs)]
        return [(a, b)[::sign] for a, b in pairs if b < seqs]

    tie = lax.optimization_barrier
    other_keys, other_values = swap_core(keys), swap_core(values)
    q_mate = swap_mate(queries)
    pair = jnp.concatenate([jnp.stack([keys, values]), jnp.stack([other_keys, other_values])], axis=1)
    pair, doc_lengths = tie((pair, doc_lengths))
    near = lax.ppermute(pair, "seq", route(0, 1))
    away = lax.ppermute(pair, "seq", route(1, 1))
    *infos, starts = tables(doc_lengths, blk, subs)
    near, infos, starts, q_mate = tie((near, infos, starts, q_mate))
    near_far = swap_far(near)
    away, near_far, d_send = tie((away, near_far, dout))
    d_mate = swap_mate(d_send)
    most = jnp.concatenate([near, away, near_far], axis=1)
    most_x = swap_core(most)
    away_far = swap_far(jnp.concatenate([away, pair[:, :blk]], axis=1))
    near_pieces = ((0, 0, HALF), (1, 0, HALF), (2, 0, 2))
    far_pieces = ((0, HALF, 2), (2, 0, 2), (1, HALF, 2), (3, 0, 2), (2, 2, 1), (3, 2, 1))
    state = forward(infos[0], starts, queries, q_mate, (most, most_x, pair), near_pieces, 0)
    away_far, state, d_mate = tie((away_far, state, d_mate))
    away_far_x = swap_core(away_far)
    far_parts = (most, most_x, away_far, away_far_x)
    stats, mine, theirs = forward(infos[1], starts, queries, q_mate, far_parts, far_pieces, 1, state, (dout, d_mate))
    common = (starts, queries, q_mate, dout, d_mate, stats, swap_mate(stats))
    grad_a, grad_b, dq = backward(infos[1], *common, far_parts, far_pieces, "all")
    grad_b, theirs = tie((grad_b, theirs))
    theirs = swap_mate(theirs)
    grad_a = (grad_a.astype(f32) + swap_core(grad_b).astype(f32)).astype(bf16)
    grad_a, dq = tie((grad_a, dq))
    grad_far = swap_far(grad_a[:, : HALF * blk])
    near_parts = (most, most_x, pair)
    far_own = grad_a[:, HALF * blk :]
    grad_a, grad_b, own, dq, dq_send = backward(infos[0], *common, near_parts, near_pieces, "half", (dq,))
    grad_b, grad_far, theirs = tie((grad_b, grad_far, theirs))
    home = (grad_a.astype(f32) + swap_core(grad_b).astype(f32) + grad_far.astype(f32)).astype(bf16)
    home, dq = tie((home, dq))
    near = lax.ppermute(home[:, : 2 * blk], "seq", route(0, -1))
    away = lax.ppermute(home[:, 2 * blk :], "seq", route(1, -1))
    dq_back = swap_mate(dq_send)
    grad_own, grad_other, attended, dq_mine = backward(
        infos[0], *common, (pair,), ((0, 0, 2),), "own", (dq, own, mine, theirs)
    )
    grad_own, far_own = tie((grad_own, far_own))
    grad_far_own = swap_far(far_own)
    near, away, dq_back, grad_own, grad_other = tie((near, away, dq_back, grad_own, grad_other))
    back = near.astype(f32) + away.astype(f32)
    other = swap_core((back[:, blk:] + grad_other.astype(f32)).astype(bf16))
    query_grad = (dq_mine + dq_back.astype(f32)).astype(bf16)
    total = [
        (grad_own[i].astype(f32) + grad_far_own[i].astype(f32) + back[i, :blk] + other[i].astype(f32)).astype(bf16)
        for i in range(2)
    ]
    return attended, query_grad, total[0], total[1]


def solution(mesh):
    rows = P(("seq", "sub"), None)
    return jax.shard_map(
        per_device,
        mesh=mesh,
        in_specs=(rows, rows, rows, rows, P()),
        out_specs=(rows, rows, rows, rows),
        check_vma=False,
    )
```
